256 devices in a mesh: role: 4 (over x), grp: 2 (over y_hi), dev: 32 (over y_lo, z, core).
Axes of the slice: x: 4, y: 4 (y_hi: 2, y_lo: 2; y = y_hi * 2 + y_lo), z: 8, core: 2. Of those that a mesh axis runs over, the one named last changes fastest.
Arguments:
- q_latent: bfloat16 [1536, 2, 128, 512], P(('role', 'grp', 'dev')), may hold values from -256 to 256
- q_rope: bfloat16 [1536, 2, 8192], P(('role', 'grp', 'dev')), may hold values from -256 to 256
- pool_latent: bfloat16 [2, 256, 128, 512], P(None, ('role', 'grp', 'dev')), may hold values from -6 to 6
- pool_rope: bfloat16 [2, 256, 64, 128], P(None, ('role', 'grp', 'dev')), may hold values from -6 to 6
- panel_latent: bfloat16 [1536, 2, 128, 512], P(('role', 'grp', 'dev')), may hold values from -6 to 6
- panel_rope: bfloat16 [1536, 2, 64, 128], P(('role', 'grp', 'dev')), may hold values from -6 to 6
- panel_from: int32 [1536], P(('role', 'grp', 'dev')), may hold values from 0 to 3, as said below
- prefix_id: int32 [1536], P(('role', 'grp', 'dev')), may hold values from 0 to 3
- block_mask: int32 [1536, 16], P(('role', 'grp', 'dev')), may hold values 0 or 1
- suffix_len: int32 [256, 6], P(('role', 'grp', 'dev')), may hold values from 1 to 128, 448 in all within a row
Outputs:
- attended: bfloat16 [1536, 2, 128, 512], P(('role', 'grp', 'dev'))
The draws below stay inside these ranges and needn't reach their ends.
Inputs may be any that keep to these rules, and one draw needn't show every extreme that they name: For every c < 384, the values panel_from[c + p * 384] over the pools p are a permutation of the pool indices. Among the 6 requests of one device, no pool is named more than 2 times, and some pool is named exactly 2 times.
All inputs are finite; a program needn't handle non-finite values. No bound on the sum of `block_mask` on one device may be relied on, other than what follows from the above.
Results may differ from the reference program's by a relative error of at most 0.0065.
Values may be sent and summed in bfloat16 or wider, within the bound.
No kernel may reach another device: no remote copies, remote signals or barrier semaphores. Data moves between devices by JAX's collectives and lax.ppermute only.
A program may use at most 128 MiB of HBM per device.

```python
import math
import jax
import jax.numpy as jnp
import numpy as np
from jax import lax

HEADS = 128
D_LAT = 512
D_ROPE = 64
LAYERS = 2
TILE = 128
SUFFIX = 128
PREFIXES = 4
R_DEV = 6
REQUESTS = 1536
ROLE_ROWS = 384
POOL = 256
POOL_ROLE = 64
PRE_BLOCKS = 16


def draw_q_latent(key, part):
    key = jax.random.fold_in(key, 1)
    values = 1.25 * jax.random.truncated_normal(key, -5.0, 5.0, (REQUESTS, LAYERS, HEADS, D_LAT), jnp.float32)
    return values.astype(jnp.bfloat16)


def draw_q_rope(key, part):
    key = jax.random.fold_in(key, 2)
    values = 1.25 * jax.random.truncated_normal(key, -5.0, 5.0, (REQUESTS, LAYERS, HEADS, D_ROPE), jnp.float32)
    return values.reshape(REQUESTS, LAYERS, HEADS * D_ROPE).astype(jnp.bfloat16)


def draw_panel_from(key, part):
    key = jax.random.fold_in(key, 7)
    pool_count = REQUESTS // ROLE_ROWS
    block_count = ROLE_ROWS // R_DEV
    order_key, offset_key = jax.random.split(key)
    scores = jax.random.randint(order_key, (block_count, R_DEV), 0, 1 << 20) * R_DEV
    scores = scores + jnp.arange(R_DEV, dtype=jnp.int32)[None, :]
    ranking = jnp.argsort(scores, axis=1).astype(jnp.int32)
    offsets = jax.random.randint(offset_key, (block_count, 1), 0, pool_count).astype(jnp.int32)
    shifts = ((ranking + offsets) % pool_count).reshape(ROLE_ROWS)
    pools = jnp.arange(pool_count, dtype=jnp.int32)[:, None]
    return ((pools + shifts[None, :]) % pool_count).reshape(REQUESTS).astype(jnp.int32)


def with_ends(values, stream_key, smallest, high):
    longest = values.shape.index(max(values.shape))
    spots = []
    for shift in (0, 1):
        where = [jax.random.randint(jax.random.fold_in(stream_key, axis), (), 0, length) for axis, length in enumerate(values.shape)]
        where[longest] = (where[longest] + shift) % values.shape[longest]
        spots.append(tuple(where))
    return values.at[spots[0]].set(smallest).at[spots[1]].set(high)


def levels(own_key, extent, shards, smallest, high):
    level = 1.0
    for axis_at, blocks in shards:
        steps = jax.random.uniform(jax.random.fold_in(jax.random.fold_in(own_key, 6), axis_at), (blocks,), jnp.float32, smallest / len(shards), high / len(shards))
        level = level * jnp.repeat(jnp.exp(steps), extent[axis_at] // blocks).reshape((-1,) + (1,) * (len(extent) - 1 - axis_at))
    return level


def profile(amount, total, most, skew):
    loads = [(1 << 20) // math.isqrt(grade ** skew) + 1 for grade in range(2, amount + 1)]
    surplus, holding = total - most - (amount - 1), [1] * (amount - 1)
    while surplus > 0:
        movable = [i for i in range(amount - 1) if holding[i] < most]
        pool, left = sum([loads[i] for i in movable]), surplus
        for i in movable:
            addition = min(most - holding[i], max(1, left * loads[i] // pool), surplus)
            holding[i] = holding[i] + addition
            surplus = surplus - addition
    return np.array([most] + holding)


def ragged(rng, number_of, total, bound, skew):
    if number_of == 2:
        one = jax.random.randint(rng, (), max(1, total - bound), min(bound, total - 1) + 1)
        return jnp.stack([one, total - one])
    lengths = jnp.asarray(profile(number_of, total, bound, skew), jnp.int32)
    pairs = (number_of - 1) // 2
    source_of, sink = lengths[1:1 + 2 * pairs:2], lengths[2:2 + 2 * pairs:2]
    margin = jnp.minimum(source_of - 1, bound - sink)
    shifted = jax.random.randint(jax.random.fold_in(rng, 1), (pairs,), 0, 1 << 20) % (margin + 1)
    lengths = lengths.at[1:1 + 2 * pairs:2].set(source_of - shifted).at[2:2 + 2 * pairs:2].set(sink + shifted)
    return lengths[jax.random.permutation(jax.random.fold_in(rng, 2), number_of)]


def scatter_about(rng, extent, spread, most, cuts=(), kind=jnp.bfloat16):
    drawn = spread * jax.random.normal(rng, extent, jnp.float32)
    if cuts:
        drawn = drawn * levels(rng, extent, cuts, -0.22, 0.18)
    return jnp.clip(drawn, -most, most).astype(kind)


def setup_inputs(seed: int = 0) -> dict:
    key_list = jax.random.split(jax.random.key(seed), 11)
    return {
        "q_latent": draw_q_latent(jax.random.fold_in(key_list[10], 71), 0),
        "q_rope": draw_q_rope(jax.random.fold_in(key_list[10], 71), 0),
        "pool_latent": scatter_about(key_list[2], (LAYERS, POOL, TILE, D_LAT), 1.0, 6.0, ((1, 256),)),
        "pool_rope": scatter_about(key_list[3], (LAYERS, POOL, D_ROPE, TILE), 1.0, 6.0, ((1, 256),)),
        "panel_latent": scatter_about(key_list[4], (REQUESTS, LAYERS, SUFFIX, D_LAT), 1.0, 6.0, ((0, 256),)),
        "panel_rope": scatter_about(key_list[5], (REQUESTS, LAYERS, D_ROPE, SUFFIX), 1.0, 6.0, ((0, 256),)),
        "panel_from": draw_panel_from(jax.random.fold_in(key_list[10], 71), 0),
        "prefix_id": with_ends(jax.random.randint(key_list[7], (REQUESTS,), 0, PREFIXES), jax.random.fold_in(key_list[7], 1), 0, PREFIXES - 1).astype(jnp.int32),
        "block_mask": with_ends((jax.random.randint(key_list[8], (REQUESTS, PRE_BLOCKS), 0, 4) < 3).astype(jnp.int32), jax.random.fold_in(key_list[8], 1), 0, 1),
        "suffix_len": jax.vmap(lambda own: ragged(own, R_DEV, SUFFIX + (R_DEV - 1) * SUFFIX // 2, SUFFIX, 0))(jax.random.split(key_list[9], (REQUESTS // R_DEV))).reshape((REQUESTS // R_DEV, R_DEV)).astype(jnp.int32),
    }


score_scale = 192.0 ** -0.5


def reference(q_latent, q_rope, pool_latent, pool_rope, panel_latent, panel_rope, panel_from, prefix_id, block_mask, suffix_len):
    lengths_flat = suffix_len.reshape(-1)

    def attend_one(request):
        pool_index = request // ROLE_ROWS
        source = panel_from[request] * ROLE_ROWS + request % ROLE_ROWS
        start_block = (pool_index * POOL_ROLE + prefix_id[request] * PRE_BLOCKS).astype(jnp.int32)
        blocks_lat = lax.dynamic_slice_in_dim(pool_latent, start_block, PRE_BLOCKS, 1)
        blocks_rope = lax.dynamic_slice_in_dim(pool_rope, start_block, PRE_BLOCKS, 1)
        prefix_lat = blocks_lat.reshape(LAYERS, PRE_BLOCKS * TILE, D_LAT)
        prefix_rope = jnp.transpose(blocks_rope, (0, 2, 1, 3)).reshape(LAYERS, D_ROPE, PRE_BLOCKS * TILE)
        keys_lat = jnp.concatenate([prefix_lat, panel_latent[source]], axis=1).astype(jnp.float32)
        keys_rope = jnp.concatenate([prefix_rope, panel_rope[source]], axis=2).astype(jnp.float32)
        keep_pre = jnp.repeat(block_mask[request] == 1, TILE)
        keep_own = jnp.arange(SUFFIX, dtype=jnp.int32) < lengths_flat[request]
        live_keys = jnp.concatenate([keep_pre, keep_own])
        query_lat = q_latent[request].astype(jnp.float32)
        query_rope = q_rope[request].reshape(LAYERS, HEADS, D_ROPE).astype(jnp.float32)
        scores = jnp.einsum("lhd,ltd->lht", query_lat, keys_lat) + jnp.einsum("lhd,ldt->lht", query_rope, keys_rope)
        scores = scores * score_scale
        scores = jnp.where(live_keys[None, None, :], scores, -jnp.inf)
        peak_score = jnp.max(scores, axis=2, keepdims=True)
        exp_all = jnp.exp(scores - peak_score)
        weights = (exp_all / jnp.sum(exp_all, axis=2, keepdims=True)).astype(jnp.bfloat16)
        attended = jnp.einsum("lht,ltd->lhd", weights.astype(jnp.float32), keys_lat)
        return attended.astype(jnp.bfloat16)

    return lax.map(attend_one, jnp.arange(REQUESTS, dtype=jnp.int32))
```

```python
import functools
import math

import jax
import jax.numpy as jnp
from jax import lax
from jax.experimental import pallas as pl
from jax.experimental.pallas import tpu as pltpu
from jax.sharding import Mesh
from jax.sharding import PartitionSpec as P

HEADS = 128
D_LAT = 512
D_ROPE = 64
LAYERS = 2
TILE = 128
ROWS = 144
R_DEV = 6
ROLES = 4
NY = 4
NZ = 8
NAMES = ("role", "yh", "yl", "z", "core")
Y = ("yh", "yl")

LOG2_SCALE = 192.0 ** (-0.5) * math.log2(math.e)
NEG = -1e30

VMEM = pl.BlockSpec(memory_space=pltpu.VMEM)
SMEM = pl.BlockSpec(memory_space=pltpu.SMEM)
ANY = pl.BlockSpec(memory_space=pl.ANY)
BF = jnp.bfloat16
F32 = jnp.float32


def pack_kernel(coords, lat, rope, own, oth):
    core = coords[0]
    for ref, layer in ((own, core), (oth, 1 - core)):
        ref[:TILE, :] = lat[layer, 0]
        for j in range(4):
            ref[TILE:, 128 * j : 128 * (j + 1)] = rope[layer, 0, 16 * j : 16 * (j + 1), :]


def pack_blocks(coords, lat, rope):
    shape = jax.ShapeDtypeStruct((ROWS, D_LAT), BF)
    return pl.pallas_call(
        pack_kernel,
        out_shape=(shape, shape),
        in_specs=[SMEM, VMEM, VMEM],
        out_specs=(VMEM, VMEM),
        name="pack_blocks",
    )(coords, lat, rope)


def panel_copies(lat, rope, slot, layer, out, sems):
    copies = [pltpu.make_async_copy(lat.at[slot, layer], out.at[pl.ds(0, TILE)], sems.at[0])]
    for j in range(4):
        copies.append(
            pltpu.make_async_copy(
                rope.at[slot, layer, pl.ds(16 * j, 16)],
                out.at[pl.ds(TILE, 16), pl.ds(128 * j, 128)],
                sems.at[1 + j],
            )
        )
    return copies


def pick_kernel(coords, wanted, lat, rope, out1, out2, out3, sems):
    role = coords[1]
    copies = []
    for k, out in enumerate((out1, out2, out3)):
        first, second, seen = jnp.int32(0), jnp.int32(0), jnp.int32(0)
        for s in range(R_DEV):
            hit = wanted[k, s] == role
            first = jnp.where(hit & (seen == 0), s, first)
            second = jnp.where(hit & (seen == 1), s, second)
            seen = seen + hit.astype(jnp.int32)
        for j, slot in enumerate((first, second)):
            for layer in range(LAYERS):
                copies += panel_copies(lat, rope, slot, layer, out.at[j, layer], sems.at[k, j, layer])
    for copy in copies:
        copy.start()
    for copy in copies:
        copy.wait()


def pick_panels(coords, wanted, lat, rope):
    shape = jax.ShapeDtypeStruct((2, LAYERS, ROWS, D_LAT), BF)
    return pl.pallas_call(
        pick_kernel,
        out_shape=(shape,) * 3,
        in_specs=[SMEM, SMEM, ANY, ANY],
        out_specs=(ANY,) * 3,
        scratch_shapes=[pltpu.SemaphoreType.DMA((3, 2, LAYERS, 5))],
        name="pick_panels",
    )(coords, wanted, lat, rope)


def place_kernel(coords, source, got1, got2, got3, lat, rope, mine, other, sems):
    core, role = coords[0], coords[1]
    for phase in (0, 1):
        counts = [jnp.int32(0)] * ROLES
        for s in range(R_DEV):
            shift = (role - source[s] + ROLES) % ROLES
            rank = jnp.int32(0)
            for k in range(ROLES):
                rank = jnp.where(shift == k, counts[k], rank)
                counts[k] = counts[k] + (shift == k).astype(jnp.int32)
            rank = jnp.minimum(rank, 1)
            for o, (out, layer) in enumerate(((mine, core), (other, 1 - core))):
                def run(copies):
                    for copy in copies:
                        copy.start() if phase == 0 else copy.wait()

                @pl.when(shift == 0)
                def _():
                    run(panel_copies(lat, rope, s, layer, out.at[s], sems.at[s, o]))

                for k, got in enumerate((got1, got2, got3)):

                    @pl.when(shift == k + 1)
                    def _():
                        run([pltpu.make_async_copy(got.at[rank, layer], out.at[s], sems.at[s, o, 0])])


def place_panels(coords, source, got, lat, rope):
    shape = jax.ShapeDtypeStruct((R_DEV, ROWS, D_LAT), BF)
    return pl.pallas_call(
        place_kernel,
        out_shape=(shape, shape),
        in_specs=[SMEM, SMEM, ANY, ANY, ANY, ANY, ANY],
        out_specs=(ANY, ANY),
        scratch_shapes=[pltpu.SemaphoreType.DMA((R_DEV, 2, 5))],
        name="place_panels",
    )(coords, source, *got, lat, rope)


def flash_kernel(plan, halves, first, last, n_arrays, *refs):
    coords, meta_own, meta_par, q_own, q_par = refs[:5]
    arrays = refs[5 : 5 + n_arrays]
    rest = list(refs[5 + n_arrays :])
    if not first:
        acc_in, ml_in = rest[0], rest[1]
        rest = rest[2:]
    if last:
        outs = rest[: len(halves)]
        rest = rest[len(halves) :]
    else:
        acc_out, ml_out = rest[0], rest[1]
        rest = rest[2:]
    keys, rope_keys = rest
    core, row, col = coords[0], coords[2], coords[3]
    n = len(plan)

    for h, half in enumerate(halves):
        meta = (meta_own, meta_par)[half]
        q_ref = (q_own, q_par)[half]

        def body(r, carry):
            dy = (meta[r, 0] - row + NY) % NY

            def put(i, tile):
                keys[TILE * i : TILE * (i + 1), :] = tile[:TILE, :]
                for j in range(4):
                    rope_keys[16 * j : 16 * (j + 1), TILE * i : TILE * (i + 1)] = tile[TILE:, 128 * j : 128 * (j + 1)]

            for i, source in enumerate(plan):
                if source[0] == "b":
                    put(i, arrays[source[1]][source[2] + dy])
                elif source[0] == "p":
                    put(i, arrays[source[1 + half]][r])
            for d in range(NY):
                if any(source[0] == "a" for source in plan):

                    @pl.when(dy == d)
                    def _():
                        for i, source in enumerate(plan):
                            if source[0] == "a":
                                if d == 0:
                                    put(i, arrays[source[1]][source[2]])
                                else:
                                    put(i, arrays[source[3][d - 1]][source[4]])

            q_lat = q_ref[r, :, :D_LAT]
            q_rope = q_ref[r, :, D_LAT:]
            scores = lax.dot_general(q_lat, keys[...], (((1,), (1,)), ((), ())), preferred_element_type=F32)
            scores = scores + jnp.dot(q_rope, rope_keys[...], preferred_element_type=F32)
            scores = scores * LOG2_SCALE
            parts = []
            for i, source in enumerate(plan):
                part = scores[:, TILE * i : TILE * (i + 1)]
                if source[0] == "p":
                    token = lax.broadcasted_iota(jnp.int32, (HEADS, TILE), 1)
                    part = jnp.where(token < meta[r, 1], part, NEG)
                else:
                    dz = source[-1]
                    parity = core if source[0] == "a" else 1 - core
                    block = 2 * ((col + (dz + NZ)) % NZ) + parity
                    live = meta[r, 2 + block] == 1
                    part = jnp.where(live, part, NEG)
                parts.append(part)
            scores = jnp.concatenate(parts, axis=1) if n > 1 else parts[0]
            peak = jnp.max(scores, axis=1, keepdims=True)
            s = half * R_DEV + r
            if first:
                new = peak
                weights = jnp.exp2(scores - new)
                total = jnp.sum(weights, axis=1, keepdims=True)
                acc = jnp.dot(weights.astype(BF), keys[...], preferred_element_type=F32)
            else:
                old = ml_in[s, :, :1]
                new = jnp.maximum(old, peak)
                fade = jnp.exp2(old - new)
                weights = jnp.exp2(scores - new)
                total = fade * ml_in[s, :, 128:129] + jnp.sum(weights, axis=1, keepdims=True)
                acc = acc_in[s] * fade + jnp.dot(weights.astype(BF), keys[...], preferred_element_type=F32)
            if last:
                outs[h][r] = (acc / total).astype(BF)
            else:
                acc_out[s] = acc
                ml_out[s, :, :128] = jnp.broadcast_to(new, (HEADS, 128))
                ml_out[s, :, 128:] = jnp.broadcast_to(total, (HEADS, 128))
            return carry

        lax.fori_loop(0, R_DEV, body, 0)


def flash(name, plan, arrays, common, state, halves=(0, 1), last=False):
    n = len(plan)
    first = state is None
    ops = list(common) + list(arrays)
    specs = [SMEM, SMEM, SMEM, VMEM, VMEM] + [VMEM] * len(arrays)
    aliases = {}
    if not first:
        if not last:
            aliases = {len(ops): 0, len(ops) + 1: 1}
        ops += list(state)
        specs += [VMEM, VMEM]
    if last:
        out_shape = tuple(jax.ShapeDtypeStruct((R_DEV, HEADS, D_LAT), BF) for _ in halves)
    else:
        out_shape = (
            jax.ShapeDtypeStruct((2 * R_DEV, HEADS, D_LAT), F32),
            jax.ShapeDtypeStruct((2 * R_DEV, HEADS, 256), F32),
        )
    pairs = R_DEV * len(halves) * n * HEADS * TILE
    return pl.pallas_call(
        functools.partial(flash_kernel, plan, halves, first, last, len(arrays)),
        out_shape=out_shape,
        in_specs=specs,
        out_specs=(VMEM,) * len(out_shape),
        scratch_shapes=[pltpu.VMEM((TILE * n, D_LAT), BF), pltpu.VMEM((D_ROPE, TILE * n), BF)],
        input_output_aliases=aliases,
        cost_estimate=pl.CostEstimate(flops=4 * pairs * (D_LAT + D_ROPE + D_LAT), bytes_accessed=4 << 20, transcendentals=pairs),
        compiler_params=pltpu.CompilerParams(vmem_limit_bytes=40 << 20),
        name=name,
    )(*ops)


def ring(n, shift):
    return [(i, (i - shift) % n) for i in range(n)]


def from_z(x, dz):
    return lax.ppermute(x, "z", ring(NZ, dz))


def from_y(x, dy):
    return lax.ppermute(x, Y, ring(NY, dy))


def from_role(x, shift):
    return lax.ppermute(x, "role", ring(ROLES, shift))


def from_core(x):
    return lax.ppermute(x, "core", [(0, 1), (1, 0)])


def from_y_core(x, dy):
    pairs = [(2 * i + c, 2 * ((i - dy) % NY) + 1 - c) for i in range(NY) for c in range(2)]
    return lax.ppermute(x, ("yh", "yl", "core"), pairs)


def shards(q_latent, q_rope, pool_latent, pool_rope, panel_latent, panel_rope, panel_from, prefix_id, block_mask, suffix_len):
    core = lax.axis_index("core")
    coords = jnp.stack([core, lax.axis_index("role"), lax.axis_index(Y), lax.axis_index("z")]).astype(jnp.int32)

    a0, oth = pack_blocks(coords, pool_latent, pool_rope)
    a_up, a_dn = from_z(a0, 1), from_z(a0, -1)
    b = [from_core(oth)] + [from_y_core(oth, dy) for dy in (1, 3, 2)]
    b = [b[0], b[1], b[3], b[2]]

    wanted = jnp.stack([from_role(panel_from, k) for k in (1, 2, 3)])
    meta_own = jnp.concatenate([prefix_id[:, None], suffix_len.reshape(R_DEV, 1), block_mask], axis=1)
    meta_par = from_core(meta_own)

    rope4 = q_rope.reshape(R_DEV, LAYERS, HEADS, D_ROPE)
    queries = jnp.concatenate([q_latent, rope4], axis=3)
    q_own = lax.dynamic_index_in_dim(queries, core, 1, keepdims=False)
    q_par = from_core(lax.dynamic_index_in_dim(queries, 1 - core, 1, keepdims=False))
    common = (coords, meta_own, meta_par, q_own, q_par)

    up0 = jnp.stack([a_up] + b)
    dn0 = jnp.stack([a_dn] + b)
    up1, dn1 = from_z(up0, 1), from_z(dn0, -1)
    g1 = jnp.stack([a0, a_up, a_dn])
    y1 = [from_y(g1, dy) for dy in (1, 3, 2)]
    y1 = [y1[0], y1[2], y1[1]]

    sent = pick_panels(coords, wanted, panel_latent, panel_rope)
    got = [from_role(x, -k) for k, x in zip((1, 2, 3), sent)]
    mine, other = place_panels(coords, panel_from, got, panel_latent, panel_rope)
    theirs = from_core(other)

    up2, dn2 = from_z(up1, 1), from_z(dn1, -1)
    g2 = jnp.stack([up1[0], dn1[0]])
    y2 = [from_y(g2, dy) for dy in (1, 3, 2)]
    y2 = [y2[0], y2[2], y2[1]]
    state = flash("flash1", [("b", 0, 1, 0), ("b", 1, 1, 1), ("b", 2, 1, -1)], [up0, up1, dn1], common, None)

    up3, dn3 = from_z(up2, 1), from_z(dn2, -1)
    g3 = jnp.stack([up2[0], dn2[0]])
    y3 = [from_y(g3, dy) for dy in (1, 3, 2)]
    y3 = [y3[0], y3[2], y3[1]]
    state = flash(
        "flash2",
        [("b", 0, 1, 2), ("b", 1, 1, -2)] + [("a", 5, i, (2, 3, 4), i, dz) for i, dz in enumerate((0, 1, -1))],
        [up2, dn2] + y1 + [g1],
        common,
        state,
    )

    up4, dn4 = from_z(up3[1:3], 1), from_z(dn3[3:5], -1)
    g4 = up3[:1]
    y4 = [from_y(g4, dy) for dy in (1, 3, 2)]
    y4 = [y4[0], y4[2], y4[1]]
    state = flash(
        "flash3",
        [("b", 0, 1, 3), ("b", 1, 1, -3)]
        + [("a", 5, i, (2, 3, 4), i, dz) for i, dz in enumerate((2, -2))]
        + [("a", 9, i, (6, 7, 8), i, dz) for i, dz in enumerate((3, -3))]
        + [("p", 10, 11)],
        [up3, dn3] + y2 + [g2] + y3 + [g3, mine, theirs],
        common,
        state,
    )

    b4 = jnp.concatenate([up4, dn4], axis=0)
    plan = [("b", 0, 0, 4), ("a", 4, 0, (1, 2, 3), 0, 4)]
    arrays = [b4] + y4 + [g4]
    (out_par,) = flash("flash4", plan, arrays, common, state, (1,), True)
    out_got = from_core(out_par)
    (out_own,) = flash("flash5", plan, arrays, common, state, (0,), True)
    return jnp.where(core == 0, jnp.stack([out_own, out_got], axis=1), jnp.stack([out_got, out_own], axis=1))


def solution(mesh):
    fine = Mesh(mesh.devices.reshape(ROLES, 2, 2, NZ, 2), NAMES)
    rows = P(NAMES)
    blocks = P(None, NAMES)
    return jax.shard_map(
        shards,
        mesh=fine,
        in_specs=(rows, rows, blocks, blocks, rows, rows, rows, rows, rows, rows),
        out_specs=rows,
        check_vma=False,
    )
```

```python
import functools
import math

import jax
import jax.numpy as jnp
from jax import lax
from jax.experimental import pallas as pl
from jax.experimental.pallas import tpu as pltpu
from jax.sharding import Mesh
from jax.sharding import PartitionSpec as P

HEADS = 128
D_LAT = 512
D_ROPE = 64
LAYERS = 2
TILE = 128
ROWS = 144
R_DEV = 6
ROLES = 4
NY = 4
NZ = 8
NAMES = ("role", "yh", "yl", "z", "core")
PLANE = ("yh", "yl", "z", "core")

LOG2E = math.log2(math.e)
LOG2_SCALE = 192.0 ** (-0.5) * LOG2E
NEG = -1e30
WIDE = D_LAT + 128

VMEM = pl.BlockSpec(memory_space=pltpu.VMEM)
SMEM = pl.BlockSpec(memory_space=pltpu.SMEM)
ANY = pl.BlockSpec(memory_space=pl.ANY)
BF = jnp.bfloat16
F32 = jnp.float32


def unit(*lead):
    return jax.ShapeDtypeStruct(lead + (LAYERS, ROWS, D_LAT), BF)


def pack_into(out, lat, rope):
    out[:TILE, :] = lat[...]
    for j in range(4):
        out[TILE:, 128 * j : 128 * (j + 1)] = rope[16 * j : 16 * (j + 1), :]


def pack_kernel(lat, rope, out):
    for layer in range(LAYERS):
        pack_into(out.at[layer], lat.at[layer, 0], rope.at[layer, 0])


def pack_blocks(lat, rope):
    return pl.pallas_call(pack_kernel, out_shape=unit(), in_specs=[VMEM, VMEM], out_specs=VMEM, name="pack_blocks")(lat, rope)


def stack_kernel(n, *refs):
    out = refs[-1]
    for i, ref in enumerate(refs[:n]):
        out[i] = ref[...]


def stack(parts, name, after=()):
    return pl.pallas_call(
        functools.partial(stack_kernel, len(parts)),
        out_shape=unit(len(parts)),
        in_specs=[VMEM] * len(parts) + [ANY] * len(after),
        out_specs=VMEM,
        name=name,
    )(*parts, *after)


def build_kernel(up_plan, dn_plan, first_up, first_dn, n_parts, coords, up_in, dn_in, *refs):
    parts, (up, dn) = refs[:n_parts], refs[-2:]
    n = up.shape[0]

    @pl.when(coords[0] == 0)
    def _():
        for i in range(n):
            up[i] = up_in[first_up + i]
            dn[i] = dn_in[first_dn + i]

    @pl.when(coords[0] == 1)
    def _():
        for out, plan in ((up, up_plan), (dn, dn_plan)):
            for i in range(n):
                if i < len(plan):
                    kind, index = plan[i]
                    out[i] = {"up": up_in, "dn": dn_in}[kind][index] if kind in ("up", "dn") else parts[index][...]
                else:
                    out[i] = jnp.zeros(out.shape[1:], out.dtype)


def build(coords, up_in, dn_in, parts, up_plan, dn_plan, name, n=4, first_up=0, first_dn=0, after=()):
    return pl.pallas_call(
        functools.partial(build_kernel, up_plan, dn_plan, first_up, first_dn, len(parts)),
        out_shape=(unit(n), unit(n)),
        in_specs=[SMEM] + [VMEM] * (2 + len(parts)) + [ANY] * len(after),
        out_specs=(VMEM, VMEM),
        compiler_params=pltpu.CompilerParams(vmem_limit_bytes=24 << 20),
        name=name,
    )(coords, up_in, dn_in, *parts, *after)


def pick_kernel(coords, wanted1, wanted2, wanted3, lat, rope, *outs):
    role = coords[1]
    for wanted, out in zip((wanted1, wanted2, wanted3), outs):
        first, second, seen = jnp.int32(0), jnp.int32(0), jnp.int32(0)
        for s in range(R_DEV):
            hit = wanted[s] == role
            first = jnp.where(hit & (seen == 0), s, first)
            second = jnp.where(hit & (seen == 1), s, second)
            seen = seen + hit.astype(jnp.int32)
        for j, slot in enumerate((first, second)):
            for layer in range(LAYERS):
                pack_into(out.at[j, layer], lat.at[slot, layer], rope.at[slot, layer])


def pick_panels(coords, wanted, lat, rope):
    return pl.pallas_call(
        pick_kernel,
        out_shape=(unit(2),) * 3,
        in_specs=[SMEM] * 4 + [VMEM, VMEM],
        out_specs=(VMEM,) * 3,
        compiler_params=pltpu.CompilerParams(vmem_limit_bytes=24 << 20),
        name="pick_panels",
    )(coords, *wanted, lat, rope)


def flash_kernel(plan, panel, halves, first, last, per_step, n_arrays, *refs):
    refs = list(refs)

    def take(count):
        taken = refs[:count]
        del refs[:count]
        return taken

    coords, metas = take(1)[0], take(2)
    queries = [take(2) for _ in halves]
    arrays = take(n_arrays)
    if panel:
        source, got1, got2, got3, own_lat, own_rope = take(6)
    state_in = None if first else take(2)
    recv = take(1)[0] if last == "own" else None
    state_out = take(2) if not last else None
    out = take(1)[0] if last else None
    scratch = refs
    core, role, row, col = (coords[i] for i in range(4))

    def one_step(step, carry):
        jobs = [(q, h, half) for q in range(per_step) for h, half in enumerate(halves)]

        def keys_of(q, h, layer):
            k = 2 * ((q * len(halves) + h) * LAYERS + layer)
            return scratch[k], scratch[k + 1]

        def put(q, h, i, place, dynamic=None):
            array, index = place
            if dynamic is not None:
                index = dynamic
            for layer in range(LAYERS):
                keys, rope_keys = keys_of(q, h, layer)
                tile = arrays[array].at[layer] if index is None else arrays[array].at[index, layer]
                fill(keys, rope_keys, i, tile)

        def fill(keys, rope_keys, i, tile):
            keys[TILE * i : TILE * (i + 1), :] = tile[:TILE, :]
            for j in range(4):
                rope_keys[16 * j : 16 * (j + 1), TILE * i : TILE * (i + 1)] = tile[TILE:, 128 * j : 128 * (j + 1)]

        def row_of(q, half):
            return (metas[half][step * per_step + q, 0] - row + NY) % NY

        @pl.when(core == 0)
        def _():
            for q, h, half in jobs:
                dy = row_of(q, half)
                slot = jnp.where(dy == 2, 3, jnp.where(dy == 3, 2, dy))
                for i, (_, places, _) in enumerate(plan):
                    if isinstance(places, int):
                        put(q, h, i, (places, None), slot)
                    else:
                        @pl.when(slot < 2)
                        def _():
                            put(q, h, i, (places[0], None), slot)

                        @pl.when(slot >= 2)
                        def _():
                            put(q, h, i, (places[1], None), slot - 2)

        @pl.when(core == 1)
        def _():
            for q, h, half in jobs:
                dy = row_of(q, half)
                for d in range(NY):

                    @pl.when(dy == d)
                    def _():
                        for i, (_, _, places) in enumerate(plan):
                            put(q, h, i, places[d])

        if panel:
            for q, h, half in jobs:
                if half == 1:
                    continue
                i = len(plan)
                r = step * per_step + q
                shift = (role - source[r] + ROLES) % ROLES
                rank = jnp.int32(0)
                for s in range(R_DEV):
                    rank = rank + ((s < r) & (source[s] == source[r])).astype(jnp.int32)
                rank = jnp.minimum(rank, 1)

                @pl.when(shift == 0)
                def _():
                    for layer in range(LAYERS):
                        keys, rope_keys = keys_of(q, h, layer)
                        keys[TILE * i : TILE * (i + 1), :] = own_lat[r, layer]
                        rope_keys[:, TILE * i : TILE * (i + 1)] = own_rope[r, layer]

                for k, got in enumerate((got1, got2, got3)):

                    @pl.when(shift == k + 1)
                    def _():
                        for layer in range(LAYERS):
                            fill(*keys_of(q, h, layer), i, got.at[rank, layer])

        def chain(q, h, half, layer):
            meta = metas[half]
            r = step * per_step + q
            u = 2 * half + layer
            keys, rope_keys = keys_of(q, h, layer)
            n = len(plan) + (1 if panel and half == 0 else 0)
            q_lat, q_rope = queries[h][0][r, layer], queries[h][1][r, layer]
            width = n * TILE
            scores = lax.dot_general(q_lat, keys[:width, :], (((1,), (1,)), ((), ())), preferred_element_type=F32)
            scores = scores + jnp.dot(q_rope, rope_keys[:, :width], preferred_element_type=F32)
            yield
            scores = scores * LOG2_SCALE
            pieces = []
            for i in range(n):
                piece = scores[:, TILE * i : TILE * (i + 1)]
                if i == len(plan):
                    token = lax.broadcasted_iota(jnp.int32, (HEADS, TILE), 1)
                    piece = jnp.where(token < meta[r, 1], piece, NEG)
                else:
                    block = 2 * ((col + (plan[i][0] + NZ)) % NZ) + core
                    piece = jnp.where(meta[r, 2 + block] == 1, piece, NEG)
                pieces.append(piece)
            scores = jnp.concatenate(pieces, axis=1) if n > 1 else pieces[0]
            peak = jnp.max(scores, axis=1, keepdims=True)
            if first:
                new = peak
                weights = jnp.exp2(scores - new)
                total = jnp.sum(weights, axis=1, keepdims=True)
            else:
                acc_in, ml_in = state_in
                old = ml_in[r, u, :, 0:1]
                new = jnp.maximum(old, peak)
                fade = jnp.exp2(old - new)
                weights = jnp.exp2(scores - new)
                total = jnp.sum(weights, axis=1, keepdims=True) + fade * ml_in[r, u, :, 1:2]
            yield
            acc = jnp.dot(weights.astype(BF), keys[:width, :], preferred_element_type=F32)
            if not first:
                acc = acc + acc_in[r, u] * fade
            yield
            if not last:
                acc_out, ml_out = state_out
                acc_out[r, u] = acc
                lane = lax.broadcasted_iota(jnp.int32, (HEADS, 128), 1)
                ml_out[r, u] = jnp.where(lane == 0, new, total)
            elif last == "par":
                lse = new + jnp.log(total) * LOG2E
                high = lse.astype(BF).astype(F32)
                mid = (lse - high).astype(BF).astype(F32)
                low = lse - high - mid
                lane = lax.broadcasted_iota(jnp.int32, (HEADS, 128), 1)
                tail = jnp.where(lane == 0, high, jnp.where(lane == 1, mid, jnp.where(lane == 2, low, 0.0)))
                out[r, layer, :, :D_LAT] = (acc * (1.0 / total)).astype(BF)
                out[r, layer, :, D_LAT:] = tail.astype(BF)
            else:
                tail = recv[r, layer, :, D_LAT:].astype(F32)
                theirs = tail[:, 0:1] + tail[:, 1:2] + tail[:, 2:3]
                top = jnp.maximum(new, theirs)
                ours, theirs = jnp.exp2(new - top), jnp.exp2(theirs - top)
                scale = 1.0 / (total * ours + theirs)
                out[r, layer] = (acc * (ours * scale) + recv[r, layer, :, :D_LAT].astype(F32) * (theirs * scale)).astype(BF)

        chains = [chain(q, h, half, layer) for q, h, half in jobs for layer in range(LAYERS)]
        for _ in range(3):
            for c in chains:
                next(c)
        for c in chains:
            next(c, None)
        return carry

    lax.fori_loop(0, R_DEV // per_step, one_step, 0)


def flash(name, plan, arrays, common, queries, state=None, panels=None, halves=(0, 1), last=None, recv=None, per_step=2):
    first = state is None
    ops = list(common)
    for half in halves:
        ops += queries[half]
    ops += arrays
    specs = [SMEM] * 3 + [VMEM] * (len(ops) - 3)
    if panels is not None:
        ops += panels
        specs += [SMEM] + [VMEM] * 5
    aliases = {}
    if not first:
        if not last:
            aliases = {len(ops): 0, len(ops) + 1: 1}
        ops += state
        specs += [VMEM, VMEM]
    if last == "own":
        ops.append(recv)
        specs.append(VMEM)
    if last:
        out_shape = jax.ShapeDtypeStruct((R_DEV, LAYERS, HEADS, WIDE if last == "par" else D_LAT), BF)
        out_specs = VMEM
    else:
        out_shape = (
            pltpu.VMEM((R_DEV, 2 * LAYERS, HEADS, D_LAT), F32),
            pltpu.VMEM((R_DEV, 2 * LAYERS, HEADS, 128), F32),
        )
        out_specs = (VMEM, VMEM)
    n = len(plan) + (1 if panels is not None else 0)
    tiles = R_DEV * LAYERS * len(halves) * n
    return pl.pallas_call(
        functools.partial(flash_kernel, plan, panels is not None, halves, first, last, per_step, len(arrays)),
        out_shape=out_shape,
        in_specs=specs,
        out_specs=out_specs,
        scratch_shapes=[pltpu.VMEM((TILE * n, D_LAT), BF), pltpu.VMEM((D_ROPE, TILE * n), BF)]
        * (LAYERS * len(halves) * per_step),
        input_output_aliases=aliases,
        cost_estimate=pl.CostEstimate(
            flops=3 * tiles * HEADS * TILE * (2 * D_LAT + D_ROPE), bytes_accessed=4 << 20, transcendentals=tiles * HEADS * TILE
        ),
        compiler_params=pltpu.CompilerParams(vmem_limit_bytes=30 << 20),
        name=name,
    )(*ops)


def place(y, z, c):
    return ((y % NY) * NZ + z % NZ) * 2 + c


def send(x, moves):
    pairs = [
        (place(y + move[0], z + move[1], c), place(y, z, c))
        for c, move in moves.items()
        for y in range(NY)
        for z in range(NZ)
    ]
    return lax.ppermute(x, PLANE, pairs)


def from_role(x, shift):
    return lax.ppermute(x, "role", [(i, (i - shift) % ROLES) for i in range(ROLES)])


def from_core(x):
    return lax.ppermute(x, "core", [(0, 1), (1, 0)])


def shards(q_latent, q_rope, pool_latent, pool_rope, panel_latent, panel_rope, panel_from, prefix_id, block_mask, suffix_len):
    coords = jnp.stack([lax.axis_index("core"), lax.axis_index("role"), lax.axis_index(("yh", "yl")), lax.axis_index("z")])
    coords = coords.astype(jnp.int32)
    own = pack_blocks(pool_latent, pool_rope)

    u0 = send(own, {0: (1, 0), 1: (0, 1)})
    d0 = send(own, {0: (-1, 0), 1: (0, -1)})
    t0 = send(own, {0: (2, 0)})
    wanted = [from_role(panel_from, k) for k in (1, 2, 3)]
    meta_own = jnp.concatenate([prefix_id[:, None], suffix_len.reshape(R_DEV, 1), block_mask], axis=1)
    meta_par = from_core(meta_own)
    m1 = stack([own, u0, d0, t0], "stack1", wanted)

    up, dn = {0: (0, 1), 1: (1, 0)}, {0: (0, -1), 1: (-1, 0)}
    u1, d1 = send(m1, up), send(m1, dn)
    a2, a2n = send(u0, {1: (0, 1)}), send(d0, {1: (0, -1)})
    rope_own = q_rope.reshape(R_DEV, LAYERS, HEADS, D_ROPE)
    q_own = [q_latent, rope_own]
    q_par = [from_core(q_latent), from_core(rope_own)]
    sent = pick_panels(coords, wanted, panel_latent, panel_rope)
    got = [from_role(x, -k) for k, x in zip((1, 2, 3), sent)]

    m2u, m2d = build(
        coords, u1, d1, [a2, a2n], [("x", 0), ("x", 1), ("up", 0), ("up", 1)], [("x", 0), ("x", 1), ("dn", 2)], "build2", after=sent
    )
    u2, d2 = send(m2u, up), send(m2d, dn)
    a3, a3n = send(a2, {1: (0, 1)}), send(a2n, {1: (0, -1)})

    m3u, m3d = build(
        coords,
        u2,
        d2,
        [a3, a3n],
        [("x", 0), ("x", 1), ("up", 0)],
        [("x", 0), ("x", 1), ("dn", 1)],
        "build3",
        after=[got[0], got[2], *q_par, meta_par],
    )
    u3, d3 = send(m3u, up), send(m3d, dn)
    t3 = send(stack([a3, a3n], "stack3"), {1: (2, 0)})
    a4 = send(a3, {1: (0, 1)})
    common = (coords, meta_own, meta_par)
    queries = (q_own, q_par)
    plan = []
    for dz, array, index in ((0, 0, 0), (1, 1, 1), (-1, 2, 2)):
        far = ((3, 2), (3, 3), (4, 2))[index]
        plan.append((dz, array, [(0, index), (1, index), far, (2, index)]))
    state = flash("flash_near", plan, [m1, u1, d1, u2, d2], common, queries)

    m4u, m4d = build(coords, u3, d3, [a4], [("x", 0)], [("x", 0)], "build4", 2, 0, 2, [got[1], state[1]])
    u4, d4 = send(m4u, up), send(m4d, dn)
    t4 = send(a4, {1: (2, 0)})
    plan = []
    for k, dz in enumerate((2, -2, 3, -3)):
        slab = (0, 1, 2, 3)[k]
        i = k % 2
        near, back = ((0, i), (1, i)) if k < 2 else ((2, i), (3, i))
        far = ((2, 2), (3, 2), (8, 0), (8, 1))[k]
        plan.append((dz, slab, [(4 + k, None), near, far, back]))
    state = flash(
        "flash_mid",
        plan,
        [u2, d2, u3, d3, a2, a2n, a3, a3n, t3],
        common,
        queries,
        state,
        [panel_from, *got, panel_latent, panel_rope],
    )

    plan = [(4, (0, 1), [(2, None), (0, 0), (3, None), (1, 0)])]
    arrays = [u4, d4, a4, t4]
    part = flash("flash_far_par", plan, arrays, common, queries, state, None, (1,), "par")
    recv = from_core(part)
    return flash("flash_far_own", plan, arrays, common, queries, state, None, (0,), "own", recv)


def solution(mesh):
    fine = Mesh(mesh.devices.reshape(ROLES, 2, 2, NZ, 2), NAMES)
    rows = P(NAMES)
    blocks = P(None, NAMES)
    return jax.shard_map(
        shards,
        mesh=fine,
        in_specs=(rows, rows, blocks, blocks, rows, rows, rows, rows, rows, rows),
        out_specs=rows,
        check_vma=False,
    )
```

```python
import functools
import math

import jax
import jax.numpy as jnp
from jax import lax
from jax.experimental import pallas as pl
from jax.experimental.pallas import tpu as pltpu
from jax.sharding import Mesh
from jax.sharding import PartitionSpec as P

HEADS = 128
D_LAT = 512
D_ROPE = 64
LAYERS = 2
TILE = 128
ROWS = 144
R_DEV = 6
ROLES = 4
NY = 4
NZ = 8
NAMES = ("role", "yh", "yl", "z", "core")
PLANE = ("yh", "yl", "z", "core")

LOG2E = math.log2(math.e)
LOG2_SCALE = 192.0 ** (-0.5) * LOG2E
NEG = -1e30
OWN_INTS = R_DEV * 19
WIDE = D_LAT + 128

VMEM = pl.BlockSpec(memory_space=pltpu.VMEM)
SMEM = pl.BlockSpec(memory_space=pltpu.SMEM)
ANY = pl.BlockSpec(memory_space=pl.ANY)
BF = jnp.bfloat16
F32 = jnp.float32


def unit(*lead):
    return jax.ShapeDtypeStruct(lead + (LAYERS, ROWS, D_LAT), BF)


def pack_into(out, lat, rope):
    out[:TILE, :] = lat[...]
    for j in range(4):
        out[TILE:, 128 * j : 128 * (j + 1)] = rope[16 * j : 16 * (j + 1), :]


def pack_kernel(lat, rope, out):
    for layer in range(LAYERS):
        pack_into(out.at[layer], lat.at[layer, 0], rope.at[layer, 0])


def pack_blocks(lat, rope):
    return pl.pallas_call(pack_kernel, out_shape=unit(), in_specs=[VMEM, VMEM], out_specs=VMEM, name="pack_blocks")(lat, rope)


def stack_kernel(n, *refs):
    out = refs[-1]
    for i, ref in enumerate(refs[:n]):
        out[i] = ref[...]


def stack(parts, name, after=()):
    return pl.pallas_call(
        functools.partial(stack_kernel, len(parts)),
        out_shape=unit(len(parts)),
        in_specs=[VMEM] * len(parts) + [ANY] * len(after),
        out_specs=VMEM,
        name=name,
    )(*parts, *after)


def build_kernel(up_plan, dn_plan, first_up, first_dn, n_parts, up_in, dn_in, *refs):
    parts, (up, dn) = refs[:n_parts], refs[-2:]
    n = up.shape[0]
    core = lax.axis_index("core")

    @pl.when(core == 0)
    def _():
        for i in range(n):
            up[i] = up_in[first_up + i]
            dn[i] = dn_in[first_dn + i]

    @pl.when(core == 1)
    def _():
        for out, plan in ((up, up_plan), (dn, dn_plan)):
            for i in range(n):
                if i < len(plan):
                    kind, index = plan[i]
                    out[i] = {"up": up_in, "dn": dn_in}[kind][index] if kind in ("up", "dn") else parts[index][...]
                else:
                    out[i] = jnp.zeros(out.shape[1:], out.dtype)


def build(up_in, dn_in, parts, up_plan, dn_plan, name, n=4, first_up=0, first_dn=0, after=()):
    return pl.pallas_call(
        functools.partial(build_kernel, up_plan, dn_plan, first_up, first_dn, len(parts)),
        out_shape=(unit(n), unit(n)),
        in_specs=[VMEM] * (2 + len(parts)) + [ANY] * len(after),
        out_specs=(VMEM, VMEM),
        compiler_params=pltpu.CompilerParams(vmem_limit_bytes=24 << 20),
        name=name,
    )(up_in, dn_in, *parts, *after)


def pick_kernel(wanted1, wanted2, wanted3, lat, rope, *outs):
    role = lax.axis_index("role")
    for wanted, out in zip((wanted1, wanted2, wanted3), outs):
        first, second, seen = jnp.int32(0), jnp.int32(0), jnp.int32(0)
        for s in range(R_DEV):
            hit = wanted[s] == role
            first = jnp.where(hit & (seen == 0), s, first)
            second = jnp.where(hit & (seen == 1), s, second)
            seen = seen + hit.astype(jnp.int32)
        for j, slot in enumerate((first, second)):
            for layer in range(LAYERS):
                pack_into(out.at[j, layer], lat.at[slot, layer], rope.at[slot, layer])


def pick_panels(wanted, lat, rope):
    return pl.pallas_call(
        pick_kernel,
        out_shape=(unit(2),) * 3,
        in_specs=[SMEM] * 3 + [VMEM, VMEM],
        out_specs=(VMEM,) * 3,
        compiler_params=pltpu.CompilerParams(vmem_limit_bytes=24 << 20),
        name="pick_panels",
    )(*wanted, lat, rope)


def flash_kernel(plan, panel, halves, first, last, per_step, n_arrays, *refs):
    refs = list(refs)

    def take(count):
        taken = refs[:count]
        del refs[:count]
        return taken

    ints = take(1)[0]
    queries = [take(2) for _ in halves]
    arrays = take(n_arrays)
    if panel:
        got1, got2, got3, own_lat, own_rope = take(5)
    state_in = None if first else take(2)
    recv = take(1)[0] if last == "own" else None
    state_out = take(2) if not last else None
    out = take(1)[0] if last else None
    scratch = refs
    core, role, row, col = (lax.axis_index(name) for name in ("core", "role", ("yh", "yl"), "z"))

    def prefix(half, r):
        return ints[OWN_INTS * half + r]

    def length(half, r):
        return ints[OWN_INTS * half + R_DEV + r]

    def source(r):
        return ints[2 * R_DEV + r]

    def live(half, r, block):
        return ints[OWN_INTS * half + 3 * R_DEV + 16 * r + block] == 1

    def one_step(step, carry):
        jobs = [(q, h, half) for q in range(per_step) for h, half in enumerate(halves)]

        def keys_of(q, h, layer):
            k = 2 * ((q * len(halves) + h) * LAYERS + layer)
            return scratch[k], scratch[k + 1]

        def put(q, h, i, place, dynamic=None):
            array, index = place
            if dynamic is not None:
                index = dynamic
            for layer in range(LAYERS):
                keys, rope_keys = keys_of(q, h, layer)
                tile = arrays[array].at[layer] if index is None else arrays[array].at[index, layer]
                fill(keys, rope_keys, i, tile)

        def fill(keys, rope_keys, i, tile):
            keys[TILE * i : TILE * (i + 1), :] = tile[:TILE, :]
            for j in range(4):
                rope_keys[16 * j : 16 * (j + 1), TILE * i : TILE * (i + 1)] = tile[TILE:, 128 * j : 128 * (j + 1)]

        def row_of(q, half):
            return (prefix(half, step * per_step + q) - row + NY) % NY

        @pl.when(core == 0)
        def _():
            for q, h, half in jobs:
                dy = row_of(q, half)
                slot = jnp.where(dy == 2, 3, jnp.where(dy == 3, 2, dy))
                for i, (_, places, _) in enumerate(plan):
                    if isinstance(places, int):
                        put(q, h, i, (places, None), slot)
                    else:
                        @pl.when(slot < 2)
                        def _():
                            put(q, h, i, (places[0], None), slot)

                        @pl.when(slot >= 2)
                        def _():
                            put(q, h, i, (places[1], None), slot - 2)

        @pl.when(core == 1)
        def _():
            for q, h, half in jobs:
                dy = row_of(q, half)
                for d in range(NY):

                    @pl.when(dy == d)
                    def _():
                        for i, (_, _, places) in enumerate(plan):
                            put(q, h, i, places[d])

        if panel:
            for q, h, half in jobs:
                if half == 1:
                    continue
                i = len(plan)
                r = step * per_step + q
                shift = (role - source(r) + ROLES) % ROLES
                rank = jnp.int32(0)
                for s in range(R_DEV):
                    rank = rank + ((s < r) & (source(s) == source(r))).astype(jnp.int32)
                rank = jnp.minimum(rank, 1)

                @pl.when(shift == 0)
                def _():
                    for layer in range(LAYERS):
                        keys, rope_keys = keys_of(q, h, layer)
                        keys[TILE * i : TILE * (i + 1), :] = own_lat[r, layer]
                        rope_keys[:, TILE * i : TILE * (i + 1)] = own_rope[r, layer]

                for k, got in enumerate((got1, got2, got3)):

                    @pl.when(shift == k + 1)
                    def _():
                        for layer in range(LAYERS):
                            fill(*keys_of(q, h, layer), i, got.at[rank, layer])

        def chain(q, h, half, layer):
            r = step * per_step + q
            u = 2 * half + layer
            keys, rope_keys = keys_of(q, h, layer)
            n = len(plan) + (1 if panel and half == 0 else 0)
            q_lat, q_rope = queries[h][0][r, layer], queries[h][1][r, layer]
            width = n * TILE
            scores = lax.dot_general(q_lat, keys[:width, :], (((1,), (1,)), ((), ())), preferred_element_type=F32)
            scores = scores + jnp.dot(q_rope, rope_keys[:, :width], preferred_element_type=F32)
            yield
            pieces = []
            for i in range(n):
                piece = scores[:, TILE * i : TILE * (i + 1)] * LOG2_SCALE
                if i == len(plan):
                    token = lax.broadcasted_iota(jnp.int32, (HEADS, TILE), 1)
                    piece = jnp.where(token < length(half, r), piece, NEG)
                else:
                    block = 2 * ((col + (plan[i][0] + NZ)) % NZ) + core
                    piece = piece + jnp.where(live(half, r, block), 0.0, NEG)
                pieces.append(piece)
            top = functools.reduce(jnp.maximum, pieces)
            top = jnp.broadcast_to(jnp.max(top, axis=1, keepdims=True), (HEADS, 128))
            if not first:
                acc_in, ml_in = state_in
                old = ml_in[r, u, :, :128]
                top = jnp.maximum(old, top)
                fade = jnp.exp2(old - top)
            pieces = [jnp.exp2(piece - top) for piece in pieces]
            total = functools.reduce(jnp.add, pieces)
            if not first:
                total = total + fade * ml_in[r, u, :, 128:]
            weights = jnp.concatenate([piece.astype(BF) for piece in pieces], axis=1) if n > 1 else pieces[0].astype(BF)
            yield
            acc = jnp.dot(weights, keys[:width, :], preferred_element_type=F32)
            acc = [acc[:, 128 * j : 128 * (j + 1)] for j in range(4)]
            if not first:
                acc = [acc[j] + acc_in[r, u, :, 128 * j : 128 * (j + 1)] * fade for j in range(4)]
            yield
            if not last:
                acc_out, ml_out = state_out
                for j in range(4):
                    acc_out[r, u, :, 128 * j : 128 * (j + 1)] = acc[j]
                ml_out[r, u, :, :128] = top
                ml_out[r, u, :, 128:] = total
                return
            total = jnp.broadcast_to(jnp.sum(total, axis=1, keepdims=True), (HEADS, 128))
            if last == "par":
                lse = top + jnp.log(total) * LOG2E
                high = lse.astype(BF).astype(F32)
                mid = (lse - high).astype(BF).astype(F32)
                low = lse - high - mid
                lane = lax.broadcasted_iota(jnp.int32, (HEADS, 128), 1)
                tail = jnp.where(lane == 0, high, jnp.where(lane == 1, mid, jnp.where(lane == 2, low, 0.0)))
                inverse = 1.0 / total
                for j in range(4):
                    out[r, layer, :, 128 * j : 128 * (j + 1)] = (acc[j] * inverse).astype(BF)
                out[r, layer, :, D_LAT:] = tail.astype(BF)
            else:
                tail = recv[r, layer, :, D_LAT:].astype(F32)
                theirs = jnp.broadcast_to(jnp.sum(tail, axis=1, keepdims=True), (HEADS, 128))
                most = jnp.maximum(top, theirs)
                ours, theirs = jnp.exp2(top - most), jnp.exp2(theirs - most)
                scale = 1.0 / (total * ours + theirs)
                ours, theirs = ours * scale, theirs * scale
                for j in range(4):
                    part = recv[r, layer, :, 128 * j : 128 * (j + 1)].astype(F32)
                    out[r, layer, :, 128 * j : 128 * (j + 1)] = (acc[j] * ours + part * theirs).astype(BF)

        chains = [chain(q, h, half, layer) for q, h, half in jobs for layer in range(LAYERS)]
        for _ in range(3):
            for c in chains:
                next(c)
        for c in chains:
            next(c, None)
        return carry

    lax.fori_loop(0, R_DEV // per_step, one_step, 0)


def flash(name, plan, arrays, ints, queries, state=None, panels=None, halves=(0, 1), last=None, recv=None, per_step=2):
    first = state is None
    ops = [ints]
    for half in halves:
        ops += queries[half]
    ops += arrays
    specs = [SMEM] + [VMEM] * (len(ops) - 1)
    if panels is not None:
        ops += panels
        specs += [VMEM] * 5
    aliases = {}
    if not first:
        if not last:
            aliases = {len(ops): 0, len(ops) + 1: 1}
        ops += state
        specs += [VMEM, VMEM]
    if last == "own":
        ops.append(recv)
        specs.append(VMEM)
    if last:
        out_shape = jax.ShapeDtypeStruct((R_DEV, LAYERS, HEADS, WIDE if last == "par" else D_LAT), BF)
        out_specs = VMEM
    else:
        out_shape = (
            pltpu.VMEM((R_DEV, 2 * LAYERS, HEADS, D_LAT), F32),
            pltpu.VMEM((R_DEV, 2 * LAYERS, HEADS, 256), F32),
        )
        out_specs = (VMEM, VMEM)
    n = len(plan) + (1 if panels is not None else 0)
    tiles = R_DEV * LAYERS * len(halves) * n
    return pl.pallas_call(
        functools.partial(flash_kernel, plan, panels is not None, halves, first, last, per_step, len(arrays)),
        out_shape=out_shape,
        in_specs=specs,
        out_specs=out_specs,
        scratch_shapes=[pltpu.VMEM((TILE * n, D_LAT), BF), pltpu.VMEM((D_ROPE, TILE * n), BF)]
        * (LAYERS * len(halves) * per_step),
        input_output_aliases=aliases,
        cost_estimate=pl.CostEstimate(
            flops=3 * tiles * HEADS * TILE * (2 * D_LAT + D_ROPE), bytes_accessed=4 << 20, transcendentals=tiles * HEADS * TILE
        ),
        compiler_params=pltpu.CompilerParams(vmem_limit_bytes=30 << 20),
        name=name,
    )(*ops)


def place(y, z, c):
    return ((y % NY) * NZ + z % NZ) * 2 + c


def send(x, moves):
    pairs = [
        (place(y + move[0], z + move[1], c), place(y, z, c))
        for c, move in moves.items()
        for y in range(NY)
        for z in range(NZ)
    ]
    return lax.ppermute(x, PLANE, pairs)


def from_role(x, shift):
    return lax.ppermute(x, "role", [(i, (i - shift) % ROLES) for i in range(ROLES)])


def from_core(x):
    return lax.ppermute(x, "core", [(0, 1), (1, 0)])


def shards(q_latent, q_rope, pool_latent, pool_rope, panel_latent, panel_rope, panel_from, prefix_id, block_mask, suffix_len):
    own = pack_blocks(pool_latent, pool_rope)

    u0 = send(own, {0: (1, 0), 1: (0, 1)})
    d0 = send(own, {0: (-1, 0), 1: (0, -1)})
    t0 = send(own, {0: (2, 0)})
    wanted = [from_role(panel_from, k) for k in (1, 2, 3)]
    own_ints = jnp.concatenate([prefix_id, suffix_len.reshape(-1), panel_from, block_mask.reshape(-1)])
    ints = jnp.concatenate([own_ints, from_core(own_ints)])
    m1 = stack([own, u0, d0, t0], "stack1")

    up, dn = {0: (0, 1), 1: (1, 0)}, {0: (0, -1), 1: (-1, 0)}
    u1, d1 = send(m1, up), send(m1, dn)
    a2, a2n = send(u0, {1: (0, 1)}), send(d0, {1: (0, -1)})
    rope_own = q_rope.reshape(R_DEV, LAYERS, HEADS, D_ROPE)
    q_own = [q_latent, rope_own]
    q_par = [from_core(q_latent), from_core(rope_own)]
    sent = pick_panels(wanted, panel_latent, panel_rope)
    got = [from_role(x, -k) for k, x in zip((1, 2, 3), sent)]

    m2u, m2d = build(
        u1, d1, [a2, a2n], [("x", 0), ("x", 1), ("up", 0), ("up", 1)], [("x", 0), ("x", 1), ("dn", 2)], "build2", after=[*sent, q_par[0]]
    )
    u2, d2 = send(m2u, up), send(m2d, dn)
    a3, a3n = send(a2, {1: (0, 1)}), send(a2n, {1: (0, -1)})

    m3u, m3d = build(
        u2,
        d2,
        [a3, a3n],
        [("x", 0), ("x", 1), ("up", 0)],
        [("x", 0), ("x", 1), ("dn", 1)],
        "build3",
        after=[got[1], q_par[1], ints],
    )
    u3, d3 = send(m3u, up), send(m3d, dn)
    a4 = send(a3, {1: (0, 1)})
    t3 = send(stack([a3, a3n], "stack3", [a4]), {1: (2, 0)})
    queries = (q_own, q_par)
    plan = []
    for dz, array, index in ((0, 0, 0), (1, 1, 1), (-1, 2, 2)):
        far = ((3, 2), (3, 3), (4, 2))[index]
        plan.append((dz, array, [(0, index), (1, index), far, (2, index)]))
    state = flash("flash_near", plan, [m1, u1, d1, u2, d2], ints, queries)

    m4u, m4d = build(u3, d3, [a4], [("x", 0)], [("x", 0)], "build4", 2, 0, 2, [got[0], got[2], state[1]])
    u4, d4 = send(m4u, up), send(m4d, dn)
    t4 = send(a4, {1: (2, 0)})
    plan = []
    for k, dz in enumerate((2, -2, 3, -3)):
        slab = (0, 1, 2, 3)[k]
        i = k % 2
        near, back = ((0, i), (1, i)) if k < 2 else ((2, i), (3, i))
        far = ((2, 2), (3, 2), (8, 0), (8, 1))[k]
        plan.append((dz, slab, [(4 + k, None), near, far, back]))
    state = flash(
        "flash_mid",
        plan,
        [u2, d2, u3, d3, a2, a2n, a3, a3n, t3],
        ints,
        queries,
        state,
    )

    plan = [(4, (0, 1), [(2, None), (0, 0), (3, None), (1, 0)])]
    arrays = [u4, d4, a4, t4]
    part = flash("flash_far_par", plan, arrays, ints, queries, state, None, (1,), "par")
    recv = from_core(part)
    return flash("flash_far_own", plan, arrays, ints, queries, state, [*got, panel_latent, panel_rope], (0,), "own", recv)


def solution(mesh):
    fine = Mesh(mesh.devices.reshape(ROLES, 2, 2, NZ, 2), NAMES)
    rows = P(NAMES)
    blocks = P(None, NAMES)
    return jax.shard_map(
        shards,
        mesh=fine,
        in_specs=(rows, rows, blocks, blocks, rows, rows, rows, rows, rows, rows),
        out_specs=rows,
        check_vma=False,
    )
```

```python
import functools
import math

import jax
import jax.numpy as jnp
from jax import lax
from jax.experimental import pallas as pl
from jax.experimental.pallas import tpu as pltpu
from jax.sharding import Mesh
from jax.sharding import PartitionSpec as P

HEADS = 128
D_LAT = 512
D_ROPE = 64
LAYERS = 2
TILE = 128
ROWS = 144
R_DEV = 6
ROLES = 4
NY = 4
NZ = 8
NAMES = ("role", "yh", "yl", "z", "core")
PLANE = ("yh", "yl", "z", "core")

LOG2E = math.log2(math.e)
LOG2_SCALE = 192.0 ** (-0.5) * LOG2E
NEG = -1e30
OWN_INTS = R_DEV * 19
WIDE = D_LAT + 128

VMEM = pl.BlockSpec(memory_space=pltpu.VMEM)
SMEM = pl.BlockSpec(memory_space=pltpu.SMEM)
ANY = pl.BlockSpec(memory_space=pl.ANY)
BF = jnp.bfloat16
F32 = jnp.float32


def unit(*lead):
    return jax.ShapeDtypeStruct(lead + (LAYERS, ROWS, D_LAT), BF)


def pack_into(out, lat, rope):
    out[:TILE, :] = lat[...]
    for j in range(4):
        out[TILE:, 128 * j : 128 * (j + 1)] = rope[16 * j : 16 * (j + 1), :]


def pack_kernel(lat, rope, out):
    for layer in range(LAYERS):
        pack_into(out.at[layer], lat.at[layer, 0], rope.at[layer, 0])


def pack_blocks(lat, rope):
    return pl.pallas_call(pack_kernel, out_shape=unit(), in_specs=[VMEM, VMEM], out_specs=VMEM, name="pack_blocks")(lat, rope)


def stack_kernel(n, *refs):
    out = refs[-1]
    for i, ref in enumerate(refs[:n]):
        out[i] = ref[...]


def stack(parts, name, after=()):
    return pl.pallas_call(
        functools.partial(stack_kernel, len(parts)),
        out_shape=unit(len(parts)),
        in_specs=[VMEM] * len(parts) + [ANY] * len(after),
        out_specs=VMEM,
        name=name,
    )(*parts, *after)


def build_kernel(up_plan, dn_plan, first_up, first_dn, n_parts, up_in, dn_in, *refs):
    parts, (up, dn) = refs[:n_parts], refs[-2:]
    n = up.shape[0]
    core = lax.axis_index("core")

    @pl.when(core == 0)
    def _():
        for i in range(n):
            up[i] = up_in[first_up + i]
            dn[i] = dn_in[first_dn + i]

    @pl.when(core == 1)
    def _():
        for out, plan in ((up, up_plan), (dn, dn_plan)):
            for i in range(n):
                if i < len(plan):
                    kind, index = plan[i]
                    out[i] = {"up": up_in, "dn": dn_in}[kind][index] if kind in ("up", "dn") else parts[index][...]
                else:
                    out[i] = jnp.zeros(out.shape[1:], out.dtype)


def build(up_in, dn_in, parts, up_plan, dn_plan, name, n=4, first_up=0, first_dn=0, after=()):
    return pl.pallas_call(
        functools.partial(build_kernel, up_plan, dn_plan, first_up, first_dn, len(parts)),
        out_shape=(unit(n), unit(n)),
        in_specs=[VMEM] * (2 + len(parts)) + [ANY] * len(after),
        out_specs=(VMEM, VMEM),
        compiler_params=pltpu.CompilerParams(vmem_limit_bytes=10 << 20),
        name=name,
    )(up_in, dn_in, *parts, *after)


def pick_kernel(wanted1, wanted2, wanted3, lat, rope, *outs):
    role = lax.axis_index("role")
    for wanted, out in zip((wanted1, wanted2, wanted3), outs):
        first, second, seen = jnp.int32(0), jnp.int32(0), jnp.int32(0)
        for s in range(R_DEV):
            hit = wanted[s] == role
            first = jnp.where(hit & (seen == 0), s, first)
            second = jnp.where(hit & (seen == 1), s, second)
            seen = seen + hit.astype(jnp.int32)
        for j, slot in enumerate((first, second)):
            for layer in range(LAYERS):
                pack_into(out.at[j, layer], lat.at[slot, layer], rope.at[slot, layer])


def pick_panels(wanted, lat, rope):
    return pl.pallas_call(
        pick_kernel,
        out_shape=(unit(2),) * 3,
        in_specs=[SMEM] * 3 + [VMEM, VMEM],
        out_specs=(VMEM,) * 3,
        compiler_params=pltpu.CompilerParams(vmem_limit_bytes=10 << 20),
        name="pick_panels",
    )(*wanted, lat, rope)


def flash_kernel(plan, panel, halves, first, last, per_step, n_arrays, *refs):
    refs = list(refs)

    def take(count):
        taken = refs[:count]
        del refs[:count]
        return taken

    ints = take(1)[0]
    queries = [take(2) for _ in halves]
    arrays = take(n_arrays)
    if panel:
        got1, got2, got3, own_lat, own_rope = take(5)
    state_in = None if first else take(2)
    recv = take(1)[0] if last == "own" else None
    state_out = take(2) if not last else None
    out = take(1)[0] if last else None
    scratch = refs
    core, role, row, col = (lax.axis_index(name) for name in ("core", "role", ("yh", "yl"), "z"))

    def prefix(half, r):
        return ints[OWN_INTS * half + r]

    def length(half, r):
        return ints[OWN_INTS * half + R_DEV + r]

    def source(r):
        return ints[2 * R_DEV + r]

    def live(half, r, block):
        return ints[OWN_INTS * half + 3 * R_DEV + 16 * r + block] == 1

    def one_step(step, carry):
        jobs = [(q, h, half) for q in range(per_step) for h, half in enumerate(halves)]

        def keys_of(q, h, layer):
            k = 2 * ((q * len(halves) + h) * LAYERS + layer)
            return scratch[k], scratch[k + 1]

        def put(q, h, i, place, dynamic=None):
            array, index = place
            if dynamic is not None:
                index = dynamic
            for layer in range(LAYERS):
                keys, rope_keys = keys_of(q, h, layer)
                tile = arrays[array].at[layer] if index is None else arrays[array].at[index, layer]
                fill(keys, rope_keys, i, tile)

        def fill(keys, rope_keys, i, tile):
            keys[TILE * i : TILE * (i + 1), :] = tile[:TILE, :]
            for j in range(4):
                rope_keys[16 * j : 16 * (j + 1), TILE * i : TILE * (i + 1)] = tile[TILE:, 128 * j : 128 * (j + 1)]

        def row_of(q, half):
            return (prefix(half, step * per_step + q) - row + NY) % NY

        @pl.when(core == 0)
        def _():
            for q, h, half in jobs:
                dy = row_of(q, half)
                slot = jnp.where(dy == 2, 3, jnp.where(dy == 3, 2, dy))
                for i, (_, places, _) in enumerate(plan):
                    if isinstance(places, int):
                        put(q, h, i, (places, None), slot)
                    else:
                        @pl.when(slot < 2)
                        def _():
                            put(q, h, i, (places[0], None), slot)

                        @pl.when(slot >= 2)
                        def _():
                            put(q, h, i, (places[1], None), slot - 2)

        @pl.when(core == 1)
        def _():
            for q, h, half in jobs:
                dy = row_of(q, half)
                for d in range(NY):

                    @pl.when(dy == d)
                    def _():
                        for i, (_, _, places) in enumerate(plan):
                            put(q, h, i, places[d])

        if panel:
            for q, h, half in jobs:
                if half == 1:
                    continue
                i = len(plan)
                r = step * per_step + q
                shift = (role - source(r) + ROLES) % ROLES
                rank = jnp.int32(0)
                for s in range(R_DEV):
                    rank = rank + ((s < r) & (source(s) == source(r))).astype(jnp.int32)
                rank = jnp.minimum(rank, 1)

                @pl.when(shift == 0)
                def _():
                    for layer in range(LAYERS):
                        keys, rope_keys = keys_of(q, h, layer)
                        keys[TILE * i : TILE * (i + 1), :] = own_lat[r, layer]
                        rope_keys[:, TILE * i : TILE * (i + 1)] = own_rope[r, layer]

                for k, got in enumerate((got1, got2, got3)):

                    @pl.when(shift == k + 1)
                    def _():
                        for layer in range(LAYERS):
                            fill(*keys_of(q, h, layer), i, got.at[rank, layer])

        def chain(q, h, half, layer):
            r = step * per_step + q
            u = 2 * half + layer
            keys, rope_keys = keys_of(q, h, layer)
            n = len(plan) + (1 if panel and half == 0 else 0)
            q_lat, q_rope = queries[h][0][r, layer], queries[h][1][r, layer]
            width = n * TILE
            scores = lax.dot_general(q_lat, keys[:width, :], (((1,), (1,)), ((), ())), preferred_element_type=F32)
            scores = scores + jnp.dot(q_rope, rope_keys[:, :width], preferred_element_type=F32)
            yield
            pieces = []
            for i in range(n):
                piece = scores[:, TILE * i : TILE * (i + 1)] * LOG2_SCALE
                if i == len(plan):
                    token = lax.broadcasted_iota(jnp.int32, (HEADS, TILE), 1)
                    piece = jnp.where(token < length(half, r), piece, NEG)
                else:
                    block = 2 * ((col + (plan[i][0] + NZ)) % NZ) + core
                    piece = piece + jnp.where(live(half, r, block), 0.0, NEG)
                pieces.append(piece)
            top = functools.reduce(jnp.maximum, pieces)
            top = jnp.broadcast_to(jnp.max(top, axis=1, keepdims=True), (HEADS, 128))
            if not first:
                acc_in, ml_in = state_in
                old = ml_in[r, u, :, :128]
                top = jnp.maximum(old, top)
                fade = jnp.exp2(old - top)
            pieces = [jnp.exp2(piece - top) for piece in pieces]
            total = functools.reduce(jnp.add, pieces)
            if not first:
                total = total + fade * ml_in[r, u, :, 128:]
            weights = jnp.concatenate([piece.astype(BF) for piece in pieces], axis=1) if n > 1 else pieces[0].astype(BF)
            yield
            acc = jnp.dot(weights, keys[:width, :], preferred_element_type=F32)
            acc = [acc[:, 128 * j : 128 * (j + 1)] for j in range(4)]
            if not first:
                acc = [acc[j] + acc_in[r, u, :, 128 * j : 128 * (j + 1)] * fade for j in range(4)]
            yield
            if not last:
                acc_out, ml_out = state_out
                for j in range(4):
                    acc_out[r, u, :, 128 * j : 128 * (j + 1)] = acc[j]
                ml_out[r, u, :, :128] = top
                ml_out[r, u, :, 128:] = total
                return
            total = jnp.broadcast_to(jnp.sum(total, axis=1, keepdims=True), (HEADS, 128))
            if last == "par":
                lse = top + jnp.log(total) * LOG2E
                high = lse.astype(BF).astype(F32)
                mid = (lse - high).astype(BF).astype(F32)
                low = lse - high - mid
                lane = lax.broadcasted_iota(jnp.int32, (HEADS, 128), 1)
                tail = jnp.where(lane == 0, high, jnp.where(lane == 1, mid, jnp.where(lane == 2, low, 0.0)))
                inverse = 1.0 / total
                for j in range(4):
                    out[r, layer, :, 128 * j : 128 * (j + 1)] = (acc[j] * inverse).astype(BF)
                out[r, layer, :, D_LAT:] = tail.astype(BF)
            else:
                tail = recv[r, layer, :, D_LAT:].astype(F32)
                theirs = jnp.broadcast_to(jnp.sum(tail, axis=1, keepdims=True), (HEADS, 128))
                most = jnp.maximum(top, theirs)
                ours, theirs = jnp.exp2(top - most), jnp.exp2(theirs - most)
                scale = 1.0 / (total * ours + theirs)
                ours, theirs = ours * scale, theirs * scale
                for j in range(4):
                    part = recv[r, layer, :, 128 * j : 128 * (j + 1)].astype(F32)
                    out[r, layer, :, 128 * j : 128 * (j + 1)] = (acc[j] * ours + part * theirs).astype(BF)

        chains = [chain(q, h, half, layer) for q, h, half in jobs for layer in range(LAYERS)]
        for _ in range(3):
            for c in chains:
                next(c)
        for c in chains:
            next(c, None)
        return carry

    lax.fori_loop(0, R_DEV // per_step, one_step, 0)


def flash(name, plan, arrays, ints, queries, state=None, panels=None, halves=(0, 1), last=None, recv=None, per_step=2):
    first = state is None
    ops = [ints]
    for half in halves:
        ops += queries[half]
    ops += arrays
    specs = [SMEM] + [VMEM] * (len(ops) - 1)
    if panels is not None:
        ops += panels
        specs += [VMEM] * 5
    aliases = {}
    if not first:
        if not last:
            aliases = {len(ops): 0, len(ops) + 1: 1}
        ops += state
        specs += [VMEM, VMEM]
    if last == "own":
        ops.append(recv)
        specs.append(VMEM)
    if last:
        out_shape = jax.ShapeDtypeStruct((R_DEV, LAYERS, HEADS, WIDE if last == "par" else D_LAT), BF)
        out_specs = VMEM
    else:
        out_shape = (
            pltpu.VMEM((R_DEV, 2 * LAYERS, HEADS, D_LAT), F32),
            pltpu.VMEM((R_DEV, 2 * LAYERS, HEADS, 256), F32),
        )
        out_specs = (VMEM, VMEM)
    n = len(plan) + (1 if panels is not None else 0)
    tiles = R_DEV * LAYERS * len(halves) * n
    return pl.pallas_call(
        functools.partial(flash_kernel, plan, panels is not None, halves, first, last, per_step, len(arrays)),
        out_shape=out_shape,
        in_specs=specs,
        out_specs=out_specs,
        scratch_shapes=[pltpu.VMEM((TILE * n, D_LAT), BF), pltpu.VMEM((D_ROPE, TILE * n), BF)]
        * (LAYERS * len(halves) * per_step),
        input_output_aliases=aliases,
        cost_estimate=pl.CostEstimate(
            flops=3 * tiles * HEADS * TILE * (2 * D_LAT + D_ROPE), bytes_accessed=4 << 20, transcendentals=tiles * HEADS * TILE
        ),
        compiler_params=pltpu.CompilerParams(vmem_limit_bytes=20 << 20),
        name=name,
    )(*ops)


def place(y, z, c):
    return ((y % NY) * NZ + z % NZ) * 2 + c


def send(x, moves):
    pairs = [
        (place(y + move[0], z + move[1], c), place(y, z, c))
        for c, move in moves.items()
        for y in range(NY)
        for z in range(NZ)
    ]
    return lax.ppermute(x, PLANE, pairs)


def from_role(x, shift):
    return lax.ppermute(x, "role", [(i, (i - shift) % ROLES) for i in range(ROLES)])


def from_core(x):
    return lax.ppermute(x, "core", [(0, 1), (1, 0)])


def shards(q_latent, q_rope, pool_latent, pool_rope, panel_latent, panel_rope, panel_from, prefix_id, block_mask, suffix_len):
    own = pack_blocks(pool_latent, pool_rope)

    u0 = send(own, {0: (1, 0), 1: (0, 1)})
    d0 = send(own, {0: (-1, 0), 1: (0, -1)})
    t0 = send(own, {0: (2, 0)})
    wanted = [from_role(panel_from, k) for k in (1, 2, 3)]
    rope_own = q_rope.reshape(R_DEV, LAYERS, HEADS, D_ROPE)
    q_own = [q_latent, rope_own]
    q_par = [from_core(q_latent), from_core(rope_own)]
    own_ints = jnp.concatenate([prefix_id, suffix_len.reshape(-1), panel_from, block_mask.reshape(-1)])
    ints = jnp.concatenate([own_ints, from_core(own_ints)])
    m1 = stack([own, u0, d0, t0], "stack1", [*q_par, ints])

    up, dn = {0: (0, 1), 1: (1, 0)}, {0: (0, -1), 1: (-1, 0)}
    u1, d1 = send(m1, up), send(m1, dn)
    a2, a2n = send(u0, {1: (0, 1)}), send(d0, {1: (0, -1)})
    sent = pick_panels(wanted, panel_latent, panel_rope)
    got = [from_role(x, -k) for k, x in zip((1, 2, 3), sent)]

    m2u, m2d = build(
        u1, d1, [a2, a2n], [("x", 0), ("x", 1), ("up", 0), ("up", 1)], [("x", 0), ("x", 1), ("dn", 2)], "build2", after=sent
    )
    u2, d2 = send(m2u, up), send(m2d, dn)
    a3, a3n = send(a2, {1: (0, 1)}), send(a2n, {1: (0, -1)})

    m3u, m3d = build(
        u2,
        d2,
        [a3, a3n],
        [("x", 0), ("x", 1), ("up", 0)],
        [("x", 0), ("x", 1), ("dn", 1)],
        "build3",
        after=[got[1]],
    )
    u3, d3 = send(m3u, up), send(m3d, dn)
    a4 = send(a3, {1: (0, 1)})
    queries = (q_own, q_par)
    plan = []
    for dz, array, index in ((0, 0, 0), (1, 1, 1), (-1, 2, 2)):
        far = ((3, 2), (3, 3), (4, 2))[index]
        plan.append((dz, array, [(0, index), (1, index), far, (2, index)]))
    state = flash("flash_near", plan, [m1, u1, d1, u2, d2], ints, queries)

    m4u, m4d = build(
        u3, d3, [a4], [("x", 0), ("up", 0)], [("x", 0), ("dn", 1)], "build4", 2, 0, 2, [got[0], got[2], state[1]]
    )
    u4, d4 = send(m4u, up), send(m4d, dn)
    t4 = send(a4, {1: (2, 0)})
    plan = [
        (2, 0, [(4, None), (0, 0), (2, 2), (1, 0)]),
        (-2, 1, [(5, None), (0, 1), (3, 2), (1, 1)]),
    ]
    state = flash("flash_mid", plan, [u2, d2, u3, d3, a2, a2n], ints, queries, state)

    plan = [
        (3, 0, [(4, None), (0, 0), (2, 1), (1, 0)]),
        (-3, 1, [(5, None), (0, 1), (3, 1), (1, 1)]),
        (4, (2, 3), [(6, None), (2, 0), (7, None), (3, 0)]),
    ]
    arrays = [u3, d3, u4, d4, a3, a3n, a4, t4]
    part = flash("flash_far_par", plan, arrays, ints, queries, state, None, (1,), "par", per_step=3)
    recv = from_core(part)
    panels = [*got, panel_latent, panel_rope]
    return flash("flash_far_own", plan, arrays, ints, queries, state, panels, (0,), "own", recv, per_step=3)


def solution(mesh):
    fine = Mesh(mesh.devices.reshape(ROLES, 2, 2, NZ, 2), NAMES)
    rows = P(NAMES)
    blocks = P(None, NAMES)
    return jax.shard_map(
        shards,
        mesh=fine,
        in_specs=(rows, rows, blocks, blocks, rows, rows, rows, rows, rows, rows),
        out_specs=rows,
        check_vma=False,
    )
```

```python
import functools
import math

import jax
import jax.numpy as jnp
from jax import lax
from jax.experimental import pallas as pl
from jax.experimental.pallas import tpu as pltpu
from jax.sharding import Mesh
from jax.sharding import PartitionSpec as P

HEADS = 128
D_LAT = 512
D_ROPE = 64
LAYERS = 2
TILE = 128
ROWS = 144
R_DEV = 6
ROLES = 4
NY = 4
NZ = 8
NAMES = ("role", "yh", "yl", "z", "core")
PLANE = ("yh", "yl", "z", "core")

LOG2E = math.log2(math.e)
LOG2_SCALE = 192.0 ** (-0.5) * LOG2E
NEG = -1e30
OWN_INTS = R_DEV * 19
WIDE = D_LAT + 128

VMEM = pl.BlockSpec(memory_space=pltpu.VMEM)
SMEM = pl.BlockSpec(memory_space=pltpu.SMEM)
ANY = pl.BlockSpec(memory_space=pl.ANY)
BF = jnp.bfloat16
F32 = jnp.float32


def unit(*lead):
    return jax.ShapeDtypeStruct(lead + (LAYERS, ROWS, D_LAT), BF)


def pack_into(out, lat, rope):
    out[:TILE, :] = lat[...]
    for j in range(4):
        out[TILE:, 128 * j : 128 * (j + 1)] = rope[16 * j : 16 * (j + 1), :]


def pack_kernel(lat, rope, prefix, length, source, mask, after, out, ints):
    for layer in range(LAYERS):
        pack_into(out.at[layer], lat.at[layer, 0], rope.at[layer, 0])
    for r in range(R_DEV):
        ints[r] = prefix[r]
        ints[R_DEV + r] = length[0, r]
        ints[2 * R_DEV + r] = source[r]
        for j in range(16):
            ints[3 * R_DEV + 16 * r + j] = mask[r, j]


def pack_blocks(lat, rope, prefix, length, source, mask, after):
    return pl.pallas_call(
        pack_kernel,
        out_shape=(unit(), jax.ShapeDtypeStruct((OWN_INTS,), jnp.int32)),
        in_specs=[VMEM, VMEM] + [SMEM] * 4 + [ANY],
        out_specs=(VMEM, SMEM),
        name="pack_blocks",
    )(lat, rope, prefix, length, source, mask, after)


def stack_kernel(n, *refs):
    out = refs[-1]
    for i, ref in enumerate(refs[:n]):
        out[i] = ref[...]


def stack(parts, name, after=()):
    return pl.pallas_call(
        functools.partial(stack_kernel, len(parts)),
        out_shape=unit(len(parts)),
        in_specs=[VMEM] * len(parts) + [ANY] * len(after),
        out_specs=VMEM,
        name=name,
    )(*parts, *after)


def build_kernel(up_plan, dn_plan, first_up, first_dn, n_parts, up_in, dn_in, *refs):
    parts, (up, dn) = refs[:n_parts], refs[-2:]
    n = up.shape[0]
    core = lax.axis_index("core")

    @pl.when(core == 0)
    def _():
        for i in range(n):
            up[i] = up_in[first_up + i]
            dn[i] = dn_in[first_dn + i]

    @pl.when(core == 1)
    def _():
        for out, plan in ((up, up_plan), (dn, dn_plan)):
            for i in range(n):
                if i < len(plan):
                    kind, index = plan[i]
                    out[i] = {"up": up_in, "dn": dn_in}[kind][index] if kind in ("up", "dn") else parts[index][...]
                else:
                    out[i] = jnp.zeros(out.shape[1:], out.dtype)


def build(up_in, dn_in, parts, up_plan, dn_plan, name, n=4, first_up=0, first_dn=0, after=()):
    return pl.pallas_call(
        functools.partial(build_kernel, up_plan, dn_plan, first_up, first_dn, len(parts)),
        out_shape=(unit(n), unit(n)),
        in_specs=[VMEM] * (2 + len(parts)) + [ANY] * len(after),
        out_specs=(VMEM, VMEM),
        compiler_params=pltpu.CompilerParams(vmem_limit_bytes=10 << 20),
        name=name,
    )(up_in, dn_in, *parts, *after)


def pick_kernel(wanted1, wanted2, wanted3, lat, rope, *outs):
    role = lax.axis_index("role")
    for wanted, out in zip((wanted1, wanted2, wanted3), outs):
        first, second, seen = jnp.int32(0), jnp.int32(0), jnp.int32(0)
        for s in range(R_DEV):
            hit = wanted[s] == role
            first = jnp.where(hit & (seen == 0), s, first)
            second = jnp.where(hit & (seen == 1), s, second)
            seen = seen + hit.astype(jnp.int32)
        for j, slot in enumerate((first, second)):
            for layer in range(LAYERS):
                pack_into(out.at[j, layer], lat.at[slot, layer], rope.at[slot, layer])


def pick_panels(wanted, lat, rope):
    return pl.pallas_call(
        pick_kernel,
        out_shape=(unit(2),) * 3,
        in_specs=[SMEM] * 3 + [VMEM, VMEM],
        out_specs=(VMEM,) * 3,
        compiler_params=pltpu.CompilerParams(vmem_limit_bytes=10 << 20),
        name="pick_panels",
    )(*wanted, lat, rope)


def flash_kernel(plan, panel, halves, first, last, per_step, n_arrays, n_after, *refs):
    refs = list(refs)

    def take(count):
        taken = refs[:count]
        del refs[:count]
        return taken

    ints = take(2)
    queries = [take(2) for _ in halves]
    arrays = take(n_arrays)
    if panel:
        got1, got2, got3, own_lat, own_rope = take(5)
    state_in = None if first else take(2)
    take(n_after)
    state_out = take(2) if not last else None
    out = take(1)[0] if last else None
    scratch = refs
    core, role, row, col = (lax.axis_index(name) for name in ("core", "role", ("yh", "yl"), "z"))

    def prefix(half, r):
        return ints[half][r]

    def length(half, r):
        return ints[half][R_DEV + r]

    def source(r):
        return ints[0][2 * R_DEV + r]

    def live(half, r, block):
        return ints[half][3 * R_DEV + 16 * r + block] == 1

    def one_step(step, carry):
        jobs = [(q, h, half) for q in range(per_step) for h, half in enumerate(halves)]

        def keys_of(q, h, layer):
            k = 2 * ((q * len(halves) + h) * LAYERS + layer)
            return scratch[k], scratch[k + 1]

        def put(q, h, i, place, dynamic=None):
            array, index = place
            if dynamic is not None:
                index = dynamic
            for layer in range(LAYERS):
                keys, rope_keys = keys_of(q, h, layer)
                tile = arrays[array].at[layer] if index is None else arrays[array].at[index, layer]
                fill(keys, rope_keys, i, tile)

        def fill(keys, rope_keys, i, tile):
            keys[TILE * i : TILE * (i + 1), :] = tile[:TILE, :]
            for j in range(4):
                rope_keys[16 * j : 16 * (j + 1), TILE * i : TILE * (i + 1)] = tile[TILE:, 128 * j : 128 * (j + 1)]

        def row_of(q, half):
            return (prefix(half, step * per_step + q) - row + NY) % NY

        @pl.when(core == 0)
        def _():
            for q, h, half in jobs:
                dy = row_of(q, half)
                slot = jnp.where(dy == 2, 3, jnp.where(dy == 3, 2, dy))
                for i, (_, places, _) in enumerate(plan):
                    if isinstance(places, int):
                        put(q, h, i, (places, None), slot)
                    else:
                        @pl.when(slot < 2)
                        def _():
                            put(q, h, i, (places[0], None), slot)

                        @pl.when(slot >= 2)
                        def _():
                            put(q, h, i, (places[1], None), slot - 2)

        @pl.when(core == 1)
        def _():
            for q, h, half in jobs:
                dy = row_of(q, half)
                for d in range(NY):

                    @pl.when(dy == d)
                    def _():
                        for i, (_, _, places) in enumerate(plan):
                            put(q, h, i, places[d])

        if panel:
            for q, h, half in jobs:
                if half == 1:
                    continue
                i = len(plan)
                r = step * per_step + q
                shift = (role - source(r) + ROLES) % ROLES
                rank = jnp.int32(0)
                for s in range(R_DEV):
                    rank = rank + ((s < r) & (source(s) == source(r))).astype(jnp.int32)
                rank = jnp.minimum(rank, 1)

                @pl.when(shift == 0)
                def _():
                    for layer in range(LAYERS):
                        keys, rope_keys = keys_of(q, h, layer)
                        keys[TILE * i : TILE * (i + 1), :] = own_lat[r, layer]
                        rope_keys[:, TILE * i : TILE * (i + 1)] = own_rope[r, layer]

                for k, got in enumerate((got1, got2, got3)):

                    @pl.when(shift == k + 1)
                    def _():
                        for layer in range(LAYERS):
                            fill(*keys_of(q, h, layer), i, got.at[rank, layer])

        def chain(q, h, half, layer):
            r = step * per_step + q
            u = 2 * half + layer
            keys, rope_keys = keys_of(q, h, layer)
            n = len(plan) + (1 if panel and half == 0 else 0)
            q_lat, q_rope = queries[h][0][r, layer], queries[h][1][r, layer]
            width = n * TILE
            scores = lax.dot_general(q_lat, keys[:width, :], (((1,), (1,)), ((), ())), preferred_element_type=F32)
            scores = scores + jnp.dot(q_rope, rope_keys[:, :width], preferred_element_type=F32)
            yield
            pieces = []
            for i in range(n):
                piece = scores[:, TILE * i : TILE * (i + 1)] * LOG2_SCALE
                if i == len(plan):
                    token = lax.broadcasted_iota(jnp.int32, (HEADS, TILE), 1)
                    piece = jnp.where(token < length(half, r), piece, NEG)
                else:
                    block = 2 * ((col + (plan[i][0] + NZ)) % NZ) + core
                    piece = piece + jnp.where(live(half, r, block), 0.0, NEG)
                pieces.append(piece)
            top = functools.reduce(jnp.maximum, pieces)
            top = jnp.broadcast_to(jnp.max(top, axis=1, keepdims=True), (HEADS, 128))
            if not first:
                acc_in, ml_in = state_in
                old = ml_in[r, u, :, :128]
                top = jnp.maximum(old, top)
                fade = jnp.exp2(old - top)
            pieces = [jnp.exp2(piece - top) for piece in pieces]
            total = functools.reduce(jnp.add, pieces)
            if not first:
                total = total + fade * ml_in[r, u, :, 128:]
            weights = jnp.concatenate([piece.astype(BF) for piece in pieces], axis=1) if n > 1 else pieces[0].astype(BF)
            yield
            acc = jnp.dot(weights, keys[:width, :], preferred_element_type=F32)
            acc = [acc[:, 128 * j : 128 * (j + 1)] for j in range(4)]
            if not first:
                acc = [acc[j] + acc_in[r, u, :, 128 * j : 128 * (j + 1)] * fade for j in range(4)]
            yield
            if not last:
                acc_out, ml_out = state_out
                for j in range(4):
                    acc_out[r, u, :, 128 * j : 128 * (j + 1)] = acc[j]
                ml_out[r, u, :, :128] = top
                ml_out[r, u, :, 128:] = total
                return
            total = jnp.broadcast_to(jnp.sum(total, axis=1, keepdims=True), (HEADS, 128))
            lse = top + jnp.log(total) * LOG2E
            high = lse.astype(BF).astype(F32)
            mid = (lse - high).astype(BF).astype(F32)
            low = lse - high - mid
            lane = lax.broadcasted_iota(jnp.int32, (HEADS, 128), 1)
            tail = jnp.where(lane == 0, high, jnp.where(lane == 1, mid, jnp.where(lane == 2, low, 0.0)))
            inverse = 1.0 / total
            for j in range(4):
                out[r, layer, :, 128 * j : 128 * (j + 1)] = (acc[j] * inverse).astype(BF)
            out[r, layer, :, D_LAT:] = tail.astype(BF)

        chains = [chain(q, h, half, layer) for q, h, half in jobs for layer in range(LAYERS)]
        for _ in range(3):
            for c in chains:
                next(c)
        for c in chains:
            next(c, None)
        return carry

    lax.fori_loop(0, R_DEV // per_step, one_step, 0)


def merge_kernel(acc, ml, recv, out):
    for q in range(out.shape[0]):
        r = out.shape[0] * pl.program_id(0) + q
        for layer in range(LAYERS):
            top = ml[r, layer, :, :128]
            total = jnp.broadcast_to(jnp.sum(ml[r, layer, :, 128:], axis=1, keepdims=True), (HEADS, 128))
            tail = recv[r, layer, :, D_LAT:].astype(F32)
            theirs = jnp.broadcast_to(jnp.sum(tail, axis=1, keepdims=True), (HEADS, 128))
            most = jnp.maximum(top, theirs)
            ours, theirs = jnp.exp2(top - most), jnp.exp2(theirs - most)
            scale = 1.0 / (total * ours + theirs)
            ours, theirs = ours * scale, theirs * scale
            for j in range(4):
                cols = slice(128 * j, 128 * (j + 1))
                out[q, layer, :, cols] = (acc[r, layer, :, cols] * ours + recv[r, layer, :, cols].astype(F32) * theirs).astype(BF)


def merge(state, recv):
    return pl.pallas_call(
        merge_kernel,
        grid=(3,),
        out_shape=jax.ShapeDtypeStruct((R_DEV, LAYERS, HEADS, D_LAT), BF),
        in_specs=[VMEM] * 3,
        out_specs=pl.BlockSpec((2, LAYERS, HEADS, D_LAT), lambda i: (i, 0, 0, 0)),
        compiler_params=pltpu.CompilerParams(vmem_limit_bytes=20 << 20),
        name="merge",
    )(*state, recv)


def flash(name, plan, arrays, ints, queries, state=None, panels=None, halves=(0, 1), last=False, after=(), per_step=2):
    first = state is None
    ops = list(ints)
    for half in halves:
        ops += queries[half]
    ops += arrays
    specs = [SMEM] * 2 + [VMEM] * (len(ops) - 2)
    if panels is not None:
        ops += panels
        specs += [VMEM] * 5
    aliases = {}
    if not first:
        if not last:
            aliases = {len(ops): 0, len(ops) + 1: 1}
        ops += state
        specs += [VMEM, VMEM]
    ops += after
    specs += [ANY] * len(after)
    if last:
        out_shape = jax.ShapeDtypeStruct((R_DEV, LAYERS, HEADS, WIDE), BF)
        out_specs = VMEM
    else:
        out_shape = (
            pltpu.VMEM((R_DEV, 2 * LAYERS, HEADS, D_LAT), F32),
            pltpu.VMEM((R_DEV, 2 * LAYERS, HEADS, 256), F32),
        )
        out_specs = (VMEM, VMEM)
    n = len(plan) + (1 if panels is not None else 0)
    tiles = R_DEV * LAYERS * len(halves) * n
    return pl.pallas_call(
        functools.partial(flash_kernel, plan, panels is not None, halves, first, last, per_step, len(arrays), len(after)),
        out_shape=out_shape,
        in_specs=specs,
        out_specs=out_specs,
        scratch_shapes=[pltpu.VMEM((TILE * n, D_LAT), BF), pltpu.VMEM((D_ROPE, TILE * n), BF)]
        * (LAYERS * len(halves) * per_step),
        input_output_aliases=aliases,
        cost_estimate=pl.CostEstimate(
            flops=3 * tiles * HEADS * TILE * (2 * D_LAT + D_ROPE), bytes_accessed=4 << 20, transcendentals=tiles * HEADS * TILE
        ),
        compiler_params=pltpu.CompilerParams(vmem_limit_bytes=20 << 20),
        name=name,
    )(*ops)


def place(y, z, c):
    return ((y % NY) * NZ + z % NZ) * 2 + c


def send(x, moves):
    pairs = [
        (place(y + move[0], z + move[1], c), place(y, z, c))
        for c, move in moves.items()
        for y in range(NY)
        for z in range(NZ)
    ]
    return lax.ppermute(x, PLANE, pairs)


def from_role(x, shift):
    return lax.ppermute(x, "role", [(i, (i - shift) % ROLES) for i in range(ROLES)])


def from_core(x):
    return lax.ppermute(x, "core", [(0, 1), (1, 0)])


def shards(q_latent, q_rope, pool_latent, pool_rope, panel_latent, panel_rope, panel_from, prefix_id, block_mask, suffix_len):
    rope_own = q_rope.reshape(R_DEV, LAYERS, HEADS, D_ROPE)
    own, own_ints = pack_blocks(pool_latent, pool_rope, prefix_id, suffix_len, panel_from, block_mask, rope_own)

    u0 = send(own, {0: (1, 0), 1: (0, 1)})
    d0 = send(own, {0: (-1, 0), 1: (0, -1)})
    t0 = send(own, {0: (2, 0)})
    wanted = [from_role(panel_from, k) for k in (1, 2, 3)]
    q_own = [q_latent, rope_own]
    q_par = [from_core(q_latent), from_core(rope_own)]
    ints = [own_ints, from_core(own_ints)]
    m1 = stack([own, u0, d0, t0], "stack1", [*q_par, ints[1]])

    up, dn = {0: (0, 1), 1: (1, 0)}, {0: (0, -1), 1: (-1, 0)}
    u1, d1 = send(m1, up), send(m1, dn)
    a2, a2n = send(u0, {1: (0, 1)}), send(d0, {1: (0, -1)})
    sent = pick_panels(wanted, panel_latent, panel_rope)
    got = [from_role(x, -k) for k, x in zip((1, 2, 3), sent)]

    m2u, m2d = build(
        u1, d1, [a2, a2n], [("x", 0), ("x", 1), ("up", 0), ("up", 1)], [("x", 0), ("x", 1), ("dn", 2)], "build2", after=sent
    )
    u2, d2 = send(m2u, up), send(m2d, dn)
    a3, a3n = send(a2, {1: (0, 1)}), send(a2n, {1: (0, -1)})

    m3u, m3d = build(
        u2,
        d2,
        [a3, a3n],
        [("x", 0), ("x", 1), ("up", 0)],
        [("x", 0), ("x", 1), ("dn", 1)],
        "build3",
        after=[got[1]],
    )
    u3, d3 = send(m3u, up), send(m3d, dn)
    a4 = send(a3, {1: (0, 1)})
    queries = (q_own, q_par)
    plan = []
    for dz, array, index in ((0, 0, 0), (1, 1, 1), (-1, 2, 2)):
        far = ((3, 2), (3, 3), (4, 2))[index]
        plan.append((dz, array, [(0, index), (1, index), far, (2, index)]))
    state = flash("flash_near", plan, [m1, u1, d1, u2, d2], ints, queries)

    m4u, m4d = build(
        u3, d3, [a4], [("x", 0), ("up", 0)], [("x", 0), ("dn", 1)], "build4", 2, 0, 2, [got[0], got[2], state[1]]
    )
    u4, d4 = send(m4u, up), send(m4d, dn)
    t4 = send(a4, {1: (2, 0)})
    plan = [
        (2, 0, [(4, None), (0, 0), (2, 2), (1, 0)]),
        (-2, 1, [(5, None), (0, 1), (3, 2), (1, 1)]),
    ]
    state = flash(
        "flash_mid", plan, [u2, d2, u3, d3, a2, a2n], ints, queries, state, [*got, panel_latent, panel_rope]
    )

    plan = [
        (3, 0, [(4, None), (0, 0), (2, 1), (1, 0)]),
        (-3, 1, [(5, None), (0, 1), (3, 1), (1, 1)]),
        (4, (2, 3), [(6, None), (2, 0), (7, None), (3, 0)]),
    ]
    arrays = [u3, d3, u4, d4, a3, a3n, a4, t4]
    part = flash("flash_far_par", plan, arrays, ints, queries, state, None, (1,), True, per_step=3)
    state = flash("flash_far_own", plan, arrays, ints, queries, state, None, (0,), False, [part], per_step=3)
    return merge(state, from_core(part))


def solution(mesh):
    fine = Mesh(mesh.devices.reshape(ROLES, 2, 2, NZ, 2), NAMES)
    rows = P(NAMES)
    blocks = P(None, NAMES)
    return jax.shard_map(
        shards,
        mesh=fine,
        in_specs=(rows, rows, blocks, blocks, rows, rows, rows, rows, rows, rows),
        out_specs=rows,
        check_vma=False,
    )
```

```python
import functools
import math

import jax
import jax.numpy as jnp
from jax import lax
from jax.experimental import pallas as pl
from jax.experimental.pallas import tpu as pltpu
from jax.sharding import Mesh
from jax.sharding import PartitionSpec as P

HEADS = 128
D_LAT = 512
D_ROPE = 64
LAYERS = 2
TILE = 128
ROWS = 144
R_DEV = 6
ROLES = 4
NY = 4
NZ = 8
NAMES = ("role", "yh", "yl", "z", "core")
PLANE = ("yh", "yl", "z", "core")

LOG2E = math.log2(math.e)
LOG2_SCALE = 192.0 ** (-0.5) * LOG2E
NEG = -1e30
OWN_INTS = R_DEV * 19
WIDE = D_LAT + 128

VMEM = pl.BlockSpec(memory_space=pltpu.VMEM)
SMEM = pl.BlockSpec(memory_space=pltpu.SMEM)
ANY = pl.BlockSpec(memory_space=pl.ANY)
BF = jnp.bfloat16
F32 = jnp.float32
SMALL = pltpu.CompilerParams(vmem_limit_bytes=10 << 20)


def unit(*lead):
    return jax.ShapeDtypeStruct(lead + (LAYERS, ROWS, D_LAT), BF)


def pack_into(out, lat, rope):
    out[:TILE, :] = lat[...]
    for j in range(4):
        out[TILE:, 128 * j : 128 * (j + 1)] = rope[16 * j : 16 * (j + 1), :]


def pack_kernel(lat, rope, prefix, length, source, mask, after, out, ints):
    for layer in range(LAYERS):
        pack_into(out.at[layer], lat.at[layer, 0], rope.at[layer, 0])
    for r in range(R_DEV):
        ints[r] = prefix[r]
        ints[R_DEV + r] = length[0, r]
        ints[2 * R_DEV + r] = source[r]
        for j in range(16):
            ints[3 * R_DEV + 16 * r + j] = mask[r, j]


def pack_blocks(lat, rope, prefix, length, source, mask, after):
    return pl.pallas_call(
        pack_kernel,
        out_shape=(unit(), jax.ShapeDtypeStruct((OWN_INTS,), jnp.int32)),
        in_specs=[VMEM, VMEM] + [SMEM] * 4 + [ANY],
        out_specs=(VMEM, SMEM),
        compiler_params=SMALL,
        name="pack_blocks",
    )(lat, rope, prefix, length, source, mask, after)


def stack_kernel(n, *refs):
    out = refs[-1]
    for i, ref in enumerate(refs[:n]):
        out[i] = ref[...]


def stack(parts, name, after=()):
    return pl.pallas_call(
        functools.partial(stack_kernel, len(parts)),
        out_shape=unit(len(parts)),
        in_specs=[VMEM] * len(parts) + [ANY] * len(after),
        out_specs=VMEM,
        compiler_params=SMALL,
        name=name,
    )(*parts, *after)


def build_kernel(up_plan, dn_plan, first_up, first_dn, n_parts, up_in, dn_in, *refs):
    parts, (up, dn) = refs[:n_parts], refs[-2:]
    n = up.shape[0]
    core = lax.axis_index("core")

    @pl.when(core == 0)
    def _():
        for i in range(n):
            up[i] = up_in[first_up + i]
            dn[i] = dn_in[first_dn + i]

    @pl.when(core == 1)
    def _():
        for out, plan in ((up, up_plan), (dn, dn_plan)):
            for i in range(n):
                if i < len(plan):
                    kind, index = plan[i]
                    out[i] = {"up": up_in, "dn": dn_in}[kind][index] if kind in ("up", "dn") else parts[index][...]
                else:
                    out[i] = jnp.zeros(out.shape[1:], out.dtype)


def build(up_in, dn_in, parts, up_plan, dn_plan, name, n=4, first_up=0, first_dn=0, after=()):
    return pl.pallas_call(
        functools.partial(build_kernel, up_plan, dn_plan, first_up, first_dn, len(parts)),
        out_shape=(unit(n), unit(n)),
        in_specs=[VMEM] * (2 + len(parts)) + [ANY] * len(after),
        out_specs=(VMEM, VMEM),
        compiler_params=SMALL,
        name=name,
    )(up_in, dn_in, *parts, *after)


def pick_kernel(wanted1, wanted2, wanted3, lat, rope, *outs):
    role = lax.axis_index("role")
    for wanted, out in zip((wanted1, wanted2, wanted3), outs):
        first, second, seen = jnp.int32(0), jnp.int32(0), jnp.int32(0)
        for s in range(R_DEV):
            hit = wanted[s] == role
            first = jnp.where(hit & (seen == 0), s, first)
            second = jnp.where(hit & (seen == 1), s, second)
            seen = seen + hit.astype(jnp.int32)
        for j, slot in enumerate((first, second)):
            for layer in range(LAYERS):
                pack_into(out.at[j, layer], lat.at[slot, layer], rope.at[slot, layer])


def pick_panels(wanted, lat, rope):
    return pl.pallas_call(
        pick_kernel,
        out_shape=(unit(2),) * 3,
        in_specs=[SMEM] * 3 + [VMEM, VMEM],
        out_specs=(VMEM,) * 3,
        compiler_params=SMALL,
        name="pick_panels",
    )(*wanted, lat, rope)


def flash_kernel(plan, panel, halves, first, last, per_step, n_arrays, n_after, *refs):
    refs = list(refs)

    def take(count):
        taken = refs[:count]
        del refs[:count]
        return taken

    ints = take(2)
    queries = [take(2) for _ in halves]
    arrays = take(n_arrays)
    if panel:
        got1, got2, got3, own_lat, own_rope = take(5)
    state_in = None if first else take(2)
    take(n_after)
    state_out = take(2) if not last else None
    out = take(1)[0] if last else None
    scratch = refs
    core, role, row, col = (lax.axis_index(name) for name in ("core", "role", ("yh", "yl"), "z"))

    def prefix(half, r):
        return ints[half][r]

    def length(half, r):
        return ints[half][R_DEV + r]

    def source(r):
        return ints[0][2 * R_DEV + r]

    def live(half, r, block):
        return ints[half][3 * R_DEV + 16 * r + block] == 1

    def one_step(step, carry):
        jobs = [(q, h, half) for q in range(per_step) for h, half in enumerate(halves)]

        def keys_of(q, h, layer):
            k = 2 * ((q * len(halves) + h) * LAYERS + layer)
            return scratch[k], scratch[k + 1]

        def put(q, h, i, place, dynamic=None):
            array, index = place
            if dynamic is not None:
                index = dynamic
            for layer in range(LAYERS):
                keys, rope_keys = keys_of(q, h, layer)
                tile = arrays[array].at[layer] if index is None else arrays[array].at[index, layer]
                fill(keys, rope_keys, i, tile)

        def fill(keys, rope_keys, i, tile):
            keys[TILE * i : TILE * (i + 1), :] = tile[:TILE, :]
            for j in range(4):
                rope_keys[16 * j : 16 * (j + 1), TILE * i : TILE * (i + 1)] = tile[TILE:, 128 * j : 128 * (j + 1)]

        def row_of(q, half):
            return (prefix(half, step * per_step + q) - row + NY) % NY

        @pl.when(core == 0)
        def _():
            for q, h, half in jobs:
                dy = row_of(q, half)
                slot = jnp.where(dy == 2, 3, jnp.where(dy == 3, 2, dy))
                for i, (_, places, _) in enumerate(plan):
                    if isinstance(places, int):
                        put(q, h, i, (places, None), slot)
                    else:
                        @pl.when(slot < 2)
                        def _():
                            put(q, h, i, (places[0], None), slot)

                        @pl.when(slot >= 2)
                        def _():
                            put(q, h, i, (places[1], None), slot - 2)

        @pl.when(core == 1)
        def _():
            for q, h, half in jobs:
                dy = row_of(q, half)
                for d in range(NY):

                    @pl.when(dy == d)
                    def _():
                        for i, (_, _, places) in enumerate(plan):
                            put(q, h, i, places[d])

        if panel:
            for q, h, half in jobs:
                if half == 1:
                    continue
                i = len(plan)
                r = step * per_step + q
                shift = (role - source(r) + ROLES) % ROLES
                rank = jnp.int32(0)
                for s in range(R_DEV):
                    rank = rank + ((s < r) & (source(s) == source(r))).astype(jnp.int32)
                rank = jnp.minimum(rank, 1)

                @pl.when(shift == 0)
                def _():
                    for layer in range(LAYERS):
                        keys, rope_keys = keys_of(q, h, layer)
                        keys[TILE * i : TILE * (i + 1), :] = own_lat[r, layer]
                        rope_keys[:, TILE * i : TILE * (i + 1)] = own_rope[r, layer]

                for k, got in enumerate((got1, got2, got3)):

                    @pl.when(shift == k + 1)
                    def _():
                        for layer in range(LAYERS):
                            fill(*keys_of(q, h, layer), i, got.at[rank, layer])

        def chain(q, h, half, layer):
            r = step * per_step + q
            u = 2 * half + layer
            keys, rope_keys = keys_of(q, h, layer)
            n = len(plan) + (1 if panel and half == 0 else 0)
            q_lat, q_rope = queries[h][0][r, layer], queries[h][1][r, layer]
            width = n * TILE
            scores = lax.dot_general(q_lat, keys[:width, :], (((1,), (1,)), ((), ())), preferred_element_type=F32)
            scores = scores + jnp.dot(q_rope, rope_keys[:, :width], preferred_element_type=F32)
            yield
            pieces = []
            for i in range(n):
                piece = scores[:, TILE * i : TILE * (i + 1)] * LOG2_SCALE
                if i == len(plan):
                    token = lax.broadcasted_iota(jnp.int32, (HEADS, TILE), 1)
                    piece = jnp.where(token < length(half, r), piece, NEG)
                else:
                    block = 2 * ((col + (plan[i][0] + NZ)) % NZ) + core
                    piece = piece + jnp.where(live(half, r, block), 0.0, NEG)
                pieces.append(piece)
            top = functools.reduce(jnp.maximum, pieces)
            top = jnp.broadcast_to(jnp.max(top, axis=1, keepdims=True), (HEADS, 128))
            if not first:
                acc_in, ml_in = state_in
                old = ml_in[r, u, :, :128]
                top = jnp.maximum(old, top)
                fade = jnp.exp2(old - top)
            pieces = [jnp.exp2(piece - top) for piece in pieces]
            total = functools.reduce(jnp.add, pieces)
            if not first:
                total = total + fade * ml_in[r, u, :, 128:]
            weights = jnp.concatenate([piece.astype(BF) for piece in pieces], axis=1) if n > 1 else pieces[0].astype(BF)
            yield
            acc = jnp.dot(weights, keys[:width, :], preferred_element_type=F32)
            acc = [acc[:, 128 * j : 128 * (j + 1)] for j in range(4)]
            if not first:
                acc = [acc[j] + acc_in[r, u, :, 128 * j : 128 * (j + 1)] * fade for j in range(4)]
            yield
            if not last:
                acc_out, ml_out = state_out
                for j in range(4):
                    acc_out[r, u, :, 128 * j : 128 * (j + 1)] = acc[j]
                ml_out[r, u, :, :128] = top
                ml_out[r, u, :, 128:] = total
                return
            total = jnp.broadcast_to(jnp.sum(total, axis=1, keepdims=True), (HEADS, 128))
            lse = top + jnp.log(total) * LOG2E
            high = lse.astype(BF).astype(F32)
            mid = (lse - high).astype(BF).astype(F32)
            low = lse - high - mid
            lane = lax.broadcasted_iota(jnp.int32, (HEADS, 128), 1)
            tail = jnp.where(lane == 0, high, jnp.where(lane == 1, mid, jnp.where(lane == 2, low, 0.0)))
            inverse = 1.0 / total
            for j in range(4):
                out[r, layer, :, 128 * j : 128 * (j + 1)] = (acc[j] * inverse).astype(BF)
            out[r, layer, :, D_LAT:] = tail.astype(BF)

        chains = [chain(q, h, half, layer) for q, h, half in jobs for layer in range(LAYERS)]
        for _ in range(3):
            for c in chains:
                next(c)
        for c in chains:
            next(c, None)
        return carry

    lax.fori_loop(0, R_DEV // per_step, one_step, 0)


def merge_kernel(acc, ml, recv, out):
    for q in range(out.shape[0]):
        r = out.shape[0] * pl.program_id(0) + q
        for layer in range(LAYERS):
            top = ml[r, layer, :, :128]
            total = jnp.broadcast_to(jnp.sum(ml[r, layer, :, 128:], axis=1, keepdims=True), (HEADS, 128))
            tail = recv[r, layer, :, D_LAT:].astype(F32)
            theirs = jnp.broadcast_to(jnp.sum(tail, axis=1, keepdims=True), (HEADS, 128))
            most = jnp.maximum(top, theirs)
            ours, theirs = jnp.exp2(top - most), jnp.exp2(theirs - most)
            scale = 1.0 / (total * ours + theirs)
            ours, theirs = ours * scale, theirs * scale
            for j in range(4):
                cols = slice(128 * j, 128 * (j + 1))
                out[q, layer, :, cols] = (acc[r, layer, :, cols] * ours + recv[r, layer, :, cols].astype(F32) * theirs).astype(BF)


def merge(state, recv):
    return pl.pallas_call(
        merge_kernel,
        grid=(3,),
        out_shape=jax.ShapeDtypeStruct((R_DEV, LAYERS, HEADS, D_LAT), BF),
        in_specs=[VMEM] * 3,
        out_specs=pl.BlockSpec((2, LAYERS, HEADS, D_LAT), lambda i: (i, 0, 0, 0)),
        compiler_params=pltpu.CompilerParams(vmem_limit_bytes=20 << 20),
        name="merge",
    )(*state, recv)


def flash(name, plan, arrays, ints, queries, state=None, panels=None, halves=(0, 1), last=False, after=(), per_step=2):
    first = state is None
    ops = list(ints)
    for half in halves:
        ops += queries[half]
    ops += arrays
    specs = [SMEM] * 2 + [VMEM] * (len(ops) - 2)
    if panels is not None:
        ops += panels
        specs += [VMEM] * 5
    aliases = {}
    if not first:
        if not last:
            aliases = {len(ops): 0, len(ops) + 1: 1}
        ops += state
        specs += [VMEM, VMEM]
    ops += after
    specs += [ANY] * len(after)
    if last:
        out_shape = jax.ShapeDtypeStruct((R_DEV, LAYERS, HEADS, WIDE), BF)
        out_specs = VMEM
    else:
        out_shape = (
            pltpu.VMEM((R_DEV, 2 * LAYERS, HEADS, D_LAT), F32),
            pltpu.VMEM((R_DEV, 2 * LAYERS, HEADS, 256), F32),
        )
        out_specs = (VMEM, VMEM)
    n = len(plan) + (1 if panels is not None else 0)
    tiles = R_DEV * LAYERS * len(halves) * n
    return pl.pallas_call(
        functools.partial(flash_kernel, plan, panels is not None, halves, first, last, per_step, len(arrays), len(after)),
        out_shape=out_shape,
        in_specs=specs,
        out_specs=out_specs,
        scratch_shapes=[pltpu.VMEM((TILE * n, D_LAT), BF), pltpu.VMEM((D_ROPE, TILE * n), BF)]
        * (LAYERS * len(halves) * per_step),
        input_output_aliases=aliases,
        cost_estimate=pl.CostEstimate(
            flops=3 * tiles * HEADS * TILE * (2 * D_LAT + D_ROPE), bytes_accessed=4 << 20, transcendentals=tiles * HEADS * TILE
        ),
        compiler_params=pltpu.CompilerParams(vmem_limit_bytes=20 << 20),
        name=name,
    )(*ops)


def place(y, z, c):
    return ((y % NY) * NZ + z % NZ) * 2 + c


def send(x, moves):
    pairs = [
        (place(y + move[0], z + move[1], c), place(y, z, c))
        for c, move in moves.items()
        for y in range(NY)
        for z in range(NZ)
    ]
    return lax.ppermute(x, PLANE, pairs)


def from_role(x, shift):
    return lax.ppermute(x, "role", [(i, (i - shift) % ROLES) for i in range(ROLES)])


def from_core(x):
    return lax.ppermute(x, "core", [(0, 1), (1, 0)])


def shards(q_latent, q_rope, pool_latent, pool_rope, panel_latent, panel_rope, panel_from, prefix_id, block_mask, suffix_len):
    rope_own = q_rope.reshape(R_DEV, LAYERS, HEADS, D_ROPE)
    own, own_ints = pack_blocks(pool_latent, pool_rope, prefix_id, suffix_len, panel_from, block_mask, rope_own)

    u0 = send(own, {0: (1, 0), 1: (0, 1)})
    d0 = send(own, {0: (-1, 0), 1: (0, -1)})
    t0 = send(own, {0: (2, 0)})
    wanted = [from_role(panel_from, k) for k in (1, 2, 3)]
    q_own = [q_latent, rope_own]
    q_par = [from_core(q_latent), from_core(rope_own)]
    ints = [own_ints, from_core(own_ints)]
    m1 = stack([own, u0, d0, t0], "stack1", [*wanted, q_par[0]])

    up, dn = {0: (0, 1), 1: (1, 0)}, {0: (0, -1), 1: (-1, 0)}
    u1, d1 = send(m1, up), send(m1, dn)
    a2, a2n = send(u0, {1: (0, 1)}), send(d0, {1: (0, -1)})
    sent = pick_panels(wanted, panel_latent, panel_rope)
    got = [from_role(x, -k) for k, x in zip((1, 2, 3), sent)]

    m2u, m2d = build(
        u1, d1, [a2, a2n], [("x", 0), ("x", 1), ("up", 0), ("up", 1)], [("x", 0), ("x", 1), ("dn", 2)], "build2", after=[*sent, q_par[1], ints[1]]
    )
    u2, d2 = send(m2u, up), send(m2d, dn)
    a3, a3n = send(a2, {1: (0, 1)}), send(a2n, {1: (0, -1)})

    m3u, m3d = build(
        u2,
        d2,
        [a3, a3n],
        [("x", 0), ("x", 1), ("up", 0)],
        [("x", 0), ("x", 1), ("dn", 1)],
        "build3",
        after=[got[1]],
    )
    u3, d3 = send(m3u, up), send(m3d, dn)
    a4 = send(a3, {1: (0, 1)})
    queries = (q_own, q_par)
    plan = []
    for dz, array, index in ((0, 0, 0), (1, 1, 1), (-1, 2, 2)):
        far = ((3, 2), (3, 3), (4, 2))[index]
        plan.append((dz, array, [(0, index), (1, index), far, (2, index)]))
    state = flash("flash_near", plan, [m1, u1, d1, u2, d2], ints, queries)
    t4 = send(stack([a4], "stack4", [state[1]]), {1: (2, 0)})

    m4u, m4d = build(
        u3, d3, [a4], [("x", 0), ("up", 0)], [("x", 0), ("dn", 1)], "build4", 2, 0, 2, [got[0], got[2], state[1], t4]
    )
    u4, d4 = send(m4u, up), send(m4d, dn)
    plan = [
        (2, 0, [(4, None), (0, 0), (2, 2), (1, 0)]),
        (-2, 1, [(5, None), (0, 1), (3, 2), (1, 1)]),
    ]
    state = flash(
        "flash_mid", plan, [u2, d2, u3, d3, a2, a2n], ints, queries, state, [*got, panel_latent, panel_rope]
    )

    plan = [
        (3, 0, [(4, None), (0, 0), (2, 1), (1, 0)]),
        (-3, 1, [(5, None), (0, 1), (3, 1), (1, 1)]),
        (4, (2, 3), [(6, None), (2, 0), (7, 0), (3, 0)]),
    ]
    arrays = [u3, d3, u4, d4, a3, a3n, a4, t4]
    part = flash("flash_far_par", plan, arrays, ints, queries, state, None, (1,), True, per_step=3)
    state = flash("flash_far_own", plan, arrays, ints, queries, state, None, (0,), False, [part], per_step=3)
    return merge(state, from_core(part))


def solution(mesh):
    fine = Mesh(mesh.devices.reshape(ROLES, 2, 2, NZ, 2), NAMES)
    rows = P(NAMES)
    blocks = P(None, NAMES)
    return jax.shard_map(
        shards,
        mesh=fine,
        in_specs=(rows, rows, blocks, blocks, rows, rows, rows, rows, rows, rows),
        out_specs=rows,
        check_vma=False,
    )
```

```python
import functools
import math

import jax
import jax.numpy as jnp
from jax import lax
from jax.experimental import pallas as pl
from jax.experimental.pallas import tpu as pltpu
from jax.sharding import Mesh
from jax.sharding import PartitionSpec as P

HEADS = 128
D_LAT = 512
D_ROPE = 64
LAYERS = 2
TILE = 128
ROWS = 144
R_DEV = 6
ROLES = 4
NY = 4
NZ = 8
NAMES = ("role", "yh", "yl", "z", "core")
PLANE = ("yh", "yl", "z", "core")

LOG2E = math.log2(math.e)
LOG2_SCALE = 192.0 ** (-0.5) * LOG2E
NEG = -1e30
OWN_INTS = R_DEV * 19
WIDE = D_LAT + 128

VMEM = pl.BlockSpec(memory_space=pltpu.VMEM)
SMEM = pl.BlockSpec(memory_space=pltpu.SMEM)
ANY = pl.BlockSpec(memory_space=pl.ANY)
BF = jnp.bfloat16
F32 = jnp.float32
SMALL = pltpu.CompilerParams(vmem_limit_bytes=10 << 20)


def unit(*lead):
    return jax.ShapeDtypeStruct(lead + (LAYERS, ROWS, D_LAT), BF)


def pack_into(out, lat, rope):
    out[:TILE, :] = lat[...]
    for j in range(4):
        out[TILE:, 128 * j : 128 * (j + 1)] = rope[16 * j : 16 * (j + 1), :]


def pack_kernel(lat, rope, prefix, length, source, mask, after, out, ints):
    for layer in range(LAYERS):
        pack_into(out.at[layer], lat.at[layer, 0], rope.at[layer, 0])
    for r in range(R_DEV):
        ints[r] = prefix[r]
        ints[R_DEV + r] = length[0, r]
        ints[2 * R_DEV + r] = source[r]
        for j in range(16):
            ints[3 * R_DEV + 16 * r + j] = mask[r, j]


def pack_blocks(lat, rope, prefix, length, source, mask, after):
    return pl.pallas_call(
        pack_kernel,
        out_shape=(unit(), jax.ShapeDtypeStruct((OWN_INTS,), jnp.int32)),
        in_specs=[VMEM, VMEM] + [SMEM] * 4 + [ANY],
        out_specs=(VMEM, SMEM),
        name="pack_blocks",
    )(lat, rope, prefix, length, source, mask, after)


def stack_kernel(n, *refs):
    out = refs[-1]
    for i, ref in enumerate(refs[:n]):
        out[i] = ref[...]


def stack(parts, name, after=()):
    return pl.pallas_call(
        functools.partial(stack_kernel, len(parts)),
        out_shape=unit(len(parts)),
        in_specs=[VMEM] * len(parts) + [ANY] * len(after),
        out_specs=VMEM,
        compiler_params=SMALL,
        name=name,
    )(*parts, *after)


def build_kernel(up_plan, dn_plan, first_up, first_dn, n_parts, up_in, dn_in, *refs):
    parts, (up, dn) = refs[:n_parts], refs[-2:]
    n = up.shape[0]
    core = lax.axis_index("core")

    @pl.when(core == 0)
    def _():
        for i in range(n):
            up[i] = up_in[first_up + i]
            dn[i] = dn_in[first_dn + i]

    @pl.when(core == 1)
    def _():
        for out, plan in ((up, up_plan), (dn, dn_plan)):
            for i in range(n):
                if i < len(plan):
                    kind, index = plan[i]
                    out[i] = {"up": up_in, "dn": dn_in}[kind][index] if kind in ("up", "dn") else parts[index][...]
                else:
                    out[i] = jnp.zeros(out.shape[1:], out.dtype)


def build(up_in, dn_in, parts, up_plan, dn_plan, name, n=4, first_up=0, first_dn=0, after=()):
    return pl.pallas_call(
        functools.partial(build_kernel, up_plan, dn_plan, first_up, first_dn, len(parts)),
        out_shape=(unit(n), unit(n)),
        in_specs=[VMEM] * (2 + len(parts)) + [ANY] * len(after),
        out_specs=(VMEM, VMEM),
        compiler_params=SMALL,
        name=name,
    )(up_in, dn_in, *parts, *after)


def pick_kernel(wanted1, wanted2, wanted3, lat, rope, *outs):
    role = lax.axis_index("role")
    for wanted, out in zip((wanted1, wanted2, wanted3), outs):
        first, second, seen = jnp.int32(0), jnp.int32(0), jnp.int32(0)
        for s in range(R_DEV):
            hit = wanted[s] == role
            first = jnp.where(hit & (seen == 0), s, first)
            second = jnp.where(hit & (seen == 1), s, second)
            seen = seen + hit.astype(jnp.int32)
        for j, slot in enumerate((first, second)):
            for layer in range(LAYERS):
                pack_into(out.at[j, layer], lat.at[slot, layer], rope.at[slot, layer])


def pick_panels(wanted, lat, rope):
    return pl.pallas_call(
        pick_kernel,
        out_shape=(unit(2),) * 3,
        in_specs=[SMEM] * 3 + [VMEM, VMEM],
        out_specs=(VMEM,) * 3,
        compiler_params=SMALL,
        name="pick_panels",
    )(*wanted, lat, rope)


def flash_kernel(plan, panel, halves, first, last, per_step, n_arrays, n_after, *refs):
    refs = list(refs)

    def take(count):
        taken = refs[:count]
        del refs[:count]
        return taken

    ints = take(2)
    queries = [take(2) for _ in halves]
    arrays = take(n_arrays)
    if panel:
        got1, got2, got3, own_lat, own_rope = take(5)
    state_in = None if first else take(2)
    take(n_after)
    state_out = take(2) if not last else None
    out = take(1)[0] if last else None
    scratch = refs
    core, role, row, col = (lax.axis_index(name) for name in ("core", "role", ("yh", "yl"), "z"))

    def prefix(half, r):
        return ints[half][r]

    def length(half, r):
        return ints[half][R_DEV + r]

    def source(r):
        return ints[0][2 * R_DEV + r]

    def live(half, r, block):
        return ints[half][3 * R_DEV + 16 * r + block] == 1

    def one_step(step, carry):
        jobs = [(q, h, half) for q in range(per_step) for h, half in enumerate(halves)]

        def keys_of(q, h, layer):
            k = 2 * ((q * len(halves) + h) * LAYERS + layer)
            return scratch[k], scratch[k + 1]

        def put(q, h, i, place, dynamic=None):
            array, index = place
            if dynamic is not None:
                index = dynamic
            for layer in range(LAYERS):
                keys, rope_keys = keys_of(q, h, layer)
                tile = arrays[array].at[layer] if index is None else arrays[array].at[index, layer]
                fill(keys, rope_keys, i, tile)

        def fill(keys, rope_keys, i, tile):
            keys[TILE * i : TILE * (i + 1), :] = tile[:TILE, :]
            for j in range(4):
                rope_keys[16 * j : 16 * (j + 1), TILE * i : TILE * (i + 1)] = tile[TILE:, 128 * j : 128 * (j + 1)]

        def row_of(q, half):
            return (prefix(half, step * per_step + q) - row + NY) % NY

        @pl.when(core == 0)
        def _():
            for q, h, half in jobs:
                dy = row_of(q, half)
                slot = jnp.where(dy == 2, 3, jnp.where(dy == 3, 2, dy))
                for i, (_, places, _) in enumerate(plan):
                    if isinstance(places, int):
                        put(q, h, i, (places, None), slot)
                    else:
                        @pl.when(slot < 2)
                        def _():
                            put(q, h, i, (places[0], None), slot)

                        @pl.when(slot >= 2)
                        def _():
                            put(q, h, i, (places[1], None), slot - 2)

        @pl.when(core == 1)
        def _():
            for q, h, half in jobs:
                dy = row_of(q, half)
                for d in range(NY):

                    @pl.when(dy == d)
                    def _():
                        for i, (_, _, places) in enumerate(plan):
                            put(q, h, i, places[d])

        if panel:
            for q, h, half in jobs:
                if half == 1:
                    continue
                i = len(plan)
                r = step * per_step + q
                shift = (role - source(r) + ROLES) % ROLES
                rank = jnp.int32(0)
                for s in range(R_DEV):
                    rank = rank + ((s < r) & (source(s) == source(r))).astype(jnp.int32)
                rank = jnp.minimum(rank, 1)

                @pl.when(shift == 0)
                def _():
                    for layer in range(LAYERS):
                        keys, rope_keys = keys_of(q, h, layer)
                        keys[TILE * i : TILE * (i + 1), :] = own_lat[r, layer]
                        rope_keys[:, TILE * i : TILE * (i + 1)] = own_rope[r, layer]

                for k, got in enumerate((got1, got2, got3)):

                    @pl.when(shift == k + 1)
                    def _():
                        for layer in range(LAYERS):
                            fill(*keys_of(q, h, layer), i, got.at[rank, layer])

        def chain(q, h, half, layer):
            r = step * per_step + q
            u = 2 * half + layer
            keys, rope_keys = keys_of(q, h, layer)
            n = len(plan) + (1 if panel and half == 0 else 0)
            q_lat, q_rope = queries[h][0][r, layer], queries[h][1][r, layer]
            width = n * TILE
            scores = lax.dot_general(q_lat, keys[:width, :], (((1,), (1,)), ((), ())), preferred_element_type=F32)
            scores = scores + jnp.dot(q_rope, rope_keys[:, :width], preferred_element_type=F32)
            yield
            pieces = []
            for i in range(n):
                piece = scores[:, TILE * i : TILE * (i + 1)] * LOG2_SCALE
                if i == len(plan):
                    token = lax.broadcasted_iota(jnp.int32, (HEADS, TILE), 1)
                    piece = jnp.where(token < length(half, r), piece, NEG)
                else:
                    block = 2 * ((col + (plan[i][0] + NZ)) % NZ) + core
                    piece = piece + jnp.where(live(half, r, block), 0.0, NEG)
                pieces.append(piece)
            top = functools.reduce(jnp.maximum, pieces)
            top = jnp.broadcast_to(jnp.max(top, axis=1, keepdims=True), (HEADS, 128))
            if not first:
                acc_in, ml_in = state_in
                old = ml_in[r, u, :, :128]
                top = jnp.maximum(old, top)
                fade = jnp.exp2(old - top)
            pieces = [jnp.exp2(piece - top) for piece in pieces]
            total = functools.reduce(jnp.add, pieces)
            if not first:
                total = total + fade * ml_in[r, u, :, 128:]
            weights = jnp.concatenate([piece.astype(BF) for piece in pieces], axis=1) if n > 1 else pieces[0].astype(BF)
            yield
            acc = jnp.dot(weights, keys[:width, :], preferred_element_type=F32)
            acc = [acc[:, 128 * j : 128 * (j + 1)] for j in range(4)]
            if not first:
                acc = [acc[j] + acc_in[r, u, :, 128 * j : 128 * (j + 1)] * fade for j in range(4)]
            yield
            if not last:
                acc_out, ml_out = state_out
                for j in range(4):
                    acc_out[r, u, :, 128 * j : 128 * (j + 1)] = acc[j]
                ml_out[r, u, :, :128] = top
                ml_out[r, u, :, 128:] = total
                return
            total = jnp.broadcast_to(jnp.sum(total, axis=1, keepdims=True), (HEADS, 128))
            lse = top + jnp.log(total) * LOG2E
            high = lse.astype(BF).astype(F32)
            mid = (lse - high).astype(BF).astype(F32)
            low = lse - high - mid
            lane = lax.broadcasted_iota(jnp.int32, (HEADS, 128), 1)
            tail = jnp.where(lane == 0, high, jnp.where(lane == 1, mid, jnp.where(lane == 2, low, 0.0)))
            inverse = 1.0 / total
            for j in range(4):
                out[r, layer, :, 128 * j : 128 * (j + 1)] = (acc[j] * inverse).astype(BF)
            out[r, layer, :, D_LAT:] = tail.astype(BF)

        chains = [chain(q, h, half, layer) for q, h, half in jobs for layer in range(LAYERS)]
        for _ in range(3):
            for c in chains:
                next(c)
        for c in chains:
            next(c, None)
        return carry

    lax.fori_loop(0, R_DEV // per_step, one_step, 0)


def merge_kernel(acc, ml, recv, out):
    for q in range(out.shape[0]):
        r = out.shape[0] * pl.program_id(0) + q
        for layer in range(LAYERS):
            top = ml[r, layer, :, :128]
            total = jnp.broadcast_to(jnp.sum(ml[r, layer, :, 128:], axis=1, keepdims=True), (HEADS, 128))
            tail = recv[r, layer, :, D_LAT:].astype(F32)
            theirs = jnp.broadcast_to(jnp.sum(tail, axis=1, keepdims=True), (HEADS, 128))
            most = jnp.maximum(top, theirs)
            ours, theirs = jnp.exp2(top - most), jnp.exp2(theirs - most)
            scale = 1.0 / (total * ours + theirs)
            ours, theirs = ours * scale, theirs * scale
            for j in range(4):
                cols = slice(128 * j, 128 * (j + 1))
                out[q, layer, :, cols] = (acc[r, layer, :, cols] * ours + recv[r, layer, :, cols].astype(F32) * theirs).astype(BF)


def merge(state, recv):
    return pl.pallas_call(
        merge_kernel,
        grid=(3,),
        out_shape=jax.ShapeDtypeStruct((R_DEV, LAYERS, HEADS, D_LAT), BF),
        in_specs=[VMEM] * 3,
        out_specs=pl.BlockSpec((2, LAYERS, HEADS, D_LAT), lambda i: (i, 0, 0, 0)),
        compiler_params=pltpu.CompilerParams(vmem_limit_bytes=20 << 20),
        name="merge",
    )(*state, recv)


def flash(name, plan, arrays, ints, queries, state=None, panels=None, halves=(0, 1), last=False, after=(), per_step=2):
    first = state is None
    ops = list(ints)
    for half in halves:
        ops += queries[half]
    ops += arrays
    specs = [SMEM] * 2 + [VMEM] * (len(ops) - 2)
    if panels is not None:
        ops += panels
        specs += [VMEM] * 5
    aliases = {}
    if not first:
        if not last:
            aliases = {len(ops): 0, len(ops) + 1: 1}
        ops += state
        specs += [VMEM, VMEM]
    ops += after
    specs += [ANY] * len(after)
    if last:
        out_shape = jax.ShapeDtypeStruct((R_DEV, LAYERS, HEADS, WIDE), BF)
        out_specs = VMEM
    else:
        out_shape = (
            pltpu.VMEM((R_DEV, 2 * LAYERS, HEADS, D_LAT), F32),
            pltpu.VMEM((R_DEV, 2 * LAYERS, HEADS, 256), F32),
        )
        out_specs = (VMEM, VMEM)
    n = len(plan) + (1 if panels is not None else 0)
    tiles = R_DEV * LAYERS * len(halves) * n
    return pl.pallas_call(
        functools.partial(flash_kernel, plan, panels is not None, halves, first, last, per_step, len(arrays), len(after)),
        out_shape=out_shape,
        in_specs=specs,
        out_specs=out_specs,
        scratch_shapes=[pltpu.VMEM((TILE * n, D_LAT), BF), pltpu.VMEM((D_ROPE, TILE * n), BF)]
        * (LAYERS * len(halves) * per_step),
        input_output_aliases=aliases,
        cost_estimate=pl.CostEstimate(
            flops=3 * tiles * HEADS * TILE * (2 * D_LAT + D_ROPE), bytes_accessed=4 << 20, transcendentals=tiles * HEADS * TILE
        ),
        compiler_params=pltpu.CompilerParams(vmem_limit_bytes=20 << 20),
        name=name,
    )(*ops)


def place(y, z, c):
    return ((y % NY) * NZ + z % NZ) * 2 + c


def send(x, moves):
    pairs = [
        (place(y + move[0], z + move[1], c), place(y, z, c))
        for c, move in moves.items()
        for y in range(NY)
        for z in range(NZ)
    ]
    return lax.ppermute(x, PLANE, pairs)


def from_role(x, shift):
    return lax.ppermute(x, "role", [(i, (i - shift) % ROLES) for i in range(ROLES)])


def from_core(x):
    return lax.ppermute(x, "core", [(0, 1), (1, 0)])


def shards(q_latent, q_rope, pool_latent, pool_rope, panel_latent, panel_rope, panel_from, prefix_id, block_mask, suffix_len):
    rope_own = q_rope.reshape(R_DEV, LAYERS, HEADS, D_ROPE)
    own, own_ints = pack_blocks(pool_latent, pool_rope, prefix_id, suffix_len, panel_from, block_mask, rope_own)

    u0 = send(own, {0: (1, 0), 1: (0, 1)})
    d0 = send(own, {0: (-1, 0), 1: (0, -1)})
    t0 = send(own, {0: (2, 0)})
    wanted = [from_role(panel_from, k) for k in (1, 2, 3)]
    q_own = [q_latent, rope_own]
    m1 = stack([own, u0, d0, t0], "stack1", wanted)

    up, dn = {0: (0, 1), 1: (1, 0)}, {0: (0, -1), 1: (-1, 0)}
    u1, d1 = send(m1, up), send(m1, dn)
    late_up, late_dn, late_latent, _ = lax.optimization_barrier((u0, d0, q_latent, m1))
    a2, a2n = send(late_up, {1: (0, 1)}), send(late_dn, {1: (0, -1)})
    late_rope, late_ints, _ = lax.optimization_barrier((rope_own, own_ints, a2))
    q_par = [from_core(late_latent), from_core(late_rope)]
    ints = [own_ints, from_core(late_ints)]
    sent = pick_panels(wanted, panel_latent, panel_rope)
    got = [from_role(x, -k) for k, x in zip((1, 2, 3), sent)]

    m2u, m2d = build(
        u1, d1, [a2, a2n], [("x", 0), ("x", 1), ("up", 0), ("up", 1)], [("x", 0), ("x", 1), ("dn", 2)], "build2", after=[*sent, *q_par, ints[1]]
    )
    u2, d2 = send(m2u, up), send(m2d, dn)
    a3, a3n = send(a2, {1: (0, 1)}), send(a2n, {1: (0, -1)})

    m3u, m3d = build(
        u2,
        d2,
        [a3, a3n],
        [("x", 0), ("x", 1), ("up", 0)],
        [("x", 0), ("x", 1), ("dn", 1)],
        "build3",
        after=[got[1]],
    )
    u3, d3 = send(m3u, up), send(m3d, dn)
    a4 = send(a3, {1: (0, 1)})
    queries = (q_own, q_par)
    plan = []
    for dz, array, index in ((0, 0, 0), (1, 1, 1), (-1, 2, 2)):
        far = ((3, 2), (3, 3), (4, 2))[index]
        plan.append((dz, array, [(0, index), (1, index), far, (2, index)]))
    state = flash("flash_near", plan, [m1, u1, d1, u2, d2], ints, queries)

    m4u, m4d = build(
        u3, d3, [a4], [("x", 0), ("up", 0)], [("x", 0), ("dn", 1)], "build4", 2, 0, 2, [got[0], got[2], state[1]]
    )
    u4, d4 = send(m4u, up), send(m4d, dn)
    t4 = send(a4, {1: (2, 0)})
    plan = [
        (2, 0, [(4, None), (0, 0), (2, 2), (1, 0)]),
        (-2, 1, [(5, None), (0, 1), (3, 2), (1, 1)]),
    ]
    state = flash(
        "flash_mid", plan, [u2, d2, u3, d3, a2, a2n], ints, queries, state, [*got, panel_latent, panel_rope]
    )

    plan = [
        (3, 0, [(4, None), (0, 0), (2, 1), (1, 0)]),
        (-3, 1, [(5, None), (0, 1), (3, 1), (1, 1)]),
        (4, (2, 3), [(6, None), (2, 0), (7, None), (3, 0)]),
    ]
    arrays = [u3, d3, u4, d4, a3, a3n, a4, t4]
    part = flash("flash_far_par", plan, arrays, ints, queries, state, None, (1,), True, per_step=3)
    state = flash("flash_far_own", plan, arrays, ints, queries, state, None, (0,), False, [part], per_step=3)
    return merge(state, from_core(part))


def solution(mesh):
    fine = Mesh(mesh.devices.reshape(ROLES, 2, 2, NZ, 2), NAMES)
    rows = P(NAMES)
    blocks = P(None, NAMES)
    return jax.shard_map(
        shards,
        mesh=fine,
        in_specs=(rows, rows, blocks, blocks, rows, rows, rows, rows, rows, rows),
        out_specs=rows,
        check_vma=False,
    )
```

```python
import functools
import math

import jax
import jax.numpy as jnp
from jax import lax
from jax.experimental import pallas as pl
from jax.experimental.pallas import tpu as pltpu
from jax.sharding import Mesh
from jax.sharding import PartitionSpec as P

HEADS = 128
D_LAT = 512
D_ROPE = 64
LAYERS = 2
TILE = 128
ROWS = 144
R_DEV = 6
ROLES = 4
NY = 4
NZ = 8
NAMES = ("role", "yh", "yl", "z", "core")
PLANE = ("yh", "yl", "z", "core")

LOG2E = math.log2(math.e)
LOG2_SCALE = 192.0 ** (-0.5) * LOG2E
NEG = -1e30
OWN_INTS = R_DEV * 19
WIDE = D_LAT + 128

VMEM = pl.BlockSpec(memory_space=pltpu.VMEM)
SMEM = pl.BlockSpec(memory_space=pltpu.SMEM)
ANY = pl.BlockSpec(memory_space=pl.ANY)
BF = jnp.bfloat16
F32 = jnp.float32
SMALL = pltpu.CompilerParams(vmem_limit_bytes=10 << 20)


def unit(*lead):
    return jax.ShapeDtypeStruct(lead + (LAYERS, ROWS, D_LAT), BF)


def pack_into(out, lat, rope):
    out[:TILE, :] = lat[...]
    for j in range(4):
        out[TILE:, 128 * j : 128 * (j + 1)] = rope[16 * j : 16 * (j + 1), :]


def pack_kernel(lat, rope, prefix, length, source, mask, out, ints):
    for layer in range(LAYERS):
        pack_into(out.at[layer], lat.at[layer, 0], rope.at[layer, 0])
    for r in range(R_DEV):
        ints[r] = prefix[r]
        ints[R_DEV + r] = length[0, r]
        ints[2 * R_DEV + r] = source[r]
        for j in range(16):
            ints[3 * R_DEV + 16 * r + j] = mask[r, j]


def pack_blocks(lat, rope, prefix, length, source, mask):
    return pl.pallas_call(
        pack_kernel,
        out_shape=(unit(), jax.ShapeDtypeStruct((OWN_INTS,), jnp.int32)),
        in_specs=[VMEM, VMEM] + [SMEM] * 4,
        out_specs=(VMEM, SMEM),
        name="pack_blocks",
    )(lat, rope, prefix, length, source, mask)


def stack_kernel(n, *refs):
    out = refs[-1]
    for i, ref in enumerate(refs[:n]):
        out[i] = ref[...]


def stack(parts, name, after=()):
    return pl.pallas_call(
        functools.partial(stack_kernel, len(parts)),
        out_shape=unit(len(parts)),
        in_specs=[VMEM] * len(parts) + [ANY] * len(after),
        out_specs=VMEM,
        compiler_params=SMALL,
        name=name,
    )(*parts, *after)


def build_kernel(up_plan, dn_plan, first_up, first_dn, n_parts, up_in, dn_in, *refs):
    parts, (up, dn) = refs[:n_parts], refs[-2:]
    n = up.shape[0]
    core = lax.axis_index("core")

    @pl.when(core == 0)
    def _():
        for i in range(n):
            up[i] = up_in[first_up + i]
            dn[i] = dn_in[first_dn + i]

    @pl.when(core == 1)
    def _():
        for out, plan in ((up, up_plan), (dn, dn_plan)):
            for i in range(n):
                if i < len(plan):
                    kind, index = plan[i]
                    out[i] = {"up": up_in, "dn": dn_in}[kind][index] if kind in ("up", "dn") else parts[index][...]
                else:
                    out[i] = jnp.zeros(out.shape[1:], out.dtype)


def build(up_in, dn_in, parts, up_plan, dn_plan, name, n=4, first_up=0, first_dn=0, after=()):
    return pl.pallas_call(
        functools.partial(build_kernel, up_plan, dn_plan, first_up, first_dn, len(parts)),
        out_shape=(unit(n), unit(n)),
        in_specs=[VMEM] * (2 + len(parts)) + [ANY] * len(after),
        out_specs=(VMEM, VMEM),
        compiler_params=SMALL,
        name=name,
    )(up_in, dn_in, *parts, *after)


def pick_kernel(wanted1, wanted2, wanted3, lat, rope, *outs):
    role = lax.axis_index("role")
    for wanted, out in zip((wanted1, wanted2, wanted3), outs):
        first, second, seen = jnp.int32(0), jnp.int32(0), jnp.int32(0)
        for s in range(R_DEV):
            hit = wanted[s] == role
            first = jnp.where(hit & (seen == 0), s, first)
            second = jnp.where(hit & (seen == 1), s, second)
            seen = seen + hit.astype(jnp.int32)
        for j, slot in enumerate((first, second)):
            for layer in range(LAYERS):
                pack_into(out.at[j, layer], lat.at[slot, layer], rope.at[slot, layer])


def pick_panels(wanted, lat, rope):
    return pl.pallas_call(
        pick_kernel,
        out_shape=(unit(2),) * 3,
        in_specs=[SMEM] * 3 + [VMEM, VMEM],
        out_specs=(VMEM,) * 3,
        compiler_params=SMALL,
        name="pick_panels",
    )(*wanted, lat, rope)


def flash_kernel(plans, panel, halves, first, last, per_step, n_arrays, n_after, *refs):
    refs = list(refs)

    def take(count):
        taken = refs[:count]
        del refs[:count]
        return taken

    ints = take(2)
    queries = [take(2) for _ in halves]
    arrays = take(n_arrays)
    if panel:
        got1, got2, got3, own_lat, own_rope = take(5)
    state_in = None if first else take(2)
    take(n_after)
    state_out = take(2) if not last else None
    out = take(1)[0] if last else None
    scratch = refs
    core, role, row, col = (lax.axis_index(name) for name in ("core", "role", ("yh", "yl"), "z"))

    def prefix(half, r):
        return ints[half][r]

    def length(half, r):
        return ints[half][R_DEV + r]

    def source(r):
        return ints[0][2 * R_DEV + r]

    def live(half, r, block):
        return ints[half][3 * R_DEV + 16 * r + block] == 1

    def one_step(step, carry, which, plan):
        jobs = [(q, h, half) for q in range(per_step) for h, half in enumerate(halves)]

        def keys_of(q, h, layer):
            k = 2 * ((q * len(halves) + h) * LAYERS + layer)
            return scratch[k], scratch[k + 1]

        def put(q, h, i, place, dynamic=None):
            array, index = place
            if dynamic is not None:
                index = dynamic
            for layer in range(LAYERS):
                keys, rope_keys = keys_of(q, h, layer)
                tile = arrays[array].at[layer] if index is None else arrays[array].at[index, layer]
                fill(keys, rope_keys, i, tile)

        def fill(keys, rope_keys, i, tile):
            keys[TILE * i : TILE * (i + 1), :] = tile[:TILE, :]
            for j in range(4):
                rope_keys[16 * j : 16 * (j + 1), TILE * i : TILE * (i + 1)] = tile[TILE:, 128 * j : 128 * (j + 1)]

        def row_of(q, half):
            return (prefix(half, step * per_step + q) - row + NY) % NY

        for q, h, half in jobs:
            dy = row_of(q, half)
            if which == 0:
                slot = jnp.where(dy == 2, 3, jnp.where(dy == 3, 2, dy))
                for i, (_, places) in enumerate(plan):
                    if isinstance(places, int):
                        put(q, h, i, (places, None), slot)
                    else:

                        @pl.when(slot < 2)
                        def _():
                            put(q, h, i, (places[0], None), slot)

                        @pl.when(slot >= 2)
                        def _():
                            put(q, h, i, (places[1], None), slot - 2)

            else:
                for d in range(NY):

                    @pl.when(dy == d)
                    def _():
                        for i, (_, places) in enumerate(plan):
                            put(q, h, i, places[d])

        if panel:
            for q, h, half in jobs:
                if half == 1:
                    continue
                i = len(plan)
                r = step * per_step + q
                shift = (role - source(r) + ROLES) % ROLES
                rank = jnp.int32(0)
                for s in range(R_DEV):
                    rank = rank + ((s < r) & (source(s) == source(r))).astype(jnp.int32)
                rank = jnp.minimum(rank, 1)

                @pl.when(shift == 0)
                def _():
                    for layer in range(LAYERS):
                        keys, rope_keys = keys_of(q, h, layer)
                        keys[TILE * i : TILE * (i + 1), :] = own_lat[r, layer]
                        rope_keys[:, TILE * i : TILE * (i + 1)] = own_rope[r, layer]

                for k, got in enumerate((got1, got2, got3)):

                    @pl.when(shift == k + 1)
                    def _():
                        for layer in range(LAYERS):
                            fill(*keys_of(q, h, layer), i, got.at[rank, layer])

        def chain(q, h, half, layer):
            r = step * per_step + q
            u = 2 * half + layer
            keys, rope_keys = keys_of(q, h, layer)
            n = len(plan) + (1 if panel and half == 0 else 0)
            q_lat, q_rope = queries[h][0][r, layer], queries[h][1][r, layer]
            width = n * TILE
            scores = lax.dot_general(q_lat, keys[:width, :], (((1,), (1,)), ((), ())), preferred_element_type=F32)
            scores = scores + jnp.dot(q_rope, rope_keys[:, :width], preferred_element_type=F32)
            yield
            pieces = []
            for i in range(n):
                piece = scores[:, TILE * i : TILE * (i + 1)] * LOG2_SCALE
                if i == len(plan):
                    token = lax.broadcasted_iota(jnp.int32, (HEADS, TILE), 1)
                    piece = jnp.where(token < length(half, r), piece, NEG)
                else:
                    block = 2 * ((col + (plan[i][0] + NZ)) % NZ) + which
                    piece = piece + jnp.where(live(half, r, block), 0.0, NEG)
                pieces.append(piece)
            top = functools.reduce(jnp.maximum, pieces)
            top = jnp.broadcast_to(jnp.max(top, axis=1, keepdims=True), (HEADS, 128))
            if not first:
                acc_in, ml_in = state_in
                old = ml_in[r, u, :, :128]
                top = jnp.maximum(old, top)
                fade = jnp.exp2(old - top)
            pieces = [jnp.exp2(piece - top) for piece in pieces]
            total = functools.reduce(jnp.add, pieces)
            if not first:
                total = total + fade * ml_in[r, u, :, 128:]
            weights = jnp.concatenate([piece.astype(BF) for piece in pieces], axis=1) if n > 1 else pieces[0].astype(BF)
            yield
            acc = jnp.dot(weights, keys[:width, :], preferred_element_type=F32)
            acc = [acc[:, 128 * j : 128 * (j + 1)] for j in range(4)]
            if not first:
                acc = [acc[j] + acc_in[r, u, :, 128 * j : 128 * (j + 1)] * fade for j in range(4)]
            yield
            if not last:
                acc_out, ml_out = state_out
                for j in range(4):
                    acc_out[r, u, :, 128 * j : 128 * (j + 1)] = acc[j]
                ml_out[r, u, :, :128] = top
                ml_out[r, u, :, 128:] = total
                return
            total = jnp.broadcast_to(jnp.sum(total, axis=1, keepdims=True), (HEADS, 128))
            lse = top + jnp.log(total) * LOG2E
            high = lse.astype(BF).astype(F32)
            mid = (lse - high).astype(BF).astype(F32)
            low = lse - high - mid
            lane = lax.broadcasted_iota(jnp.int32, (HEADS, 128), 1)
            tail = jnp.where(lane == 0, high, jnp.where(lane == 1, mid, jnp.where(lane == 2, low, 0.0)))
            inverse = 1.0 / total
            for j in range(4):
                out[r, layer, :, 128 * j : 128 * (j + 1)] = (acc[j] * inverse).astype(BF)
            out[r, layer, :, D_LAT:] = tail.astype(BF)

        chains = [chain(q, h, half, layer) for q, h, half in jobs for layer in range(LAYERS)]
        for _ in range(3):
            for c in chains:
                next(c)
        for c in chains:
            next(c, None)
        return carry

    for which, plan in enumerate(plans):

        @pl.when(core == which)
        def _():
            lax.fori_loop(0, R_DEV // per_step, functools.partial(one_step, which=which, plan=plan), 0)


def merge_kernel(acc, ml, recv, out):
    for q in range(out.shape[0]):
        r = out.shape[0] * pl.program_id(0) + q
        for layer in range(LAYERS):
            top = ml[r, layer, :, :128]
            total = jnp.broadcast_to(jnp.sum(ml[r, layer, :, 128:], axis=1, keepdims=True), (HEADS, 128))
            tail = recv[r, layer, :, D_LAT:].astype(F32)
            theirs = jnp.broadcast_to(jnp.sum(tail, axis=1, keepdims=True), (HEADS, 128))
            most = jnp.maximum(top, theirs)
            ours, theirs = jnp.exp2(top - most), jnp.exp2(theirs - most)
            scale = 1.0 / (total * ours + theirs)
            ours, theirs = ours * scale, theirs * scale
            for j in range(4):
                cols = slice(128 * j, 128 * (j + 1))
                out[q, layer, :, cols] = (acc[r, layer, :, cols] * ours + recv[r, layer, :, cols].astype(F32) * theirs).astype(BF)


def merge(state, recv):
    return pl.pallas_call(
        merge_kernel,
        grid=(3,),
        out_shape=jax.ShapeDtypeStruct((R_DEV, LAYERS, HEADS, D_LAT), BF),
        in_specs=[VMEM] * 3,
        out_specs=pl.BlockSpec((2, LAYERS, HEADS, D_LAT), lambda i: (i, 0, 0, 0)),
        compiler_params=pltpu.CompilerParams(vmem_limit_bytes=20 << 20),
        name="merge",
    )(*state, recv)


def flash(name, plans, arrays, ints, queries, state=None, panels=None, halves=(0, 1), last=False, after=(), per_step=2):
    first = state is None
    ops = list(ints)
    for half in halves:
        ops += queries[half]
    ops += arrays
    specs = [SMEM] * 2 + [VMEM] * (len(ops) - 2)
    if panels is not None:
        ops += panels
        specs += [VMEM] * 5
    aliases = {}
    if not first:
        if not last:
            aliases = {len(ops): 0, len(ops) + 1: 1}
        ops += state
        specs += [VMEM, VMEM]
    ops += after
    specs += [ANY] * len(after)
    if last:
        out_shape = jax.ShapeDtypeStruct((R_DEV, LAYERS, HEADS, WIDE), BF)
        out_specs = VMEM
    else:
        out_shape = (
            pltpu.VMEM((R_DEV, 2 * LAYERS, HEADS, D_LAT), F32),
            pltpu.VMEM((R_DEV, 2 * LAYERS, HEADS, 256), F32),
        )
        out_specs = (VMEM, VMEM)
    n = max(len(plan) for plan in plans) + (1 if panels is not None else 0)
    tiles = R_DEV * LAYERS * len(halves) * n
    return pl.pallas_call(
        functools.partial(flash_kernel, plans, panels is not None, halves, first, last, per_step, len(arrays), len(after)),
        out_shape=out_shape,
        in_specs=specs,
        out_specs=out_specs,
        scratch_shapes=[pltpu.VMEM((TILE * n, D_LAT), BF), pltpu.VMEM((D_ROPE, TILE * n), BF)]
        * (LAYERS * len(halves) * per_step),
        input_output_aliases=aliases,
        cost_estimate=pl.CostEstimate(
            flops=3 * tiles * HEADS * TILE * (2 * D_LAT + D_ROPE), bytes_accessed=4 << 20, transcendentals=tiles * HEADS * TILE
        ),
        compiler_params=pltpu.CompilerParams(vmem_limit_bytes=20 << 20),
        name=name,
    )(*ops)


def place(y, z, c):
    return ((y % NY) * NZ + z % NZ) * 2 + c


def send(x, moves):
    pairs = [
        (place(y + move[0], z + move[1], c), place(y, z, c))
        for c, move in moves.items()
        for y in range(NY)
        for z in range(NZ)
    ]
    return lax.ppermute(x, PLANE, pairs)


def from_role(x, shift):
    return lax.ppermute(x, "role", [(i, (i - shift) % ROLES) for i in range(ROLES)])


def from_core(x):
    return lax.ppermute(x, "core", [(0, 1), (1, 0)])


def shards(q_latent, q_rope, pool_latent, pool_rope, panel_latent, panel_rope, panel_from, prefix_id, block_mask, suffix_len):
    rope_own = q_rope.reshape(R_DEV, LAYERS, HEADS, D_ROPE)
    own, own_ints = pack_blocks(pool_latent, pool_rope, prefix_id, suffix_len, panel_from, block_mask)

    u0 = send(own, {0: (1, 0), 1: (0, 1)})
    d0 = send(own, {0: (-1, 0), 1: (0, -1)})
    t0 = send(own, {0: (2, 0)})
    wanted = [from_role(panel_from, k) for k in (1, 2, 3)]
    q_own = [q_latent, rope_own]
    m1 = stack([own, u0, d0, t0], "stack1", [*wanted, rope_own])

    up, dn = {0: (0, 1), 1: (1, 0)}, {0: (0, -1), 1: (-1, 0)}
    u1, d1 = send(m1, up), send(m1, dn)
    late_up, late_dn, late_latent, _ = lax.optimization_barrier((u0, d0, q_latent, m1))
    a2, a2n = send(late_up, {1: (0, 1)}), send(late_dn, {1: (0, -1)})
    late_rope, late_ints, _ = lax.optimization_barrier((rope_own, own_ints, a2))
    q_par = [from_core(late_latent), from_core(late_rope)]
    ints = [own_ints, from_core(late_ints)]
    sent = pick_panels(wanted, panel_latent, panel_rope)
    got = [from_role(x, -k) for k, x in zip((1, 2, 3), sent)]

    m2u, m2d = build(
        u1, d1, [a2, a2n], [("x", 0), ("x", 1), ("up", 0), ("up", 1)], [("x", 0), ("x", 1), ("dn", 2)], "build2", after=[*sent, *q_par, ints[1]]
    )
    u2, d2 = send(m2u, up), send(m2d, dn)
    a3, a3n = send(a2, {1: (0, 1)}), send(a2n, {1: (0, -1)})

    m3u, m3d = build(
        u2,
        d2,
        [a3, a3n],
        [("x", 0), ("x", 1), ("up", 0)],
        [("x", 0), ("x", 1), ("dn", 1)],
        "build3",
        after=[got[1]],
    )
    u3, d3 = send(m3u, up), send(m3d, dn)
    a4 = send(a3, {1: (0, 1)})
    queries = (q_own, q_par)
    plans = (
        [(0, 0), (1, 1), (-1, 2), (2, 3), (-2, 4)],
        [
            (0, [(0, 0), (1, 0), (3, 2), (2, 0)]),
            (1, [(0, 1), (1, 1), (3, 3), (2, 1)]),
            (-1, [(0, 2), (1, 2), (4, 2), (2, 2)]),
        ],
    )
    state = flash("flash_near", plans, [m1, u1, d1, u2, d2], ints, queries)

    m4u, m4d = build(
        u3, d3, [a4], [("x", 0), ("up", 0)], [("x", 0), ("dn", 1)], "build4", 2, 0, 2, [got[0], got[2], state[1]]
    )
    u4, d4 = send(m4u, up), send(m4d, dn)
    t4 = send(a4, {1: (2, 0)})
    plans = (
        [(3, 2), (-3, 3)],
        [(2, [(4, None), (0, 0), (2, 2), (1, 0)]), (-2, [(5, None), (0, 1), (3, 2), (1, 1)])],
    )
    state = flash(
        "flash_mid", plans, [u2, d2, u3, d3, a2, a2n], ints, queries, state, [*got, panel_latent, panel_rope]
    )

    plans = (
        [(4, (2, 3))],
        [
            (3, [(4, None), (0, 0), (2, 1), (1, 0)]),
            (-3, [(5, None), (0, 1), (3, 1), (1, 1)]),
            (4, [(6, None), (2, 0), (7, None), (3, 0)]),
        ],
    )
    arrays = [u3, d3, u4, d4, a3, a3n, a4, t4]
    part = flash("flash_far_par", plans, arrays, ints, queries, state, None, (1,), True, per_step=3)
    state = flash("flash_far_own", plans, arrays, ints, queries, state, None, (0,), False, [part], per_step=3)
    return merge(state, from_core(part))


def solution(mesh):
    fine = Mesh(mesh.devices.reshape(ROLES, 2, 2, NZ, 2), NAMES)
    rows = P(NAMES)
    blocks = P(None, NAMES)
    return jax.shard_map(
        shards,
        mesh=fine,
        in_specs=(rows, rows, blocks, blocks, rows, rows, rows, rows, rows, rows),
        out_specs=rows,
        check_vma=False,
    )
```

```python
import functools
import math

import jax
import jax.numpy as jnp
from jax import lax
from jax.experimental import pallas as pl
from jax.experimental.pallas import tpu as pltpu
from jax.sharding import Mesh
from jax.sharding import PartitionSpec as P

HEADS = 128
D_LAT = 512
D_ROPE = 64
LAYERS = 2
TILE = 128
ROWS = 144
R_DEV = 6
ROLES = 4
NY = 4
NZ = 8
NAMES = ("role", "yh", "yl", "z", "core")
PLANE = ("yh", "yl", "z", "core")

LOG2E = math.log2(math.e)
LOG2_SCALE = 192.0 ** (-0.5) * LOG2E
NEG = -1e30
OWN_INTS = R_DEV * 19
WIDE = D_LAT + 128

VMEM = pl.BlockSpec(memory_space=pltpu.VMEM)
SMEM = pl.BlockSpec(memory_space=pltpu.SMEM)
ANY = pl.BlockSpec(memory_space=pl.ANY)
BF = jnp.bfloat16
F32 = jnp.float32
SMALL = pltpu.CompilerParams(vmem_limit_bytes=10 << 20)


def unit(*lead):
    return jax.ShapeDtypeStruct(lead + (LAYERS, ROWS, D_LAT), BF)


def pack_into(out, lat, rope):
    out[:TILE, :] = lat[...]
    for j in range(4):
        out[TILE:, 128 * j : 128 * (j + 1)] = rope[16 * j : 16 * (j + 1), :]


def pack_kernel(lat, rope, prefix, length, source, mask, out, ints):
    for layer in range(LAYERS):
        pack_into(out.at[layer], lat.at[layer, 0], rope.at[layer, 0])
    for r in range(R_DEV):
        ints[r] = prefix[r]
        ints[R_DEV + r] = length[0, r]
        ints[2 * R_DEV + r] = source[r]
        for j in range(16):
            ints[3 * R_DEV + 16 * r + j] = mask[r, j]


def pack_blocks(lat, rope, prefix, length, source, mask):
    return pl.pallas_call(
        pack_kernel,
        out_shape=(unit(), jax.ShapeDtypeStruct((OWN_INTS,), jnp.int32)),
        in_specs=[VMEM, VMEM] + [SMEM] * 4,
        out_specs=(VMEM, SMEM),
        name="pack_blocks",
    )(lat, rope, prefix, length, source, mask)


def stack_kernel(n, *refs):
    out = refs[-1]
    for i, ref in enumerate(refs[:n]):
        out[i] = ref[...]


def stack(parts, name, after=()):
    return pl.pallas_call(
        functools.partial(stack_kernel, len(parts)),
        out_shape=unit(len(parts)),
        in_specs=[VMEM] * len(parts) + [ANY] * len(after),
        out_specs=VMEM,
        compiler_params=SMALL,
        name=name,
    )(*parts, *after)


def build_kernel(up_plan, dn_plan, first_up, first_dn, n_parts, up_in, dn_in, *refs):
    parts, (up, dn) = refs[:n_parts], refs[-2:]
    n = up.shape[0]
    core = lax.axis_index("core")

    @pl.when(core == 0)
    def _():
        for i in range(n):
            up[i] = up_in[first_up + i]
            dn[i] = dn_in[first_dn + i]

    @pl.when(core == 1)
    def _():
        for out, plan in ((up, up_plan), (dn, dn_plan)):
            for i in range(n):
                if i < len(plan):
                    kind, index = plan[i]
                    out[i] = {"up": up_in, "dn": dn_in}[kind][index] if kind in ("up", "dn") else parts[index][...]
                else:
                    out[i] = jnp.zeros(out.shape[1:], out.dtype)


def build(up_in, dn_in, parts, up_plan, dn_plan, name, n=4, first_up=0, first_dn=0, after=()):
    return pl.pallas_call(
        functools.partial(build_kernel, up_plan, dn_plan, first_up, first_dn, len(parts)),
        out_shape=(unit(n), unit(n)),
        in_specs=[VMEM] * (2 + len(parts)) + [ANY] * len(after),
        out_specs=(VMEM, VMEM),
        compiler_params=SMALL,
        name=name,
    )(up_in, dn_in, *parts, *after)


def pick_kernel(wanted1, wanted2, wanted3, lat, rope, *outs):
    role = lax.axis_index("role")
    for wanted, out in zip((wanted1, wanted2, wanted3), outs):
        first, second, seen = jnp.int32(0), jnp.int32(0), jnp.int32(0)
        for s in range(R_DEV):
            hit = wanted[s] == role
            first = jnp.where(hit & (seen == 0), s, first)
            second = jnp.where(hit & (seen == 1), s, second)
            seen = seen + hit.astype(jnp.int32)
        for j, slot in enumerate((first, second)):
            for layer in range(LAYERS):
                pack_into(out.at[j, layer], lat.at[slot, layer], rope.at[slot, layer])


def pick_panels(wanted, lat, rope):
    return pl.pallas_call(
        pick_kernel,
        out_shape=(unit(2),) * 3,
        in_specs=[SMEM] * 3 + [VMEM, VMEM],
        out_specs=(VMEM,) * 3,
        compiler_params=SMALL,
        name="pick_panels",
    )(*wanted, lat, rope)


def flash_kernel(plans, panel, halves, first, last, per_step, n_arrays, n_after, *refs):
    refs = list(refs)

    def take(count):
        taken = refs[:count]
        del refs[:count]
        return taken

    ints = take(2)
    queries = [take(2) for _ in halves]
    arrays = take(n_arrays)
    if panel:
        got1, got2, got3, own_lat, own_rope = take(5)
    state_in = None if first else take(2)
    take(n_after)
    state_out = take(2) if not last else None
    out = take(1)[0] if last else None
    scratch = refs
    core, role, row, col = (lax.axis_index(name) for name in ("core", "role", ("yh", "yl"), "z"))

    def prefix(half, r):
        return ints[half][r]

    def length(half, r):
        return ints[half][R_DEV + r]

    def source(r):
        return ints[0][2 * R_DEV + r]

    def live(half, r, block):
        return ints[half][3 * R_DEV + 16 * r + block] == 1

    def one_step(step, carry, which, plan):
        jobs = [(q, h, half) for q in range(per_step) for h, half in enumerate(halves)]

        def keys_of(q, h, layer):
            k = 2 * ((q * len(halves) + h) * LAYERS + layer)
            return scratch[k], scratch[k + 1]

        def put(q, h, i, place, dynamic=None):
            array, index = place
            if dynamic is not None:
                index = dynamic
            for layer in range(LAYERS):
                keys, rope_keys = keys_of(q, h, layer)
                tile = arrays[array].at[layer] if index is None else arrays[array].at[index, layer]
                fill(keys, rope_keys, i, tile)

        def fill(keys, rope_keys, i, tile):
            keys[TILE * i : TILE * (i + 1), :] = tile[:TILE, :]
            for j in range(4):
                rope_keys[16 * j : 16 * (j + 1), TILE * i : TILE * (i + 1)] = tile[TILE:, 128 * j : 128 * (j + 1)]

        def row_of(q, half):
            return (prefix(half, step * per_step + q) - row + NY) % NY

        for q, h, half in jobs:
            dy = row_of(q, half)
            if which == 0:
                slot = jnp.where(dy == 2, 3, jnp.where(dy == 3, 2, dy))
                for i, (_, places) in enumerate(plan):
                    if isinstance(places, int):
                        put(q, h, i, (places, None), slot)
                    else:

                        @pl.when(slot < 2)
                        def _():
                            put(q, h, i, (places[0], None), slot)

                        @pl.when(slot >= 2)
                        def _():
                            put(q, h, i, (places[1], None), slot - 2)

            else:
                for d in range(NY):

                    @pl.when(dy == d)
                    def _():
                        for i, (_, places) in enumerate(plan):
                            put(q, h, i, places[d])

        if panel:
            for q, h, half in jobs:
                if half == 1:
                    continue
                i = len(plan)
                r = step * per_step + q
                shift = (role - source(r) + ROLES) % ROLES
                rank = jnp.int32(0)
                for s in range(R_DEV):
                    rank = rank + ((s < r) & (source(s) == source(r))).astype(jnp.int32)
                rank = jnp.minimum(rank, 1)

                @pl.when(shift == 0)
                def _():
                    for layer in range(LAYERS):
                        keys, rope_keys = keys_of(q, h, layer)
                        keys[TILE * i : TILE * (i + 1), :] = own_lat[r, layer]
                        rope_keys[:, TILE * i : TILE * (i + 1)] = own_rope[r, layer]

                for k, got in enumerate((got1, got2, got3)):

                    @pl.when(shift == k + 1)
                    def _():
                        for layer in range(LAYERS):
                            fill(*keys_of(q, h, layer), i, got.at[rank, layer])

        def chain(q, h, half, layer):
            r = step * per_step + q
            u = 2 * half + layer
            keys, rope_keys = keys_of(q, h, layer)
            n = len(plan) + (1 if panel and half == 0 else 0)
            q_lat, q_rope = queries[h][0][r, layer], queries[h][1][r, layer]
            width = n * TILE
            scores = lax.dot_general(q_lat, keys[:width, :], (((1,), (1,)), ((), ())), preferred_element_type=F32)
            scores = scores + jnp.dot(q_rope, rope_keys[:, :width], preferred_element_type=F32)
            yield
            pieces = []
            for i in range(n):
                piece = scores[:, TILE * i : TILE * (i + 1)] * LOG2_SCALE
                if i == len(plan):
                    token = lax.broadcasted_iota(jnp.int32, (HEADS, TILE), 1)
                    piece = jnp.where(token < length(half, r), piece, NEG)
                else:
                    block = 2 * ((col + (plan[i][0] + NZ)) % NZ) + which
                    piece = piece + jnp.where(live(half, r, block), 0.0, NEG)
                pieces.append(piece)
            top = functools.reduce(jnp.maximum, pieces)
            top = jnp.broadcast_to(jnp.max(top, axis=1, keepdims=True), (HEADS, 128))
            if not first:
                acc_in, ml_in = state_in
                old = ml_in[r, u, :, :128]
                top = jnp.maximum(old, top)
                fade = jnp.exp2(old - top)
            pieces = [jnp.exp2(piece - top) for piece in pieces]
            total = functools.reduce(jnp.add, pieces)
            if not first:
                total = total + fade * ml_in[r, u, :, 128:]
            weights = jnp.concatenate([piece.astype(BF) for piece in pieces], axis=1) if n > 1 else pieces[0].astype(BF)
            yield
            acc = jnp.dot(weights, keys[:width, :], preferred_element_type=F32)
            acc = [acc[:, 128 * j : 128 * (j + 1)] for j in range(4)]
            if not first:
                acc = [acc[j] + acc_in[r, u, :, 128 * j : 128 * (j + 1)] * fade for j in range(4)]
            yield
            if not last:
                acc_out, ml_out = state_out
                for j in range(4):
                    acc_out[r, u, :, 128 * j : 128 * (j + 1)] = acc[j]
                ml_out[r, u, :, :128] = top
                ml_out[r, u, :, 128:] = total
                return
            total = jnp.broadcast_to(jnp.sum(total, axis=1, keepdims=True), (HEADS, 128))
            lse = top + jnp.log(total) * LOG2E
            high = lse.astype(BF).astype(F32)
            mid = (lse - high).astype(BF).astype(F32)
            low = lse - high - mid
            lane = lax.broadcasted_iota(jnp.int32, (HEADS, 128), 1)
            tail = jnp.where(lane == 0, high, jnp.where(lane == 1, mid, jnp.where(lane == 2, low, 0.0)))
            inverse = 1.0 / total
            for j in range(4):
                out[r, layer, :, 128 * j : 128 * (j + 1)] = (acc[j] * inverse).astype(BF)
            out[r, layer, :, D_LAT:] = tail.astype(BF)

        chains = [chain(q, h, half, layer) for q, h, half in jobs for layer in range(LAYERS)]
        for _ in range(3):
            for c in chains:
                next(c)
        for c in chains:
            next(c, None)
        return carry

    for which, plan in enumerate(plans):

        @pl.when(core == which)
        def _():
            lax.fori_loop(0, R_DEV // per_step, functools.partial(one_step, which=which, plan=plan), 0)


def merge_kernel(acc, ml, recv, out):
    for q in range(out.shape[0]):
        r = out.shape[0] * pl.program_id(0) + q
        for layer in range(LAYERS):
            top = ml[r, layer, :, :128]
            total = jnp.broadcast_to(jnp.sum(ml[r, layer, :, 128:], axis=1, keepdims=True), (HEADS, 128))
            tail = recv[r, layer, :, D_LAT:].astype(F32)
            theirs = jnp.broadcast_to(jnp.sum(tail, axis=1, keepdims=True), (HEADS, 128))
            most = jnp.maximum(top, theirs)
            ours, theirs = jnp.exp2(top - most), jnp.exp2(theirs - most)
            scale = 1.0 / (total * ours + theirs)
            ours, theirs = ours * scale, theirs * scale
            for j in range(4):
                cols = slice(128 * j, 128 * (j + 1))
                out[q, layer, :, cols] = (acc[r, layer, :, cols] * ours + recv[r, layer, :, cols].astype(F32) * theirs).astype(BF)


def merge(state, recv):
    return pl.pallas_call(
        merge_kernel,
        grid=(3,),
        out_shape=jax.ShapeDtypeStruct((R_DEV, LAYERS, HEADS, D_LAT), BF),
        in_specs=[VMEM] * 3,
        out_specs=pl.BlockSpec((2, LAYERS, HEADS, D_LAT), lambda i: (i, 0, 0, 0)),
        compiler_params=pltpu.CompilerParams(vmem_limit_bytes=20 << 20),
        name="merge",
    )(*state, recv)


def flash(name, plans, arrays, ints, queries, state=None, panels=None, halves=(0, 1), last=False, after=(), per_step=2):
    first = state is None
    ops = list(ints)
    for half in halves:
        ops += queries[half]
    ops += arrays
    specs = [SMEM] * 2 + [VMEM] * (len(ops) - 2)
    if panels is not None:
        ops += panels
        specs += [VMEM] * 5
    aliases = {}
    if not first:
        if not last:
            aliases = {len(ops): 0, len(ops) + 1: 1}
        ops += state
        specs += [VMEM, VMEM]
    ops += after
    specs += [ANY] * len(after)
    if last:
        out_shape = jax.ShapeDtypeStruct((R_DEV, LAYERS, HEADS, WIDE), BF)
        out_specs = VMEM
    else:
        out_shape = (
            pltpu.VMEM((R_DEV, 2 * LAYERS, HEADS, D_LAT), F32),
            pltpu.VMEM((R_DEV, 2 * LAYERS, HEADS, 256), F32),
        )
        out_specs = (VMEM, VMEM)
    n = max(len(plan) for plan in plans) + (1 if panels is not None else 0)
    tiles = R_DEV * LAYERS * len(halves) * n
    return pl.pallas_call(
        functools.partial(flash_kernel, plans, panels is not None, halves, first, last, per_step, len(arrays), len(after)),
        out_shape=out_shape,
        in_specs=specs,
        out_specs=out_specs,
        scratch_shapes=[pltpu.VMEM((TILE * n, D_LAT), BF), pltpu.VMEM((D_ROPE, TILE * n), BF)]
        * (LAYERS * len(halves) * per_step),
        input_output_aliases=aliases,
        cost_estimate=pl.CostEstimate(
            flops=3 * tiles * HEADS * TILE * (2 * D_LAT + D_ROPE), bytes_accessed=4 << 20, transcendentals=tiles * HEADS * TILE
        ),
        compiler_params=pltpu.CompilerParams(vmem_limit_bytes=20 << 20),
        name=name,
    )(*ops)


def place(y, z, c):
    return ((y % NY) * NZ + z % NZ) * 2 + c


def send(x, moves):
    pairs = [
        (place(y + move[0], z + move[1], c), place(y, z, c))
        for c, move in moves.items()
        for y in range(NY)
        for z in range(NZ)
    ]
    return lax.ppermute(x, PLANE, pairs)


def from_role(x, shift):
    return lax.ppermute(x, "role", [(i, (i - shift) % ROLES) for i in range(ROLES)])


def from_core(x):
    return lax.ppermute(x, "core", [(0, 1), (1, 0)])


def shards(q_latent, q_rope, pool_latent, pool_rope, panel_latent, panel_rope, panel_from, prefix_id, block_mask, suffix_len):
    rope_own = q_rope.reshape(R_DEV, LAYERS, HEADS, D_ROPE)
    own, own_ints = pack_blocks(pool_latent, pool_rope, prefix_id, suffix_len, panel_from, block_mask)

    u0 = send(own, {0: (1, 0), 1: (0, 1)})
    d0 = send(own, {0: (-1, 0), 1: (0, -1)})
    t0 = send(own, {0: (2, 0)})
    a2, a2n = send(u0, {1: (0, 1)}), send(d0, {1: (0, -1)})
    q_own = [q_latent, rope_own]
    m1 = stack([own, u0, d0, t0], "stack1", [rope_own, a2, a2n])

    up, dn = {0: (0, 1), 1: (1, 0)}, {0: (0, -1), 1: (-1, 0)}
    u1, d1 = send(m1, up), send(m1, dn)
    late_latent, late_from, _ = lax.optimization_barrier((q_latent, panel_from, m1))
    wanted = [from_role(late_from, k) for k in (1, 2, 3)]
    lat_par = from_core(late_latent)
    sent = pick_panels(wanted, panel_latent, panel_rope)
    got = [from_role(x, -k) for k, x in zip((1, 2, 3), sent)]

    m2u, m2d = build(
        u1, d1, [a2, a2n], [("x", 0), ("x", 1), ("up", 0), ("up", 1)], [("x", 0), ("x", 1), ("dn", 2)], "build2", after=[*sent, lat_par]
    )
    u2, d2 = send(m2u, up), send(m2d, dn)
    a3, a3n = send(a2, {1: (0, 1)}), send(a2n, {1: (0, -1)})
    late_rope, late_ints, _ = lax.optimization_barrier((rope_own, own_ints, a3))
    q_par = [lat_par, from_core(late_rope)]
    ints = [own_ints, from_core(late_ints)]

    m3u, m3d = build(
        u2,
        d2,
        [a3, a3n],
        [("x", 0), ("x", 1), ("up", 0)],
        [("x", 0), ("x", 1), ("dn", 1)],
        "build3",
        after=[got[1], q_par[1], ints[1]],
    )
    u3, d3 = send(m3u, up), send(m3d, dn)
    a4 = send(a3, {1: (0, 1)})
    queries = (q_own, q_par)
    plans = (
        [(0, 0), (1, 1), (-1, 2), (2, 3), (-2, 4)],
        [
            (0, [(0, 0), (1, 0), (3, 2), (2, 0)]),
            (1, [(0, 1), (1, 1), (3, 3), (2, 1)]),
            (-1, [(0, 2), (1, 2), (4, 2), (2, 2)]),
        ],
    )
    state = flash("flash_near", plans, [m1, u1, d1, u2, d2], ints, queries)

    m4u, m4d = build(
        u3, d3, [a4], [("x", 0), ("up", 0)], [("x", 0), ("dn", 1)], "build4", 2, 0, 2, [got[0], got[2], state[1]]
    )
    u4, d4 = send(m4u, up), send(m4d, dn)
    t4 = send(a4, {1: (2, 0)})
    plans = (
        [(3, 2), (-3, 3)],
        [(2, [(4, None), (0, 0), (2, 2), (1, 0)]), (-2, [(5, None), (0, 1), (3, 2), (1, 1)])],
    )
    state = flash(
        "flash_mid", plans, [u2, d2, u3, d3, a2, a2n], ints, queries, state, [*got, panel_latent, panel_rope]
    )

    plans = (
        [(4, (2, 3))],
        [
            (3, [(4, None), (0, 0), (2, 1), (1, 0)]),
            (-3, [(5, None), (0, 1), (3, 1), (1, 1)]),
            (4, [(6, None), (2, 0), (7, None), (3, 0)]),
        ],
    )
    arrays = [u3, d3, u4, d4, a3, a3n, a4, t4]
    part = flash("flash_far_par", plans, arrays, ints, queries, state, None, (1,), True, per_step=3)
    state = flash("flash_far_own", plans, arrays, ints, queries, state, None, (0,), False, [part], per_step=3)
    return merge(state, from_core(part))


def solution(mesh):
    fine = Mesh(mesh.devices.reshape(ROLES, 2, 2, NZ, 2), NAMES)
    rows = P(NAMES)
    blocks = P(None, NAMES)
    return jax.shard_map(
        shards,
        mesh=fine,
        in_specs=(rows, rows, blocks, blocks, rows, rows, rows, rows, rows, rows),
        out_specs=rows,
        check_vma=False,
    )
```

```python
import functools
import math

import jax
import jax.numpy as jnp
from jax import lax
from jax.experimental import pallas as pl
from jax.experimental.pallas import tpu as pltpu
from jax.sharding import Mesh
from jax.sharding import PartitionSpec as P

HEADS = 128
D_LAT = 512
D_ROPE = 64
LAYERS = 2
TILE = 128
ROWS = 144
R_DEV = 6
ROLES = 4
NY = 4
NZ = 8
NAMES = ("role", "yh", "yl", "z", "core")
PLANE = ("yh", "yl", "z", "core")

LOG2E = math.log2(math.e)
LOG2_SCALE = 192.0 ** (-0.5) * LOG2E
NEG = -1e30
OWN_INTS = R_DEV * 19
WIDE = D_LAT + 128

VMEM = pl.BlockSpec(memory_space=pltpu.VMEM)
SMEM = pl.BlockSpec(memory_space=pltpu.SMEM)
ANY = pl.BlockSpec(memory_space=pl.ANY)
BF = jnp.bfloat16
F32 = jnp.float32
SMALL = pltpu.CompilerParams(vmem_limit_bytes=10 << 20)


def unit(*lead):
    return jax.ShapeDtypeStruct(lead + (LAYERS, ROWS, D_LAT), BF)


def pack_into(out, lat, rope):
    out[:TILE, :] = lat[...]
    for j in range(4):
        out[TILE:, 128 * j : 128 * (j + 1)] = rope[16 * j : 16 * (j + 1), :]


def pack_kernel(lat, rope, prefix, length, source, mask, out, ints):
    for layer in range(LAYERS):
        pack_into(out.at[layer], lat.at[layer, 0], rope.at[layer, 0])
    for r in range(R_DEV):
        ints[r] = prefix[r]
        ints[R_DEV + r] = length[0, r]
        ints[2 * R_DEV + r] = source[r]
        for j in range(16):
            ints[3 * R_DEV + 16 * r + j] = mask[r, j]


def pack_blocks(lat, rope, prefix, length, source, mask):
    return pl.pallas_call(
        pack_kernel,
        out_shape=(unit(), jax.ShapeDtypeStruct((OWN_INTS,), jnp.int32)),
        in_specs=[VMEM, VMEM] + [SMEM] * 4,
        out_specs=(VMEM, SMEM),
        name="pack_blocks",
    )(lat, rope, prefix, length, source, mask)


def stack_kernel(n, *refs):
    out = refs[-1]
    for i, ref in enumerate(refs[:n]):
        out[i] = ref[...]


def stack(parts, name, after=()):
    return pl.pallas_call(
        functools.partial(stack_kernel, len(parts)),
        out_shape=unit(len(parts)),
        in_specs=[VMEM] * len(parts) + [ANY] * len(after),
        out_specs=VMEM,
        compiler_params=SMALL,
        name=name,
    )(*parts, *after)


def build_kernel(up_plan, dn_plan, first_up, first_dn, n_parts, up_in, dn_in, *refs):
    parts, (up, dn) = refs[:n_parts], refs[-2:]
    n = up.shape[0]
    core = lax.axis_index("core")

    @pl.when(core == 0)
    def _():
        for i in range(n):
            up[i] = up_in[first_up + i]
            dn[i] = dn_in[first_dn + i]

    @pl.when(core == 1)
    def _():
        for out, plan in ((up, up_plan), (dn, dn_plan)):
            for i in range(n):
                if i < len(plan):
                    kind, index = plan[i]
                    out[i] = {"up": up_in, "dn": dn_in}[kind][index] if kind in ("up", "dn") else parts[index][...]
                else:
                    out[i] = jnp.zeros(out.shape[1:], out.dtype)


def build(up_in, dn_in, parts, up_plan, dn_plan, name, n=4, first_up=0, first_dn=0, after=()):
    return pl.pallas_call(
        functools.partial(build_kernel, up_plan, dn_plan, first_up, first_dn, len(parts)),
        out_shape=(unit(n), unit(n)),
        in_specs=[VMEM] * (2 + len(parts)) + [ANY] * len(after),
        out_specs=(VMEM, VMEM),
        compiler_params=SMALL,
        name=name,
    )(up_in, dn_in, *parts, *after)


def pick_kernel(wanted1, wanted2, wanted3, lat, rope, *outs):
    role = lax.axis_index("role")
    for wanted, out in zip((wanted1, wanted2, wanted3), outs):
        first, second, seen = jnp.int32(0), jnp.int32(0), jnp.int32(0)
        for s in range(R_DEV):
            hit = wanted[s] == role
            first = jnp.where(hit & (seen == 0), s, first)
            second = jnp.where(hit & (seen == 1), s, second)
            seen = seen + hit.astype(jnp.int32)
        for j, slot in enumerate((first, second)):
            for layer in range(LAYERS):
                pack_into(out.at[j, layer], lat.at[slot, layer], rope.at[slot, layer])


def pick_panels(wanted, lat, rope):
    return pl.pallas_call(
        pick_kernel,
        out_shape=(unit(2),) * 3,
        in_specs=[SMEM] * 3 + [VMEM, VMEM],
        out_specs=(VMEM,) * 3,
        compiler_params=SMALL,
        name="pick_panels",
    )(*wanted, lat, rope)


def flash_kernel(plans, panel, halves, first, last, per_step, n_arrays, n_after, *refs):
    refs = list(refs)

    def take(count):
        taken = refs[:count]
        del refs[:count]
        return taken

    ints = take(2)
    queries = [take(2) for _ in halves]
    arrays = take(n_arrays)
    if panel:
        got1, got2, got3, own_lat, own_rope = take(5)
    state_in = None if first else take(2)
    take(n_after)
    state_out = take(2) if not last else None
    out = take(1)[0] if last else None
    scratch = refs
    core, role, row, col = (lax.axis_index(name) for name in ("core", "role", ("yh", "yl"), "z"))

    def prefix(half, r):
        return ints[half][r]

    def length(half, r):
        return ints[half][R_DEV + r]

    def source(r):
        return ints[0][2 * R_DEV + r]

    def live(half, r, block):
        return ints[half][3 * R_DEV + 16 * r + block] == 1

    def one_step(step, carry, which, plan):
        jobs = [(q, h, half) for q in range(per_step) for h, half in enumerate(halves)]

        def keys_of(q, h, layer):
            k = 2 * ((q * len(halves) + h) * LAYERS + layer)
            return scratch[k], scratch[k + 1]

        def put(q, h, i, place, dynamic=None):
            array, index = place
            if dynamic is not None:
                index = dynamic
            for layer in range(LAYERS):
                keys, rope_keys = keys_of(q, h, layer)
                tile = arrays[array].at[layer] if index is None else arrays[array].at[index, layer]
                fill(keys, rope_keys, i, tile)

        def fill(keys, rope_keys, i, tile):
            keys[TILE * i : TILE * (i + 1), :] = tile[:TILE, :]
            for j in range(4):
                rope_keys[16 * j : 16 * (j + 1), TILE * i : TILE * (i + 1)] = tile[TILE:, 128 * j : 128 * (j + 1)]

        def row_of(q, half):
            return (prefix(half, step * per_step + q) - row + NY) % NY

        for q, h, half in jobs:
            dy = row_of(q, half)
            if which == 0:
                slot = jnp.where(dy == 2, 3, jnp.where(dy == 3, 2, dy))
                for i, (_, places) in enumerate(plan):
                    if isinstance(places, int):
                        put(q, h, i, (places, None), slot)
                    else:

                        @pl.when(slot < 2)
                        def _():
                            put(q, h, i, (places[0], None), slot)

                        @pl.when(slot >= 2)
                        def _():
                            put(q, h, i, (places[1], None), slot - 2)

            else:
                for d in range(NY):

                    @pl.when(dy == d)
                    def _():
                        for i, (_, places) in enumerate(plan):
                            put(q, h, i, places[d])

        if panel:
            for q, h, half in jobs:
                if half == 1:
                    continue
                i = len(plan)
                r = step * per_step + q
                shift = (role - source(r) + ROLES) % ROLES
                rank = jnp.int32(0)
                for s in range(R_DEV):
                    rank = rank + ((s < r) & (source(s) == source(r))).astype(jnp.int32)
                rank = jnp.minimum(rank, 1)

                @pl.when(shift == 0)
                def _():
                    for layer in range(LAYERS):
                        keys, rope_keys = keys_of(q, h, layer)
                        keys[TILE * i : TILE * (i + 1), :] = own_lat[r, layer]
                        rope_keys[:, TILE * i : TILE * (i + 1)] = own_rope[r, layer]

                for k, got in enumerate((got1, got2, got3)):

                    @pl.when(shift == k + 1)
                    def _():
                        for layer in range(LAYERS):
                            fill(*keys_of(q, h, layer), i, got.at[rank, layer])

        def chain(q, h, half, layer):
            r = step * per_step + q
            u = 2 * half + layer
            keys, rope_keys = keys_of(q, h, layer)
            n = len(plan) + (1 if panel and half == 0 else 0)
            q_lat, q_rope = queries[h][0][r, layer], queries[h][1][r, layer]
            width = n * TILE
            scores = lax.dot_general(q_lat, keys[:width, :], (((1,), (1,)), ((), ())), preferred_element_type=F32)
            scores = scores + jnp.dot(q_rope, rope_keys[:, :width], preferred_element_type=F32)
            yield
            pieces = []
            for i in range(n):
                piece = scores[:, TILE * i : TILE * (i + 1)] * LOG2_SCALE
                if i == len(plan):
                    token = lax.broadcasted_iota(jnp.int32, (HEADS, TILE), 1)
                    piece = jnp.where(token < length(half, r), piece, NEG)
                else:
                    block = 2 * ((col + (plan[i][0] + NZ)) % NZ) + which
                    piece = piece + jnp.where(live(half, r, block), 0.0, NEG)
                pieces.append(piece)
            top = functools.reduce(jnp.maximum, pieces)
            top = jnp.broadcast_to(jnp.max(top, axis=1, keepdims=True), (HEADS, 128))
            if not first:
                acc_in, ml_in = state_in
                old = ml_in[r, u, :, :128]
                top = jnp.maximum(old, top)
                fade = jnp.exp2(old - top)
            pieces = [jnp.exp2(piece - top) for piece in pieces]
            total = functools.reduce(jnp.add, pieces)
            if not first:
                total = total + fade * ml_in[r, u, :, 128:]
            weights = jnp.concatenate([piece.astype(BF) for piece in pieces], axis=1) if n > 1 else pieces[0].astype(BF)
            yield
            acc = jnp.dot(weights, keys[:width, :], preferred_element_type=F32)
            acc = [acc[:, 128 * j : 128 * (j + 1)] for j in range(4)]
            if not first:
                acc = [acc[j] + acc_in[r, u, :, 128 * j : 128 * (j + 1)] * fade for j in range(4)]
            yield
            if not last:
                acc_out, ml_out = state_out
                for j in range(4):
                    acc_out[r, u, :, 128 * j : 128 * (j + 1)] = acc[j]
                ml_out[r, u, :, :128] = top
                ml_out[r, u, :, 128:] = total
                return
            total = jnp.broadcast_to(jnp.sum(total, axis=1, keepdims=True), (HEADS, 128))
            lse = top + jnp.log(total) * LOG2E
            high = lse.astype(BF).astype(F32)
            mid = (lse - high).astype(BF).astype(F32)
            low = lse - high - mid
            lane = lax.broadcasted_iota(jnp.int32, (HEADS, 128), 1)
            tail = jnp.where(lane == 0, high, jnp.where(lane == 1, mid, jnp.where(lane == 2, low, 0.0)))
            inverse = 1.0 / total
            for j in range(4):
                out[r, layer, :, 128 * j : 128 * (j + 1)] = (acc[j] * inverse).astype(BF)
            out[r, layer, :, D_LAT:] = tail.astype(BF)

        chains = [chain(q, h, half, layer) for q, h, half in jobs for layer in range(LAYERS)]
        for _ in range(3):
            for c in chains:
                next(c)
        for c in chains:
            next(c, None)
        return carry

    for which, plan in enumerate(plans):

        @pl.when(core == which)
        def _():
            lax.fori_loop(0, R_DEV // per_step, functools.partial(one_step, which=which, plan=plan), 0)


def merge_kernel(acc, ml, recv, out):
    for q in range(out.shape[0]):
        r = out.shape[0] * pl.program_id(0) + q
        for layer in range(LAYERS):
            top = ml[r, layer, :, :128]
            total = jnp.broadcast_to(jnp.sum(ml[r, layer, :, 128:], axis=1, keepdims=True), (HEADS, 128))
            tail = recv[r, layer, :, D_LAT:].astype(F32)
            theirs = jnp.broadcast_to(jnp.sum(tail, axis=1, keepdims=True), (HEADS, 128))
            most = jnp.maximum(top, theirs)
            ours, theirs = jnp.exp2(top - most), jnp.exp2(theirs - most)
            scale = 1.0 / (total * ours + theirs)
            ours, theirs = ours * scale, theirs * scale
            for j in range(4):
                cols = slice(128 * j, 128 * (j + 1))
                out[q, layer, :, cols] = (acc[r, layer, :, cols] * ours + recv[r, layer, :, cols].astype(F32) * theirs).astype(BF)


def merge(state, recv):
    return pl.pallas_call(
        merge_kernel,
        grid=(3,),
        out_shape=jax.ShapeDtypeStruct((R_DEV, LAYERS, HEADS, D_LAT), BF),
        in_specs=[VMEM] * 3,
        out_specs=pl.BlockSpec((2, LAYERS, HEADS, D_LAT), lambda i: (i, 0, 0, 0)),
        compiler_params=pltpu.CompilerParams(vmem_limit_bytes=20 << 20),
        name="merge",
    )(*state, recv)


def flash(name, plans, arrays, ints, queries, state=None, panels=None, halves=(0, 1), last=False, after=(), per_step=2):
    first = state is None
    ops = list(ints)
    for half in halves:
        ops += queries[half]
    ops += arrays
    specs = [SMEM] * 2 + [VMEM] * (len(ops) - 2)
    if panels is not None:
        ops += panels
        specs += [VMEM] * 5
    aliases = {}
    if not first:
        if not last:
            aliases = {len(ops): 0, len(ops) + 1: 1}
        ops += state
        specs += [VMEM, VMEM]
    ops += after
    specs += [ANY] * len(after)
    if last:
        out_shape = jax.ShapeDtypeStruct((R_DEV, LAYERS, HEADS, WIDE), BF)
        out_specs = VMEM
    else:
        out_shape = (
            pltpu.VMEM((R_DEV, 2 * LAYERS, HEADS, D_LAT), F32),
            pltpu.VMEM((R_DEV, 2 * LAYERS, HEADS, 256), F32),
        )
        out_specs = (VMEM, VMEM)
    n = max(len(plan) for plan in plans) + (1 if panels is not None else 0)
    tiles = R_DEV * LAYERS * len(halves) * n
    return pl.pallas_call(
        functools.partial(flash_kernel, plans, panels is not None, halves, first, last, per_step, len(arrays), len(after)),
        out_shape=out_shape,
        in_specs=specs,
        out_specs=out_specs,
        scratch_shapes=[pltpu.VMEM((TILE * n, D_LAT), BF), pltpu.VMEM((D_ROPE, TILE * n), BF)]
        * (LAYERS * len(halves) * per_step),
        input_output_aliases=aliases,
        cost_estimate=pl.CostEstimate(
            flops=3 * tiles * HEADS * TILE * (2 * D_LAT + D_ROPE), bytes_accessed=4 << 20, transcendentals=tiles * HEADS * TILE
        ),
        compiler_params=pltpu.CompilerParams(vmem_limit_bytes=20 << 20),
        name=name,
    )(*ops)


def place(y, z, c):
    return ((y % NY) * NZ + z % NZ) * 2 + c


def send(x, moves):
    pairs = [
        (place(y + move[0], z + move[1], c), place(y, z, c))
        for c, move in moves.items()
        for y in range(NY)
        for z in range(NZ)
    ]
    return lax.ppermute(x, PLANE, pairs)


def from_role(x, shift):
    return lax.ppermute(x, "role", [(i, (i - shift) % ROLES) for i in range(ROLES)])


def from_core(x):
    return lax.ppermute(x, "core", [(0, 1), (1, 0)])


def shards(q_latent, q_rope, pool_latent, pool_rope, panel_latent, panel_rope, panel_from, prefix_id, block_mask, suffix_len):
    rope_own = q_rope.reshape(R_DEV, LAYERS, HEADS, D_ROPE)
    own, own_ints = pack_blocks(pool_latent, pool_rope, prefix_id, suffix_len, panel_from, block_mask)

    u0 = send(own, {0: (1, 0), 1: (0, 1)})
    d0 = send(own, {0: (-1, 0), 1: (0, -1)})
    t0 = send(own, {0: (2, 0)})
    a2, a2n = send(u0, {1: (0, 1)}), send(d0, {1: (0, -1)})
    q_own = [q_latent, rope_own]
    lat_par = from_core(q_latent)
    m1 = stack([own, u0, d0, t0], "stack1", [rope_own, a2, a2n, lat_par])

    up, dn = {0: (0, 1), 1: (1, 0)}, {0: (0, -1), 1: (-1, 0)}
    u1, d1 = send(m1, up), send(m1, dn)
    late_from, _ = lax.optimization_barrier((panel_from, m1))
    wanted = [from_role(late_from, k) for k in (1, 2, 3)]
    sent = pick_panels(wanted, panel_latent, panel_rope)
    got = [from_role(x, -k) for k, x in zip((1, 2, 3), sent)]

    m2u, m2d = build(
        u1, d1, [a2, a2n], [("x", 0), ("x", 1), ("up", 0), ("up", 1)], [("x", 0), ("x", 1), ("dn", 2)], "build2", after=sent
    )
    u2, d2 = send(m2u, up), send(m2d, dn)
    a3, a3n = send(a2, {1: (0, 1)}), send(a2n, {1: (0, -1)})
    late_rope, late_ints, _ = lax.optimization_barrier((rope_own, own_ints, a3))
    q_par = [lat_par, from_core(late_rope)]
    ints = [own_ints, from_core(late_ints)]

    m3u, m3d = build(
        u2,
        d2,
        [a3, a3n],
        [("x", 0), ("x", 1), ("up", 0)],
        [("x", 0), ("x", 1), ("dn", 1)],
        "build3",
        after=[got[1], q_par[1], ints[1]],
    )
    u3, d3 = send(m3u, up), send(m3d, dn)
    a4 = send(a3, {1: (0, 1)})
    queries = (q_own, q_par)
    plans = (
        [(0, 0), (1, 1), (-1, 2), (2, 3), (-2, 4)],
        [
            (0, [(0, 0), (1, 0), (3, 2), (2, 0)]),
            (1, [(0, 1), (1, 1), (3, 3), (2, 1)]),
            (-1, [(0, 2), (1, 2), (4, 2), (2, 2)]),
        ],
    )
    state = flash("flash_near", plans, [m1, u1, d1, u2, d2], ints, queries)

    m4u, m4d = build(
        u3, d3, [a4], [("x", 0), ("up", 0)], [("x", 0), ("dn", 1)], "build4", 2, 0, 2, [got[0], got[2], state[1]]
    )
    u4, d4 = send(m4u, up), send(m4d, dn)
    t4 = send(a4, {1: (2, 0)})
    plans = (
        [(3, 2), (-3, 3)],
        [(2, [(4, None), (0, 0), (2, 2), (1, 0)]), (-2, [(5, None), (0, 1), (3, 2), (1, 1)])],
    )
    state = flash(
        "flash_mid", plans, [u2, d2, u3, d3, a2, a2n], ints, queries, state, [*got, panel_latent, panel_rope]
    )

    plans = (
        [(4, (2, 3))],
        [
            (3, [(4, None), (0, 0), (2, 1), (1, 0)]),
            (-3, [(5, None), (0, 1), (3, 1), (1, 1)]),
            (4, [(6, None), (2, 0), (7, None), (3, 0)]),
        ],
    )
    arrays = [u3, d3, u4, d4, a3, a3n, a4, t4]
    part = flash("flash_far_par", plans, arrays, ints, queries, state, None, (1,), True, per_step=3)
    state = flash("flash_far_own", plans, arrays, ints, queries, state, None, (0,), False, [part], per_step=3)
    return merge(state, from_core(part))


def solution(mesh):
    fine = Mesh(mesh.devices.reshape(ROLES, 2, 2, NZ, 2), NAMES)
    rows = P(NAMES)
    blocks = P(None, NAMES)
    return jax.shard_map(
        shards,
        mesh=fine,
        in_specs=(rows, rows, blocks, blocks, rows, rows, rows, rows, rows, rows),
        out_specs=rows,
        check_vma=False,
    )
```
